512 devices in a mesh: grp: 16 (over z), pen: 32 (over x, y, core).
Axes of the slice: x: 4, y: 4, z: 16, core: 2. Of those that a mesh axis runs over, the one named last changes fastest.
Arguments:
- residual: float32 [512, 512, 512], P('grp', 'pen'), may hold values from -53 to 53
- direction: float32 [512, 512, 512], P('grp', 'pen'), may hold values from -74 to 74
- material: int32 [512, 512, 512], P('grp', 'pen'), may hold values 0 or 1
Outputs:
- new_residual: float32 [512, 512, 512], P('grp', 'pen')
- new_direction: float32 [512, 512, 512], P('grp', 'pen')
The draws below stay inside these ranges and needn't reach their ends.
All inputs are finite; a program needn't handle non-finite values. No bound on the sum of `material` on one device may be relied on, other than what follows from the above.
Results may differ from the reference program's by a relative error of at most 0.000076.
Values sent between devices are 32-bit elements; how exact they have to be, the bound alone decides.
No kernel may reach another device: no remote copies, remote signals or barrier semaphores. Data moves between devices by JAX's collectives and lax.ppermute only.
A program may use at most 128 MiB of HBM per device.

```python
import math
import jax
import jax.numpy as jnp
from jax import lax

NZ = 512
NX = 512
NY = 512


def field_profile():
    across = jnp.arange(NX, dtype=jnp.float32) / max(NX - 1, 1)
    downward = jnp.arange(NY, dtype=jnp.float32) / max(NY - 1, 1)
    return 3.0 ** (0.5 * (across[:, None, None] + downward[None, :, None]) - 0.5 + 0.5 * (across[:, None, None] + downward[None, :, None]))


def shared_normals(key):
    first_key, second_key = jax.random.split(key)
    common = jnp.clip(jax.random.normal(first_key, (NX, NY, NZ), jnp.float32), -5.0, 5.0)
    own_part = jnp.clip(jax.random.normal(second_key, (NX, NY, NZ), jnp.float32), -5.0, 5.0)
    return (common, own_part)


def draw_residual(key, part):
    common, own_part = shared_normals(key)
    profile = field_profile()
    return profile * common


def draw_direction(key, part):
    common, own_part = shared_normals(key)
    profile = field_profile()
    mixed = 0.8 * common + 0.6 * own_part
    return profile * mixed


def touch_ends(entries, own_key, low, largest):
    extent = entries.shape
    spot = [jax.random.randint(jax.random.fold_in(own_key, axis), (), 0, extent[axis]) for axis in range(len(extent))]
    entries = entries.at[tuple(spot)].set(low)
    longest = extent.index(max(extent))
    spot[longest] = (spot[longest] + 1) % extent[longest]
    return entries.at[tuple(spot)].set(largest)


def setup_inputs(seed: int = 0) -> dict:
    arg_keys = jax.random.split(jax.random.key(seed), 4)
    return {
        "residual": draw_residual(jax.random.fold_in(arg_keys[3], 71), 0),
        "direction": draw_direction(jax.random.fold_in(arg_keys[3], 71), 0),
        "material": touch_ends((jax.random.randint(arg_keys[2], (NX, NY, NZ), 0, 2) < 1).astype(jnp.int32), jax.random.fold_in(arg_keys[2], 1), 0, 1),
    }


absorption = 0.02
mean_conduct = 5.0

def dct_matrix(length):
    degree = jnp.arange(length, dtype=jnp.int32)[:, None]
    sample = jnp.arange(length, dtype=jnp.int32)[None, :]
    phases = degree * (2 * sample + 1) % (4 * length)
    weight = jnp.where(degree == 0, math.sqrt(1.0 / length), math.sqrt(2.0 / length))
    return weight * jnp.cos(math.pi * phases.astype(jnp.float32) / (2.0 * length))

def eigen_values(modes, length):
    return 4.0 * jnp.sin(math.pi * modes.astype(jnp.float32) / (2.0 * length)) ** 2

def apply_operator(direction, stiffness):
    scaled = stiffness * direction
    padded = jnp.pad(scaled, 1)
    beside = padded[2:, 1:-1, 1:-1] + padded[:-2, 1:-1, 1:-1]
    beside = beside + padded[1:-1, 2:, 1:-1] + padded[1:-1, :-2, 1:-1]
    beside = beside + padded[1:-1, 1:-1, 2:] + padded[1:-1, 1:-1, :-2]
    return absorption * direction + stiffness * (6.0 * scaled - beside)

def precondition(field_in):
    highest = lax.Precision.HIGHEST
    along_x = dct_matrix(NX)
    along_y = dct_matrix(NY)
    along_z = dct_matrix(NZ)
    spectrum = jnp.einsum('xyz,kz->xyk', field_in, along_z, precision=highest)
    spectrum = jnp.einsum('xyk,ay->xak', spectrum, along_y, precision=highest)
    spectrum = jnp.einsum('xak,bx->bak', spectrum, along_x, precision=highest)
    eigen_x = eigen_values(jnp.arange(NX, dtype=jnp.int32), NX)
    eigen_y = eigen_values(jnp.arange(NY, dtype=jnp.int32), NY)
    eigen_z = eigen_values(jnp.arange(NZ, dtype=jnp.int32), NZ)
    spectrum = spectrum / (absorption + mean_conduct * (eigen_x[:, None, None] + eigen_y[None, :, None] + eigen_z[None, None, :]))
    spectrum = jnp.einsum('bak,bx->xak', spectrum, along_x, precision=highest)
    spectrum = jnp.einsum('xak,ay->xyk', spectrum, along_y, precision=highest)
    return jnp.einsum('xyk,kz->xyz', spectrum, along_z, precision=highest)

def reference(residual, direction, material):
    stiffness = jnp.sqrt(1.0 + 29.0 * material.astype(jnp.float32))
    operated = apply_operator(direction, stiffness)
    curvature = jnp.sum(direction * operated)
    projection = jnp.sum(residual * direction)
    step_size = projection / curvature
    new_residual = residual - step_size * operated
    smoothed = precondition(new_residual)
    conjugacy = jnp.sum(smoothed * operated)
    new_direction = smoothed - conjugacy / curvature * direction
    return (new_residual, new_direction)
```

```python
import functools
import math

import jax
import jax.numpy as jnp
import numpy as np
from jax import lax
from jax.experimental import pallas as pl
from jax.experimental.pallas import tpu as pltpu
from jax.sharding import PartitionSpec as P

N = 512
GRP = 16
PEN = 32
BX = N // GRP
BY = N // PEN
BK = N // PEN
ABSORPTION = 0.02
CONDUCT = 5.0
SOLID = math.sqrt(30.0)
F32 = jnp.float32
VMEM = pl.BlockSpec(memory_space=pltpu.VMEM)
SMEM = pl.BlockSpec(memory_space=pltpu.SMEM)
PARAMS = pltpu.CompilerParams(vmem_limit_bytes=48 * 1024 * 1024)


def dct_matrix():
    k = np.arange(N)[:, None]
    n = np.arange(N)[None, :]
    weight = np.where(k == 0, math.sqrt(1.0 / N), math.sqrt(2.0 / N))
    return (weight * np.cos(math.pi * (k * (2 * n + 1) % (4 * N)) / (2.0 * N))).astype(np.float32)


def eigen_values():
    return (4.0 * np.sin(math.pi * np.arange(N) / (2.0 * N)) ** 2).astype(np.float32)


def matmul(a, b, dims):
    return lax.dot_general(
        a, b, (dims, ((), ())), precision=lax.Precision.HIGHEST, preferred_element_type=F32
    )


def decay(shift):
    rho = 2.0 / (2.0 + shift + jnp.sqrt(shift * (shift + 4.0)))
    return rho, rho / (CONDUCT * (1.0 - rho * rho))


def swap_units(rows):
    rows = list(rows)
    unit = lax.broadcasted_iota(jnp.int32, rows[0].shape, 1) // 16
    for d in (4, 2, 1):
        keep = (unit & d) == 0
        for i in range(8):
            if i & d == 0:
                a, b = rows[i], rows[i + d]
                rows[i] = jnp.where(keep, a, pltpu.roll(b, 16 * d, 1))
                rows[i + d] = jnp.where(keep, pltpu.roll(a, 128 - 16 * d, 1), b)
    return rows


def to_tile(x):
    x = x[:8] + x[8:]
    return x[:, 0:128] + x[:, 128:256] + x[:, 256:384] + x[:, 384:512]


def fold(x, step):
    return x + pltpu.roll(x, step, 0)


def stiffness_of(material):
    return jnp.where(material == 1, jnp.float32(SOLID), jnp.float32(1.0))


def faces_kernel(d_ref, m_ref, xlo_ref, xhi_ref, ylo_ref, yhi_ref):
    xlo_ref[0] = stiffness_of(m_ref[0]) * d_ref[0]
    xhi_ref[0] = stiffness_of(m_ref[BX - 1]) * d_ref[BX - 1]
    ylo_ref[...] = stiffness_of(m_ref[:, 0, :]) * d_ref[:, 0, :]
    yhi_ref[...] = stiffness_of(m_ref[:, BY - 1, :]) * d_ref[:, BY - 1, :]


def forward_kernel(r_ref, d_ref, m_ref, xl_ref, xh_ref, yl_ref, yh_ref, c_ref, q_ref, send_ref, u_ref):
    u_ref[0] = xl_ref[0]
    u_ref[BX + 1] = xh_ref[0]

    def scale(x, _):
        u_ref[x + 1] = stiffness_of(m_ref[x]) * d_ref[x]
        return 0

    lax.fori_loop(0, BX, scale, 0)
    row = lax.broadcasted_iota(jnp.int32, (BY, N), 0)
    lane = lax.broadcasted_iota(jnp.int32, (BY, N), 1)

    def stencil(x, sums):
        u = u_ref[x + 1]
        d = d_ref[x]
        beside = u_ref[x] + u_ref[x + 2]
        beside += jnp.where(row == 0, yl_ref[pl.ds(x, 1), :], pltpu.roll(u, 1, 0))
        beside += jnp.where(row == BY - 1, yh_ref[pl.ds(x, 1), :], pltpu.roll(u, BY - 1, 0))
        beside += jnp.where(lane == 0, 0.0, pltpu.roll(u, 1, 1))
        beside += jnp.where(lane == N - 1, 0.0, pltpu.roll(u, N - 1, 1))
        q = ABSORPTION * d + stiffness_of(m_ref[x]) * (6.0 * u - beside)
        q_ref[x] = q
        return sums[0] + to_tile(d * q), sums[1] + to_tile(r_ref[x] * d)

    zero = jnp.zeros((8, 128), F32)
    curvature, projection = lax.fori_loop(0, BX, stencil, (zero, zero))
    half = lax.broadcasted_iota(jnp.int32, (8, 128), 0) < 4
    sums = jnp.where(half, fold(curvature, 4), fold(projection, 4))
    for field, ref in enumerate((r_ref, q_ref)):
        modes = matmul(c_ref[...], ref[...].reshape(BX * BY, N), ((1,), (1,)))
        for b in range(4):
            part = modes[:, 128 * b : 128 * b + 128].reshape(PEN, 2, 8, 128)
            for a in range(2):
                send_ref[:, 8 * field + 4 * a + b] = part[:, a]
    for j in range(PEN):
        send_ref[j, 16] = sums


def blocks_kernel(recv_ref, c_ref, ez_ref, ey_ref, fr_ref, fq_ref, send_ref, y_ref):
    for field, out_ref in enumerate((fr_ref, fq_ref)):
        for b in range(4):
            for s in range(4):
                for a in range(2):
                    t = 8 * field + 4 * a + b
                    rows = swap_units([recv_ref[8 * s + i, t] for i in range(8)])
                    for i in range(8):
                        y_ref[8 * b + i, 8 * a : 8 * a + 8, 128 * s : 128 * s + 128] = rows[i]
        out_ref[...] = matmul(y_ref[...].reshape(BX * BK, N), c_ref[...], ((1,), (1,))).reshape(BX, BK, N)

    dots = [jnp.zeros((8, 128), F32), jnp.zeros((8, 128), F32)]
    k0 = lax.axis_index("pen") * BK
    for h in range(2):
        rows = pl.ds(8 * h, 8)
        ez = jnp.concatenate(
            [jnp.full((1, N), ez_ref[k0 + 8 * h + i], F32) for i in range(8)], axis=0
        )
        rho, factor = decay(ABSORPTION / CONDUCT + ez + ey_ref[...])

        def sweep(x, carry):
            power, vr, vq, wr, wq, rq, qq = carry
            r = fr_ref[x, rows]
            q = fq_ref[x, rows]
            vr = r + rho * vr
            vq = q + rho * vq
            wr = wr + power * r
            wq = wq + power * q
            rq = rq + (vr * q + vq * r - r * q)
            qq = qq + (2.0 * vq - q) * q
            return power * rho, vr, vq, wr, wq, rq, qq

        zero = jnp.zeros((8, N), F32)
        carry = lax.fori_loop(0, BX, sweep, (jnp.ones((8, N), F32),) + (zero,) * 6)
        _, vr, vq, wr, wq, rq, qq = carry
        for t, parts in enumerate(((vr, wr), (vq, wq))):
            for side, x in enumerate(parts):
                for b in range(4):
                    for i in range(8):
                        send_ref[8 * h + i, t, 4 * side + b : 4 * side + b + 1, :] = x[
                            i : i + 1, 128 * b : 128 * b + 128
                        ]
        for i, x in enumerate((rq, qq)):
            x = factor * x
            dots[i] += x[:, 0:128] + x[:, 128:256] + x[:, 256:384] + x[:, 384:512]

    sums = recv_ref[0, 16]
    for j in range(1, PEN):
        sums = sums + recv_ref[j, 16]
    row = lax.broadcasted_iota(jnp.int32, (8, 128), 0)
    sums = fold(sums, 6)
    rq = fold(fold(dots[0], 4), 2)
    qq = fold(fold(dots[1], 4), 2)
    sums = jnp.where(
        row < 2, sums, jnp.where(row < 4, pltpu.roll(sums, 6, 0), jnp.where(row < 6, rq, qq))
    )
    for j in range(GRP):
        send_ref[j, 2] = sums


def interface_kernel(recv_ref, ez_ref, ey_ref, send_ref, control_ref):
    row = lax.broadcasted_iota(jnp.int32, (8, 128), 0)
    sums = recv_ref[0, 2]
    for p in range(1, GRP):
        sums = sums + recv_ref[p, 2]

    def total(low):
        return jnp.full((8, 128), jnp.sum(jnp.where((row >= low) & (row < low + 2), sums, 0.0)), F32)

    curvature, projection, rq, qq = total(0), total(2), total(4), total(6)
    step = projection / curvature
    ez = ez_ref[lax.axis_index("pen") * BK + lax.axis_index("grp")]
    rho, factor = decay(ABSORPTION / CONDUCT + ez + ey_ref[...])
    across = rho
    for _ in range(5):
        across = across * across
    tiles = [recv_ref[p, 0] - step * recv_ref[p, 1] for p in range(GRP)]
    zero = jnp.zeros((8, 128), F32)
    rising = [zero]
    for p in range(GRP):
        rising.append(tiles[p] + across * rising[-1])
    falling = [zero]
    for p in reversed(range(GRP)):
        falling.append(tiles[p] + across * falling[-1])
    lower = row < 4
    ends = jnp.where(lower, rising[GRP], falling[GRP])
    powers = [jnp.ones((8, 128), F32)]
    for p in range(GRP):
        powers.append(powers[-1] * across)
    whole = powers[GRP]
    images = (pltpu.roll(ends, 4, 0) + whole * ends) / (1.0 - whole * whole)
    dots = zero
    for p in range(GRP):
        state = jnp.where(
            lower,
            rising[p] + powers[p] * images,
            falling[GRP - 1 - p] + powers[GRP - 1 - p] * images,
        )
        send_ref[p, 0] = state
        dots = dots + state * pltpu.roll(recv_ref[p, 1], 4, 0)
    dots = rho * factor * dots
    for p in range(GRP):
        send_ref[p, 1] = dots
    control_ref[0] = step
    control_ref[1] = curvature
    control_ref[2] = rq - step * qq


def solve_kernel(fr_ref, fq_ref, recv_ref, control_ref, c_ref, ez_ref, ey_ref, send_ref, f_ref, u_ref, y_ref):
    step = control_ref[0, 0:1, 0:1]
    k0 = lax.axis_index("pen") * BK
    for h in range(2):
        rows = pl.ds(8 * h, 8)
        ez = jnp.concatenate(
            [jnp.full((1, N), ez_ref[k0 + 8 * h + i], F32) for i in range(8)], axis=0
        )
        rho, factor = decay(ABSORPTION / CONDUCT + ez + ey_ref[...])

        def state(side):
            return jnp.concatenate(
                [
                    jnp.concatenate(
                        [recv_ref[8 * h + i, 0, 4 * side + b : 4 * side + b + 1, :] for i in range(8)],
                        axis=0,
                    )
                    for b in range(4)
                ],
                axis=1,
            )

        def rise(x, carry):
            f = fr_ref[x, rows] - step * fq_ref[x, rows]
            carry = f + rho * carry
            f_ref[x] = f
            u_ref[x, rows] = carry
            return carry

        def fall(i, carry):
            x = BX - 1 - i
            f = f_ref[x]
            u_ref[x, rows] = factor * (u_ref[x, rows] + rho * carry)
            return f + rho * carry

        lax.fori_loop(0, BX, rise, state(0))
        lax.fori_loop(0, BX, fall, state(1))

    y_ref[...] = matmul(u_ref[...].reshape(BX * BK, N), c_ref[...], ((1,), (0,))).reshape(BX, BK, N)
    for b in range(4):
        for s in range(4):
            for a in range(2):
                rows = swap_units(
                    [y_ref[8 * b + i, 8 * a : 8 * a + 8, 128 * s : 128 * s + 128] for i in range(8)]
                )
                for i in range(8):
                    send_ref[8 * s + i, 4 * a + b] = rows[i]
    sums = recv_ref[0, 1]
    for p in range(1, GRP):
        sums = sums + recv_ref[p, 1]
    first = (lax.broadcasted_iota(jnp.int32, (8, 128), 0) == 0) & (
        lax.broadcasted_iota(jnp.int32, (8, 128), 1) == 0
    )
    sums = sums + jnp.where(first, control_ref[2], 0.0)
    for j in range(PEN):
        send_ref[j, 8] = sums


def finish_kernel(recv_ref, r_ref, d_ref, q_ref, control_ref, c_ref, nr_ref, nd_ref, g_ref):
    for b in range(4):
        for a in range(2):
            g_ref[:, a, :, 128 * b : 128 * b + 128] = recv_ref[:, 4 * a + b]
    sums = recv_ref[0, 8]
    for j in range(1, PEN):
        sums = sums + recv_ref[j, 8]
    step = control_ref[0, 0:1, 0:1]
    conjugacy = jnp.full((8, 128), jnp.sum(sums), F32)
    ratio = (conjugacy / control_ref[1])[0:1, 0:1]
    smoothed = matmul(g_ref[...].reshape(N, BX * BY), c_ref[...], ((0,), (0,)))
    nd_ref[...] = smoothed.reshape(BX, BY, N) - ratio * d_ref[...]
    nr_ref[...] = r_ref[...] - step * q_ref[...]


def shape(*dims):
    return jax.ShapeDtypeStruct(dims, F32)


def call(kernel, ins, outs, scratch=()):
    return pl.pallas_call(
        kernel,
        in_specs=ins,
        out_specs=[VMEM] * len(outs),
        out_shape=outs,
        scratch_shapes=[pltpu.VMEM(s, F32) for s in scratch],
        compiler_params=PARAMS,
    )


def exchange(x, axis):
    return lax.all_to_all(x, axis, 0, 0)


def on_device(residual, direction, material):
    matrix = jnp.asarray(dct_matrix())
    eigen = eigen_values()
    ez = jnp.asarray(eigen)
    ey_row = jnp.asarray(eigen[None, :])
    ey_tile = jnp.asarray(np.concatenate([eigen.reshape(4, 128)] * 2, 0))
    block = shape(BX, BY, N)

    xlo, xhi, ylo, yhi = call(
        faces_kernel, [VMEM] * 2, [shape(1, BY, N), shape(1, BY, N), shape(BX, N), shape(BX, N)]
    )(direction, material)

    def up(x, axis, count):
        return lax.ppermute(x, axis, [(i, i + 1) for i in range(count - 1)])

    def down(x, axis, count):
        return lax.ppermute(x, axis, [(i + 1, i) for i in range(count - 1)])

    xl, xh = up(xhi, "grp", GRP), down(xlo, "grp", GRP)
    yl, yh = up(yhi, "pen", PEN), down(ylo, "pen", PEN)

    operated, send = call(
        forward_kernel, [VMEM] * 8, [block, shape(PEN, 17, 8, 128)], [(BX + 2, BY, N)]
    )(residual, direction, material, xl, xh, yl, yh, matrix)

    recv = exchange(send, "pen")
    field_r, field_q, send = call(
        blocks_kernel, [VMEM, VMEM, SMEM, VMEM], [block, block, shape(GRP, 3, 8, 128)], [(BX, BK, N)]
    )(recv, matrix, ez, ey_row)

    recv = exchange(send, "grp")
    send, control = call(
        interface_kernel, [VMEM, SMEM, VMEM], [shape(GRP, 2, 8, 128), shape(3, 8, 128)]
    )(recv, ez, ey_tile)

    recv = exchange(send, "grp")
    (send,) = call(
        solve_kernel,
        [VMEM] * 5 + [SMEM, VMEM],
        [shape(PEN, 9, 8, 128)],
        [(BX, 8, N), (BX, BK, N), (BX, BK, N)],
    )(field_r, field_q, recv, control, matrix, ez, ey_row)

    recv = exchange(send, "pen")
    return tuple(
        call(finish_kernel, [VMEM] * 6, [block, block], [(PEN, 2, 8, BX * BY)])(
            recv, residual, direction, operated, control, matrix
        )
    )


def solution(mesh):
    placed = P("grp", "pen", None)
    return jax.shard_map(
        on_device,
        mesh=mesh,
        in_specs=(placed, placed, placed),
        out_specs=(placed, placed),
        check_vma=False,
    )
```

```python
import functools
import math

import jax
import jax.numpy as jnp
import numpy as np
from jax import lax
from jax.experimental import pallas as pl
from jax.experimental.pallas import tpu as pltpu
from jax.sharding import PartitionSpec as P

N = 512
GRP = 16
PEN = 32
BX = N // GRP
BY = N // PEN
PARTS = 8
BK = N // PEN
ABSORPTION = 0.02
CONDUCT = 5.0
SOLID = math.sqrt(30.0)
F32 = jnp.float32
VMEM = pl.BlockSpec(memory_space=pltpu.VMEM)
SMEM = pl.BlockSpec(memory_space=pltpu.SMEM)
PARAMS = pltpu.CompilerParams(vmem_limit_bytes=48 * 1024 * 1024)


def dct_matrix():
    k = np.arange(N)[:, None]
    n = np.arange(N)[None, :]
    weight = np.where(k == 0, math.sqrt(1.0 / N), math.sqrt(2.0 / N))
    return (weight * np.cos(math.pi * (k * (2 * n + 1) % (4 * N)) / (2.0 * N))).astype(np.float32)


def eigen_values():
    return (4.0 * np.sin(math.pi * np.arange(N) / (2.0 * N)) ** 2).astype(np.float32)


def matmul(a, b, dims):
    return lax.dot_general(
        a, b, (dims, ((), ())), precision=lax.Precision.HIGHEST, preferred_element_type=F32
    )


def decay(shift):
    rho = 2.0 / (2.0 + shift + jnp.sqrt(shift * (shift + 4.0)))
    return rho, rho / (CONDUCT * (1.0 - rho * rho))


def swap_units(rows):
    rows = list(rows)
    unit = lax.broadcasted_iota(jnp.int32, rows[0].shape, 1) // 16
    for d in (4, 2, 1):
        keep = (unit & d) == 0
        for i in range(8):
            if i & d == 0:
                a, b = rows[i], rows[i + d]
                rows[i] = jnp.where(keep, a, pltpu.roll(b, 16 * d, 1))
                rows[i + d] = jnp.where(keep, pltpu.roll(a, 128 - 16 * d, 1), b)
    return rows


def to_tile(x):
    x = x[:8] + x[8:]
    return x[:, 0:128] + x[:, 128:256] + x[:, 256:384] + x[:, 384:512]


def fold(x, step):
    return x + pltpu.roll(x, step, 0)


def stiffness_of(material):
    return jnp.where(material == 1, jnp.float32(SOLID), jnp.float32(1.0))


def faces_kernel(d_hbm, m_hbm, xlo_ref, xhi_ref, ylo_ref, yhi_ref, d_ref, m_ref, sems):
    copies = []
    for i in range(PARTS):
        part = pl.ds(i * (BX // PARTS), BX // PARTS)
        for j, (source, target) in enumerate(((d_hbm, d_ref), (m_hbm, m_ref))):
            copies.append(pltpu.make_async_copy(source.at[part], target.at[part], sems.at[i, j]))
            copies[-1].start()
    for copy in copies:
        copy.wait()
    xlo_ref[0] = stiffness_of(m_ref[0]) * d_ref[0]
    xhi_ref[0] = stiffness_of(m_ref[BX - 1]) * d_ref[BX - 1]
    ylo_ref[...] = stiffness_of(m_ref[:, 0, :]) * d_ref[:, 0, :]
    yhi_ref[...] = stiffness_of(m_ref[:, BY - 1, :]) * d_ref[:, BY - 1, :]


def third_modes(field_ref, c_ref):
    return matmul(c_ref[...], field_ref[...].reshape(BX * BY, N), ((1,), (1,)))


def put_modes(modes, first, send_ref):
    for b in range(4):
        part = modes[:, 128 * b : 128 * b + 128].reshape(PEN, 2, 8, 128)
        for a in range(2):
            send_ref[:, first + 4 * a + b] = part[:, a]


def residual_kernel(r_ref, c_ref, modes_ref):
    modes_ref[...] = third_modes(r_ref, c_ref)


def operated_kernel(
    r_ref, d_ref, m_ref, modes_ref, xl_ref, xh_ref, yl_ref, yh_ref, c_ref, q_ref, send_ref, u_ref
):
    u_ref[0] = xl_ref[0]
    u_ref[BX + 1] = xh_ref[0]

    def scale(x, _):
        u_ref[x + 1] = stiffness_of(m_ref[x]) * d_ref[x]
        return 0

    lax.fori_loop(0, BX, scale, 0)
    row = lax.broadcasted_iota(jnp.int32, (BY, N), 0)
    lane = lax.broadcasted_iota(jnp.int32, (BY, N), 1)

    def stencil(x, sums):
        u = u_ref[x + 1]
        d = d_ref[x]
        beside = u_ref[x] + u_ref[x + 2]
        beside += jnp.where(row == 0, yl_ref[pl.ds(x, 1), :], pltpu.roll(u, 1, 0))
        beside += jnp.where(row == BY - 1, yh_ref[pl.ds(x, 1), :], pltpu.roll(u, BY - 1, 0))
        beside += jnp.where(lane == 0, 0.0, pltpu.roll(u, 1, 1))
        beside += jnp.where(lane == N - 1, 0.0, pltpu.roll(u, N - 1, 1))
        q = ABSORPTION * d + stiffness_of(m_ref[x]) * (6.0 * u - beside)
        q_ref[x] = q
        return sums[0] + to_tile(d * q), sums[1] + to_tile(r_ref[x] * d)

    zero = jnp.zeros((8, 128), F32)
    curvature, projection = lax.fori_loop(0, BX, stencil, (zero, zero))
    half = lax.broadcasted_iota(jnp.int32, (8, 128), 0) < 4
    sums = jnp.where(half, fold(curvature, 4), fold(projection, 4))
    put_modes(modes_ref[...], 0, send_ref)
    put_modes(third_modes(q_ref, c_ref), 8, send_ref)
    for j in range(PEN):
        send_ref[j, 16] = sums


def blocks_kernel(recv_ref, c_ref, ez_ref, ey_ref, fr_ref, fq_ref, send_ref, y_ref):
    for field, out_ref in enumerate((fr_ref, fq_ref)):
        for b in range(4):
            for s in range(4):
                for a in range(2):
                    t = 8 * field + 4 * a + b
                    rows = swap_units([recv_ref[8 * s + i, t] for i in range(8)])
                    for i in range(8):
                        y_ref[8 * b + i, 8 * a : 8 * a + 8, 128 * s : 128 * s + 128] = rows[i]
        out_ref[...] = matmul(y_ref[...].reshape(BX * BK, N), c_ref[...], ((1,), (1,))).reshape(BX, BK, N)
    dots = [jnp.zeros((8, 128), F32), jnp.zeros((8, 128), F32)]
    k0 = lax.axis_index("pen") * BK
    for h in range(2):
        rows = pl.ds(8 * h, 8)
        ez = jnp.concatenate(
            [jnp.full((1, N), ez_ref[k0 + 8 * h + i], F32) for i in range(8)], axis=0
        )
        rho, factor = decay(ABSORPTION / CONDUCT + ez + ey_ref[...])

        def sweep(x, carry):
            power, vr, vq, wr, wq, rq, qq = carry
            r = fr_ref[x, rows]
            q = fq_ref[x, rows]
            vr = r + rho * vr
            vq = q + rho * vq
            wr = wr + power * r
            wq = wq + power * q
            rq = rq + (vr * q + vq * r - r * q)
            qq = qq + (2.0 * vq - q) * q
            return power * rho, vr, vq, wr, wq, rq, qq

        zero = jnp.zeros((8, N), F32)
        carry = lax.fori_loop(0, BX, sweep, (jnp.ones((8, N), F32),) + (zero,) * 6)
        _, vr, vq, wr, wq, rq, qq = carry
        for t, parts in enumerate(((vr, wr), (vq, wq))):
            for side, x in enumerate(parts):
                for b in range(4):
                    for i in range(8):
                        send_ref[8 * h + i, 8 * t + 4 * side + b] = x[
                            i : i + 1, 128 * b : 128 * b + 128
                        ]
        for i, x in enumerate((rq, qq)):
            x = factor * x
            dots[i] += x[:, 0:128] + x[:, 128:256] + x[:, 256:384] + x[:, 384:512]

    sums = recv_ref[0, 16]
    for j in range(1, PEN):
        sums = sums + recv_ref[j, 16]
    row = lax.broadcasted_iota(jnp.int32, (8, 128), 0)
    four = (jnp.where(row < 4, sums, 0.0), jnp.where(row < 4, 0.0, sums), dots[0], dots[1])
    group = lax.broadcasted_iota(jnp.int32, (1, 128), 1) // 32
    packed = jnp.zeros((1, 128), F32)
    for i, x in enumerate(four):
        x = jnp.sum(x, axis=0, keepdims=True)
        x = x + pltpu.roll(x, 64, 1)
        packed = jnp.where(group == i, x + pltpu.roll(x, 32, 1), packed)
    for j in range(GRP):
        send_ref[j, 16] = packed


def interface_kernel(recv_ref, ez_ref, ey_ref, send_ref, control_ref):
    row = lax.broadcasted_iota(jnp.int32, (8, 128), 0)
    group = lax.broadcasted_iota(jnp.int32, (1, 128), 1) // 32
    sums = recv_ref[0, 16]
    for p in range(1, GRP):
        sums = sums + recv_ref[p, 16]

    def total(i):
        return jnp.full((8, 128), jnp.sum(jnp.where(group == i, sums, 0.0)), F32)

    curvature, projection, rq, qq = total(0), total(1), total(2), total(3)
    step = projection / curvature
    ez = ez_ref[lax.axis_index("pen") * BK + lax.axis_index("grp")]
    rho, factor = decay(ABSORPTION / CONDUCT + ez + ey_ref[...])
    across = rho
    for _ in range(5):
        across = across * across
    others = [recv_ref[p, 8:16].reshape(8, 128) for p in range(GRP)]
    tiles = [recv_ref[p, 0:8].reshape(8, 128) - step * others[p] for p in range(GRP)]
    zero = jnp.zeros((8, 128), F32)
    rising = [zero]
    for p in range(GRP):
        rising.append(tiles[p] + across * rising[-1])
    falling = [zero]
    for p in reversed(range(GRP)):
        falling.append(tiles[p] + across * falling[-1])
    lower = row < 4
    ends = jnp.where(lower, rising[GRP], falling[GRP])
    powers = [jnp.ones((8, 128), F32)]
    for p in range(GRP):
        powers.append(powers[-1] * across)
    whole = powers[GRP]
    images = (pltpu.roll(ends, 4, 0) + whole * ends) / (1.0 - whole * whole)
    dots = zero
    for p in range(GRP):
        state = jnp.where(
            lower,
            rising[p] + powers[p] * images,
            falling[GRP - 1 - p] + powers[GRP - 1 - p] * images,
        )
        send_ref[p, 0:8] = state.reshape(8, 1, 128)
        dots = dots + state * pltpu.roll(others[p], 4, 0)
    dots = jnp.sum(rho * factor * dots, axis=0, keepdims=True)
    for p in range(GRP):
        send_ref[p, 8] = dots
    control_ref[0] = step
    control_ref[1] = curvature
    control_ref[2] = rq - step * qq


def solve_kernel(fr_ref, fq_ref, recv_ref, control_ref, c_ref, ez_ref, ey_ref, send_ref, f_ref, u_ref, y_ref):
    step = control_ref[0, 0:1, 0:1]
    k0 = lax.axis_index("pen") * BK
    for h in range(2):
        rows = pl.ds(8 * h, 8)
        ez = jnp.concatenate(
            [jnp.full((1, N), ez_ref[k0 + 8 * h + i], F32) for i in range(8)], axis=0
        )
        rho, factor = decay(ABSORPTION / CONDUCT + ez + ey_ref[...])

        def state(side):
            return jnp.concatenate(
                [
                    jnp.concatenate(
                        [recv_ref[8 * h + i, 4 * side + b] for i in range(8)],
                        axis=0,
                    )
                    for b in range(4)
                ],
                axis=1,
            )

        def rise(x, carry):
            f = fr_ref[x, rows] - step * fq_ref[x, rows]
            carry = f + rho * carry
            f_ref[x] = f
            u_ref[x, rows] = carry
            return carry

        def fall(i, carry):
            x = BX - 1 - i
            f = f_ref[x]
            u_ref[x, rows] = factor * (u_ref[x, rows] + rho * carry)
            return f + rho * carry

        lax.fori_loop(0, BX, rise, state(0))
        lax.fori_loop(0, BX, fall, state(1))

    y_ref[...] = matmul(u_ref[...].reshape(BX * BK, N), c_ref[...], ((1,), (0,))).reshape(BX, BK, N)
    for b in range(4):
        for s in range(4):
            for a in range(2):
                rows = swap_units(
                    [y_ref[8 * b + i, 8 * a : 8 * a + 8, 128 * s : 128 * s + 128] for i in range(8)]
                )
                for i in range(8):
                    send_ref[8 * s + i, 4 * a + b] = rows[i]
    sums = recv_ref[0, 8]
    for p in range(1, GRP):
        sums = sums + recv_ref[p, 8]
    row = lax.broadcasted_iota(jnp.int32, (8, 128), 0)
    first = (row == 0) & (lax.broadcasted_iota(jnp.int32, (8, 128), 1) == 0)
    sums = jnp.where(row == 0, sums, 0.0) + jnp.where(first, control_ref[2], 0.0)
    for j in range(PEN):
        send_ref[j, 8] = sums


def finish_kernel(recv_ref, r_ref, d_ref, q_ref, control_ref, c_ref, nr_ref, nd_ref, g_ref):
    for b in range(4):
        for a in range(2):
            g_ref[:, a, :, 128 * b : 128 * b + 128] = recv_ref[:, 4 * a + b]
    sums = recv_ref[0, 8]
    for j in range(1, PEN):
        sums = sums + recv_ref[j, 8]
    step = control_ref[0, 0:1, 0:1]
    conjugacy = jnp.full((8, 128), jnp.sum(sums), F32)
    ratio = (conjugacy / control_ref[1])[0:1, 0:1]
    smoothed = matmul(g_ref[...].reshape(N, BX * BY), c_ref[...], ((0,), (0,)))
    nd_ref[...] = smoothed.reshape(BX, BY, N) - ratio * d_ref[...]
    nr_ref[...] = r_ref[...] - step * q_ref[...]


def shape(*dims):
    return jax.ShapeDtypeStruct(dims, F32)


def call(kernel, ins, outs, scratch=()):
    return pl.pallas_call(
        kernel,
        in_specs=ins,
        out_specs=[VMEM] * len(outs),
        out_shape=outs,
        scratch_shapes=[pltpu.VMEM(s, F32) if isinstance(s, tuple) else s for s in scratch],
        compiler_params=PARAMS,
    )


def exchange(x, axis):
    return lax.all_to_all(x, axis, 0, 0)


def on_device(residual, direction, material):
    matrix = jnp.asarray(dct_matrix())
    eigen = eigen_values()
    ez = jnp.asarray(eigen)
    ey_row = jnp.asarray(eigen[None, :])
    ey_tile = jnp.asarray(np.concatenate([eigen.reshape(4, 128)] * 2, 0))
    block = shape(BX, BY, N)

    xlo, xhi, ylo, yhi = call(
        faces_kernel,
        [pl.BlockSpec(memory_space=pl.ANY)] * 2,
        [shape(1, BY, N), shape(1, BY, N), shape(BX, N), shape(BX, N)],
        [
            pltpu.VMEM((BX, BY, N), F32),
            pltpu.VMEM((BX, BY, N), jnp.int32),
            pltpu.SemaphoreType.DMA((PARTS, 2)),
        ],
    )(direction, material)

    def up(x, axis, count):
        return lax.ppermute(x, axis, [(i, i + 1) for i in range(count - 1)])

    def down(x, axis, count):
        return lax.ppermute(x, axis, [(i + 1, i) for i in range(count - 1)])

    xl, xh = up(xhi, "grp", GRP), down(xlo, "grp", GRP)
    yl, yh = up(yhi, "pen", PEN), down(ylo, "pen", PEN)

    (modes_r,) = call(residual_kernel, [VMEM] * 2, [shape(N, BX * BY)])(residual, matrix)
    operated, send = call(
        operated_kernel, [VMEM] * 9, [block, shape(PEN, 17, 8, 128)], [(BX + 2, BY, N)]
    )(residual, direction, material, modes_r, xl, xh, yl, yh, matrix)

    recv = exchange(send, "pen")
    field_r, field_q, send = call(
        blocks_kernel, [VMEM, VMEM, SMEM, VMEM], [block, block, shape(GRP, 17, 1, 128)], [(BX, BK, N)]
    )(recv, matrix, ez, ey_row)

    recv = exchange(send, "grp")
    send, control = call(
        interface_kernel, [VMEM, SMEM, VMEM], [shape(GRP, 9, 1, 128), shape(3, 8, 128)]
    )(recv, ez, ey_tile)

    recv = exchange(send, "grp")
    (send,) = call(
        solve_kernel,
        [VMEM] * 5 + [SMEM, VMEM],
        [shape(PEN, 9, 8, 128)],
        [(BX, 8, N), (BX, BK, N), (BX, BK, N)],
    )(field_r, field_q, recv, control, matrix, ez, ey_row)

    recv = exchange(send, "pen")
    return tuple(
        call(finish_kernel, [VMEM] * 6, [block, block], [(PEN, 2, 8, BX * BY)])(
            recv, residual, direction, operated, control, matrix
        )
    )


def solution(mesh):
    placed = P("grp", "pen", None)
    return jax.shard_map(
        on_device,
        mesh=mesh,
        in_specs=(placed, placed, placed),
        out_specs=(placed, placed),
        check_vma=False,
    )
```

```python
import functools
import math

import jax
import jax.numpy as jnp
import numpy as np
from jax import lax
from jax.experimental import pallas as pl
from jax.experimental.pallas import tpu as pltpu
from jax.sharding import PartitionSpec as P

N = 512
GRP = 16
PEN = 32
BX = N // GRP
BY = N // PEN
PARTS = 8
BK = N // PEN
ABSORPTION = 0.02
CONDUCT = 5.0
SOLID = math.sqrt(30.0)
F32 = jnp.float32
VMEM = pl.BlockSpec(memory_space=pltpu.VMEM)
HBM = pl.BlockSpec(memory_space=pltpu.HBM)
SMEM = pl.BlockSpec(memory_space=pltpu.SMEM)
PARAMS = pltpu.CompilerParams(vmem_limit_bytes=48 * 1024 * 1024)


def dct_matrix():
    k = np.arange(N)[:, None]
    n = np.arange(N)[None, :]
    weight = np.where(k == 0, math.sqrt(1.0 / N), math.sqrt(2.0 / N))
    return (weight * np.cos(math.pi * (k * (2 * n + 1) % (4 * N)) / (2.0 * N))).astype(np.float32)


def eigen_values():
    return (4.0 * np.sin(math.pi * np.arange(N) / (2.0 * N)) ** 2).astype(np.float32)


def matmul(a, b, dims):
    return lax.dot_general(
        a, b, (dims, ((), ())), precision=lax.Precision.HIGHEST, preferred_element_type=F32
    )


def decay(shift):
    rho = 2.0 / (2.0 + shift + jnp.sqrt(shift * (shift + 4.0)))
    return rho, rho / (CONDUCT * (1.0 - rho * rho))


def swap_units(rows):
    rows = list(rows)
    unit = lax.broadcasted_iota(jnp.int32, rows[0].shape, 1) // 16
    for d in (4, 2, 1):
        keep = (unit & d) == 0
        for i in range(8):
            if i & d == 0:
                a, b = rows[i], rows[i + d]
                rows[i] = jnp.where(keep, a, pltpu.roll(b, 16 * d, 1))
                rows[i + d] = jnp.where(keep, pltpu.roll(a, 128 - 16 * d, 1), b)
    return rows


def to_tile(x):
    x = x[:8] + x[8:]
    return x[:, 0:128] + x[:, 128:256] + x[:, 256:384] + x[:, 384:512]


def fold(x, step):
    return x + pltpu.roll(x, step, 0)


def stiffness_of(material):
    return jnp.where(material == 1, jnp.float32(SOLID), jnp.float32(1.0))


def faces_kernel(d_hbm, m_hbm, xlo_ref, xhi_ref, ylo_ref, yhi_ref, d_ref, m_ref, sems):
    copies = []
    for i in range(PARTS):
        part = pl.ds(i * (BX // PARTS), BX // PARTS)
        for j, (source, target) in enumerate(((d_hbm, d_ref), (m_hbm, m_ref))):
            copies.append(pltpu.make_async_copy(source.at[part], target.at[part], sems.at[i, j]))
            copies[-1].start()
    for copy in copies:
        copy.wait()
    xlo_ref[0] = stiffness_of(m_ref[0]) * d_ref[0]
    xhi_ref[0] = stiffness_of(m_ref[BX - 1]) * d_ref[BX - 1]
    ylo_ref[...] = stiffness_of(m_ref[:, 0, :]) * d_ref[:, 0, :]
    yhi_ref[...] = stiffness_of(m_ref[:, BY - 1, :]) * d_ref[:, BY - 1, :]


def third_modes(field_ref, c_ref):
    return matmul(c_ref[...], field_ref[...].reshape(BX * BY, N), ((1,), (1,)))


def put_modes(modes, first, send_ref):
    for b in range(4):
        part = modes[:, 128 * b : 128 * b + 128].reshape(PEN, 2, 8, 128)
        for a in range(2):
            send_ref[:, first + 4 * a + b] = part[:, a]


def residual_kernel(r_ref, c_ref, send_ref):
    put_modes(third_modes(r_ref, c_ref), 0, send_ref)


def inner_kernel(r_ref, d_ref, m_ref, q_ref, sums_ref, u_ref):
    u_ref[0] = jnp.zeros((BY, N), F32)
    u_ref[BX + 1] = jnp.zeros((BY, N), F32)

    def scale(x, _):
        u_ref[x + 1] = stiffness_of(m_ref[x]) * d_ref[x]
        return 0

    lax.fori_loop(0, BX, scale, 0, unroll=4)
    row = lax.broadcasted_iota(jnp.int32, (BY, N), 0)
    lane = lax.broadcasted_iota(jnp.int32, (BY, N), 1)

    def stencil(x, sums):
        u = u_ref[x + 1]
        d = d_ref[x]
        beside = u_ref[x] + u_ref[x + 2]
        beside += jnp.where(row == 0, 0.0, pltpu.roll(u, 1, 0))
        beside += jnp.where(row == BY - 1, 0.0, pltpu.roll(u, BY - 1, 0))
        beside += jnp.where(lane == 0, 0.0, pltpu.roll(u, 1, 1))
        beside += jnp.where(lane == N - 1, 0.0, pltpu.roll(u, N - 1, 1))
        q = ABSORPTION * d + stiffness_of(m_ref[x]) * (6.0 * u - beside)
        q_ref[x] = q
        return sums[0] + to_tile(d * q), sums[1] + to_tile(r_ref[x] * d)

    zero = jnp.zeros((8, 128), F32)
    sums = lax.fori_loop(0, BX, stencil, (zero, zero), unroll=4)
    sums_ref[0], sums_ref[1] = sums


def operated_kernel(
    q_ref, sums_ref, d_ref, m_ref, xl_ref, xh_ref, yl_ref, yh_ref, c_ref, out_ref, send_ref
):
    row = lax.broadcasted_iota(jnp.int32, (8, N), 0)

    def low_high(x, total):
        for first, edge, side_ref in ((0, 0, yl_ref), (8, 7, yh_ref)):
            rows = pl.ds(first, 8)
            add = stiffness_of(m_ref[x, rows]) * jnp.where(row == edge, side_ref[pl.ds(x, 1), :], 0.0)
            out_ref[x, rows] = q_ref[x, rows] - add
            total = total + d_ref[x, rows] * add
        return total

    total = lax.fori_loop(0, BX, low_high, jnp.zeros((8, N), F32), unroll=4)
    total = jnp.concatenate([total, jnp.zeros((8, N), F32)], axis=0)
    for x, side_ref in ((0, xl_ref), (BX - 1, xh_ref)):
        add = stiffness_of(m_ref[x]) * side_ref[0]
        out_ref[x] = out_ref[x] - add
        total = total + d_ref[x] * add
    curvature = sums_ref[0] - to_tile(total)
    half = lax.broadcasted_iota(jnp.int32, (8, 128), 0) < 4
    sums = jnp.where(half, fold(curvature, 4), fold(sums_ref[1], 4))
    put_modes(third_modes(out_ref, c_ref), 0, send_ref)
    for j in range(PEN):
        send_ref[j, 8] = sums


def second_modes(recv_ref, c_ref, out_ref, y_ref):
    def part(b, _):
        for s in range(4):
            for a in range(2):
                rows = swap_units([recv_ref[8 * s + i, 4 * a + b] for i in range(8)])
                for i in range(8):
                    y_ref[8 * b + i, 8 * a : 8 * a + 8, 128 * s : 128 * s + 128] = rows[i]
        return 0

    lax.fori_loop(0, 4, part, 0)
    out_ref[...] = matmul(y_ref[...].reshape(BX * BK, N), c_ref[...], ((1,), (1,))).reshape(BX, BK, N)


def third_eigen(ez_ref, h):
    k0 = lax.axis_index("pen") * BK + 8 * h
    return jnp.concatenate([jnp.full((1, N), ez_ref[k0 + i], F32) for i in range(8)], axis=0)


def put_states(v, w, h, send_ref, first):
    for side, x in enumerate((v, w)):
        for b in range(4):
            for i in range(8):
                send_ref[8 * h + i, first + 4 * side + b] = x[i : i + 1, 128 * b : 128 * b + 128]


def residual_blocks_kernel(recv_ref, c_ref, ez_ref, ey_ref, fr_ref, states_ref, y_ref):
    second_modes(recv_ref, c_ref, fr_ref, y_ref)
    for h in range(2):
        rows = pl.ds(8 * h, 8)
        rho, _ = decay(ABSORPTION / CONDUCT + third_eigen(ez_ref, h) + ey_ref[...])

        def sweep(x, carry):
            power, v, w = carry
            f = fr_ref[x, rows]
            return power * rho, f + rho * v, w + power * f

        zero = jnp.zeros((8, N), F32)
        _, v, w = lax.fori_loop(0, BX, sweep, (jnp.ones((8, N), F32), zero, zero), unroll=4)
        put_states(v, w, h, states_ref, 0)


def operated_blocks_kernel(
    recv_ref, fr_ref, states_ref, c_ref, ez_ref, ey_ref, fq_ref, send_ref, y_ref
):
    second_modes(recv_ref, c_ref, fq_ref, y_ref)
    dots = [jnp.zeros((8, 128), F32), jnp.zeros((8, 128), F32)]
    for h in range(2):
        rows = pl.ds(8 * h, 8)
        rho, factor = decay(ABSORPTION / CONDUCT + third_eigen(ez_ref, h) + ey_ref[...])

        def sweep(x, carry):
            power, vr, vq, wq, rq, qq = carry
            r = fr_ref[x, rows]
            q = fq_ref[x, rows]
            before_r, before_q = rho * vr, rho * vq
            vq = q + before_q
            rq = rq + (before_r * q + vq * r)
            qq = qq + (vq + before_q) * q
            return power * rho, r + before_r, vq, wq + power * q, rq, qq

        zero = jnp.zeros((8, N), F32)
        carry = (jnp.ones((8, N), F32),) + (zero,) * 5
        _, _, vq, wq, rq, qq = lax.fori_loop(0, BX, sweep, carry, unroll=4)
        put_states(vq, wq, h, send_ref, 8)
        for i, x in enumerate((rq, qq)):
            x = factor * x
            dots[i] += x[:, 0:128] + x[:, 128:256] + x[:, 256:384] + x[:, 384:512]

    sums = recv_ref[0, 8]
    for j in range(1, PEN):
        sums = sums + recv_ref[j, 8]
    row = lax.broadcasted_iota(jnp.int32, (8, 128), 0)
    four = (jnp.where(row < 4, sums, 0.0), jnp.where(row < 4, 0.0, sums), dots[0], dots[1])
    group = lax.broadcasted_iota(jnp.int32, (1, 128), 1) // 32
    packed = jnp.zeros((1, 128), F32)
    for i, x in enumerate(four):
        x = jnp.sum(x, axis=0, keepdims=True)
        x = x + pltpu.roll(x, 64, 1)
        packed = jnp.where(group == i, x + pltpu.roll(x, 32, 1), packed)
    for j in range(GRP):
        send_ref[j, 0:8] = states_ref[j]
        send_ref[j, 16] = packed


def interface_kernel(recv_ref, ez_ref, ey_ref, send_ref, control_ref):
    row = lax.broadcasted_iota(jnp.int32, (8, 128), 0)
    group = lax.broadcasted_iota(jnp.int32, (1, 128), 1) // 32
    sums = recv_ref[0, 16]
    for p in range(1, GRP):
        sums = sums + recv_ref[p, 16]

    def total(i):
        return jnp.full((8, 128), jnp.sum(jnp.where(group == i, sums, 0.0)), F32)

    curvature, projection, rq, qq = total(0), total(1), total(2), total(3)
    step = projection / curvature
    ez = ez_ref[lax.axis_index("pen") * BK + lax.axis_index("grp")]
    rho, factor = decay(ABSORPTION / CONDUCT + ez + ey_ref[...])
    across = rho
    for _ in range(5):
        across = across * across
    others = [recv_ref[p, 8:16].reshape(8, 128) for p in range(GRP)]
    tiles = [recv_ref[p, 0:8].reshape(8, 128) - step * others[p] for p in range(GRP)]
    zero = jnp.zeros((8, 128), F32)
    rising = [zero]
    for p in range(GRP):
        rising.append(tiles[p] + across * rising[-1])
    falling = [zero]
    for p in reversed(range(GRP)):
        falling.append(tiles[p] + across * falling[-1])
    lower = row < 4
    ends = jnp.where(lower, rising[GRP], falling[GRP])
    powers = [jnp.ones((8, 128), F32)]
    for p in range(GRP):
        powers.append(powers[-1] * across)
    whole = powers[GRP]
    images = (pltpu.roll(ends, 4, 0) + whole * ends) / (1.0 - whole * whole)
    dots = zero
    for p in range(GRP):
        state = jnp.where(
            lower,
            rising[p] + powers[p] * images,
            falling[GRP - 1 - p] + powers[GRP - 1 - p] * images,
        )
        send_ref[p, 0:8] = state.reshape(8, 1, 128)
        dots = dots + state * pltpu.roll(others[p], 4, 0)
    dots = jnp.sum(rho * factor * dots, axis=0, keepdims=True)
    for p in range(GRP):
        send_ref[p, 8] = dots
    control_ref[0] = step
    control_ref[1] = curvature
    control_ref[2] = rq - step * qq


def solve_kernel(fr_ref, fq_ref, recv_ref, control_ref, c_ref, ez_ref, ey_ref, send_ref, f_ref, u_ref, y_ref):
    step = control_ref[0, 0:1, 0:1]
    ez = jnp.concatenate([third_eigen(ez_ref, h) for h in range(2)], axis=0)
    rho, factor = decay(ABSORPTION / CONDUCT + ez + ey_ref[...])

    def state(side):
        return jnp.concatenate(
            [
                jnp.concatenate([recv_ref[i, 4 * side + b] for i in range(BK)], axis=0)
                for b in range(4)
            ],
            axis=1,
        )

    def rise(x, carry):
        f = fr_ref[x] - step * fq_ref[x]
        carry = f + rho * carry
        f_ref[x] = f
        u_ref[x] = carry
        return carry

    def fall(i, carry):
        x = BX - 1 - i
        carry = rho * carry
        u_ref[x] = factor * (u_ref[x] + carry)
        return f_ref[x] + carry

    lax.fori_loop(0, BX, rise, state(0), unroll=4)
    lax.fori_loop(0, BX, fall, state(1), unroll=4)
    y_ref[...] = matmul(u_ref[...].reshape(BX * BK, N), c_ref[...], ((1,), (0,))).reshape(BX, BK, N)

    def part(b, _):
        for s in range(4):
            for a in range(2):
                rows = swap_units(
                    [y_ref[8 * b + i, 8 * a : 8 * a + 8, 128 * s : 128 * s + 128] for i in range(8)]
                )
                for i in range(8):
                    send_ref[8 * s + i, 4 * a + b] = rows[i]
        return 0

    lax.fori_loop(0, 4, part, 0)
    sums = recv_ref[0, 8]
    for p in range(1, GRP):
        sums = sums + recv_ref[p, 8]
    row = lax.broadcasted_iota(jnp.int32, (8, 128), 0)
    first = (row == 0) & (lax.broadcasted_iota(jnp.int32, (8, 128), 1) == 0)
    sums = jnp.where(row == 0, sums, 0.0) + jnp.where(first, control_ref[2], 0.0)
    for j in range(PEN):
        send_ref[j, 8] = sums


def new_residual_kernel(r_ref, q_ref, control_ref, out_ref):
    out_ref[...] = r_ref[...] - control_ref[0, 0:1, 0:1] * q_ref[...]


def finish_kernel(recv_ref, d_ref, control_ref, c_ref, out_ref, g_ref):
    for b in range(4):
        for a in range(2):
            g_ref[:, a, :, 128 * b : 128 * b + 128] = recv_ref[:, 4 * a + b]
    sums = recv_ref[0, 8]
    for j in range(1, PEN):
        sums = sums + recv_ref[j, 8]
    conjugacy = jnp.full((8, 128), jnp.sum(sums), F32)
    ratio = (conjugacy / control_ref[1])[0:1, 0:1]
    smoothed = matmul(g_ref[...].reshape(N, BX * BY), c_ref[...], ((0,), (0,)))
    out_ref[...] = smoothed.reshape(BX, BY, N) - ratio * d_ref[...]


def shape(*dims):
    return jax.ShapeDtypeStruct(dims, F32)


def call(kernel, ins, outs, scratch=()):
    return pl.pallas_call(
        kernel,
        in_specs=ins,
        out_specs=[VMEM] * len(outs),
        out_shape=outs,
        scratch_shapes=[pltpu.VMEM(s, F32) if isinstance(s, tuple) else s for s in scratch],
        compiler_params=PARAMS,
    )


def exchange(x, axis):
    return lax.all_to_all(x, axis, 0, 0)


def on_device(residual, direction, material):
    matrix = jnp.asarray(dct_matrix())
    eigen = eigen_values()
    ez = jnp.asarray(eigen)
    ey_row = jnp.asarray(eigen[None, :])
    ey_tile = jnp.asarray(np.concatenate([eigen.reshape(4, 128)] * 2, 0))
    block = shape(BX, BY, N)

    (send,) = call(residual_kernel, [VMEM] * 2, [shape(PEN, 8, 8, 128)])(residual, matrix)
    recv_r = exchange(send, "pen")

    xlo, xhi, ylo, yhi = call(
        faces_kernel,
        [HBM] * 2,
        [shape(1, BY, N), shape(1, BY, N), shape(BX, N), shape(BX, N)],
        [
            pltpu.VMEM((BX, BY, N), F32),
            pltpu.VMEM((BX, BY, N), jnp.int32),
            pltpu.SemaphoreType.DMA((PARTS, 2)),
        ],
    )(direction, material)

    def up(x, axis, count):
        return lax.ppermute(x, axis, [(i, i + 1) for i in range(count - 1)])

    def down(x, axis, count):
        return lax.ppermute(x, axis, [(i + 1, i) for i in range(count - 1)])

    xl, xh = up(xhi, "grp", GRP), down(xlo, "grp", GRP)
    yl, yh = up(yhi, "pen", PEN), down(ylo, "pen", PEN)

    inner, sums = call(
        inner_kernel, [VMEM] * 3, [block, shape(2, 8, 128)], [(BX + 2, BY, N)]
    )(residual, direction, material)
    operated, send = call(operated_kernel, [VMEM] * 9, [block, shape(PEN, 9, 8, 128)])(
        inner, sums, direction, material, xl, xh, yl, yh, matrix
    )
    recv_q = exchange(send, "pen")

    field_r, states = call(
        residual_blocks_kernel,
        [VMEM, VMEM, SMEM, VMEM],
        [block, shape(GRP, 8, 1, 128)],
        [(BX, BK, N)],
    )(recv_r, matrix, ez, ey_row)
    field_q, send = call(
        operated_blocks_kernel,
        [VMEM] * 4 + [SMEM, VMEM],
        [block, shape(GRP, 17, 1, 128)],
        [(BX, BK, N)],
    )(recv_q, field_r, states, matrix, ez, ey_row)

    recv = exchange(send, "grp")
    send, control = call(
        interface_kernel, [VMEM, SMEM, VMEM], [shape(GRP, 9, 1, 128), shape(3, 8, 128)]
    )(recv, ez, ey_tile)

    recv = exchange(send, "grp")
    (send,) = call(
        solve_kernel,
        [VMEM] * 5 + [SMEM, VMEM],
        [shape(PEN, 9, 8, 128)],
        [(BX, BK, N)] * 3,
    )(field_r, field_q, recv, control, matrix, ez, ey_row)

    recv = exchange(send, "pen")
    (new_residual,) = call(new_residual_kernel, [VMEM] * 3, [block])(residual, operated, control)
    (new_direction,) = call(finish_kernel, [VMEM] * 4, [block], [(PEN, 2, 8, BX * BY)])(
        recv, direction, control, matrix
    )
    return new_residual, new_direction


def solution(mesh):
    placed = P("grp", "pen", None)
    return jax.shard_map(
        on_device,
        mesh=mesh,
        in_specs=(placed, placed, placed),
        out_specs=(placed, placed),
        check_vma=False,
    )
```

```python
import functools
import math

import jax
import jax.numpy as jnp
import numpy as np
from jax import lax
from jax.experimental import pallas as pl
from jax.experimental.pallas import tpu as pltpu
from jax.sharding import PartitionSpec as P

N = 512
GRP = 16
PEN = 32
BX = N // GRP
BY = N // PEN
BK = N // PEN
ABSORPTION = 0.02
CONDUCT = 5.0
SOLID = math.sqrt(30.0)
F32 = jnp.float32
VMEM = pl.BlockSpec(memory_space=pltpu.VMEM)
HBM = pl.BlockSpec(memory_space=pltpu.HBM)
SMEM = pl.BlockSpec(memory_space=pltpu.SMEM)
PARAMS = pltpu.CompilerParams(vmem_limit_bytes=48 * 1024 * 1024)


def dct_matrix():
    k = np.arange(N)[:, None]
    n = np.arange(N)[None, :]
    weight = np.where(k == 0, math.sqrt(1.0 / N), math.sqrt(2.0 / N))
    return (weight * np.cos(math.pi * (k * (2 * n + 1) % (4 * N)) / (2.0 * N))).astype(np.float32)


def eigen_values():
    return (4.0 * np.sin(math.pi * np.arange(N) / (2.0 * N)) ** 2).astype(np.float32)


def matmul(a, b, dims):
    return lax.dot_general(
        a, b, (dims, ((), ())), precision=lax.Precision.HIGHEST, preferred_element_type=F32
    )


def decay(shift):
    rho = 2.0 / (2.0 + shift + jnp.sqrt(shift * (shift + 4.0)))
    return rho, rho / (CONDUCT * (1.0 - rho * rho))


def swap_units(rows):
    rows = list(rows)
    unit = lax.broadcasted_iota(jnp.int32, rows[0].shape, 1) // 16
    for d in (4, 2, 1):
        keep = (unit & d) == 0
        for i in range(8):
            if i & d == 0:
                a, b = rows[i], rows[i + d]
                rows[i] = jnp.where(keep, a, pltpu.roll(b, 16 * d, 1))
                rows[i + d] = jnp.where(keep, pltpu.roll(a, 128 - 16 * d, 1), b)
    return rows


def to_tile(x):
    x = x[:8] + x[8:]
    return x[:, 0:128] + x[:, 128:256] + x[:, 256:384] + x[:, 384:512]


def fold(x, step):
    return x + pltpu.roll(x, step, 0)


def stiffness_of(material):
    return jnp.where(material == 1, jnp.float32(SOLID), jnp.float32(1.0))


def faces_kernel(d_ref, m_ref, xlo_ref, xhi_ref, ylo_ref, yhi_ref):
    xlo_ref[0] = stiffness_of(m_ref[0]) * d_ref[0]
    xhi_ref[0] = stiffness_of(m_ref[BX - 1]) * d_ref[BX - 1]
    ylo_ref[...] = stiffness_of(m_ref[:, 0, :]) * d_ref[:, 0, :]
    yhi_ref[...] = stiffness_of(m_ref[:, BY - 1, :]) * d_ref[:, BY - 1, :]


def start(copies):
    for copy in copies:
        copy.start()
    return copies


def wait(copies):
    for copy in copies:
        copy.wait()


def send_third_modes(field_ref, c_ref, ready, send_ref, send_hbm, sems):
    copies = []
    for h in range(2):
        ready(h)
        field = field_ref[16 * h : 16 * h + 16].reshape(16 * BY, N)
        modes = matmul(c_ref[...], field, ((1,), (1,)))
        for b in range(2):
            part = modes[:, 128 * b : 128 * b + 128].reshape(PEN, 2, 8, 128)
            for a in range(2):
                tile = 4 * a + 2 * h + b
                send_ref[:, tile] = part[:, a]
        for a in range(2):
            tiles = pl.ds(4 * a + 2 * h, 2)
            copies += start(
                [pltpu.make_async_copy(send_ref.at[:, tiles], send_hbm.at[:, tiles], sems.at[2 * h + a])]
            )
    return copies


def residual_kernel(r_hbm, c_hbm, send_hbm, r_ref, c_ref, send_ref, sems):
    into_c = [
        pltpu.make_async_copy(c_hbm.at[rows], c_ref.at[rows], sems.at[4 + i])
        for i, rows in enumerate(pl.ds(128 * i, 128) for i in range(4))
    ]
    into_r = [
        pltpu.make_async_copy(r_hbm.at[part], r_ref.at[part], sems.at[8 + i])
        for i, part in enumerate(pl.ds(8 * i, 8) for i in range(4))
    ]
    for i in (0, 1):
        start(into_c[2 * i : 2 * i + 2] + into_r[2 * i : 2 * i + 2])

    def ready(h):
        if h == 0:
            wait(into_c)
        wait(into_r[2 * h : 2 * h + 2])

    wait(send_third_modes(r_ref, c_ref, ready, send_ref, send_hbm, sems))


def inner_kernel(r_ref, d_ref, m_ref, q_ref, sums_ref, u_ref):
    u_ref[0] = jnp.zeros((BY, N), F32)
    u_ref[BX + 1] = jnp.zeros((BY, N), F32)

    def scale(x, _):
        u_ref[x + 1] = stiffness_of(m_ref[x]) * d_ref[x]
        return 0

    lax.fori_loop(0, BX, scale, 0, unroll=4)
    row = lax.broadcasted_iota(jnp.int32, (BY, N), 0)
    lane = lax.broadcasted_iota(jnp.int32, (BY, N), 1)

    def stencil(x, sums):
        u = u_ref[x + 1]
        d = d_ref[x]
        beside = u_ref[x] + u_ref[x + 2]
        beside += jnp.where(row == 0, 0.0, pltpu.roll(u, 1, 0))
        beside += jnp.where(row == BY - 1, 0.0, pltpu.roll(u, BY - 1, 0))
        beside += jnp.where(lane == 0, 0.0, pltpu.roll(u, 1, 1))
        beside += jnp.where(lane == N - 1, 0.0, pltpu.roll(u, N - 1, 1))
        q = ABSORPTION * d + stiffness_of(m_ref[x]) * (6.0 * u - beside)
        q_ref[x] = q
        return sums[0] + to_tile(d * q), sums[1] + to_tile(r_ref[x] * d)

    zero = jnp.zeros((8, 128), F32)
    sums = lax.fori_loop(0, BX, stencil, (zero, zero), unroll=4)
    sums_ref[0], sums_ref[1] = sums


def operated_kernel(
    q_ref, sums_ref, d_ref, m_ref, xl_ref, xh_ref, yl_ref, yh_ref, c_ref, out_hbm, send_hbm, out_ref, send_ref, sems
):
    row = lax.broadcasted_iota(jnp.int32, (8, N), 0)

    def low_high(x, total):
        for first, edge, side_ref in ((0, 0, yl_ref), (8, 7, yh_ref)):
            rows = pl.ds(first, 8)
            add = stiffness_of(m_ref[x, rows]) * jnp.where(row == edge, side_ref[pl.ds(x, 1), :], 0.0)
            out_ref[x, rows] = q_ref[x, rows] - add
            total = total + d_ref[x, rows] * add
        return total

    total = lax.fori_loop(0, BX, low_high, jnp.zeros((8, N), F32), unroll=4)
    total = jnp.concatenate([total, jnp.zeros((8, N), F32)], axis=0)
    for x, side_ref in ((0, xl_ref), (BX - 1, xh_ref)):
        add = stiffness_of(m_ref[x]) * side_ref[0]
        out_ref[x] = out_ref[x] - add
        total = total + d_ref[x] * add
    curvature = sums_ref[0] - to_tile(total)
    half = lax.broadcasted_iota(jnp.int32, (8, 128), 0) < 4
    sums = jnp.where(half, fold(curvature, 4), fold(sums_ref[1], 4))
    for j in range(PEN):
        send_ref[j, 8] = sums
    copies = start(
        [
            pltpu.make_async_copy(out_ref, out_hbm, sems.at[4]),
            pltpu.make_async_copy(send_ref.at[:, pl.ds(8, 1)], send_hbm.at[:, pl.ds(8, 1)], sems.at[5]),
        ]
    )
    copies += send_third_modes(out_ref, c_ref, lambda h: None, send_ref, send_hbm, sems)
    wait(copies)


def second_modes(recv_ref, c_ref, out_ref, y_ref, ready=lambda b: None):
    def part(b, _):
        ready(b)
        for s in range(4):
            for a in range(2):
                rows = swap_units([recv_ref[8 * s + i, 4 * a + b] for i in range(8)])
                for i in range(8):
                    y_ref[8 * b + i, 8 * a : 8 * a + 8, 128 * s : 128 * s + 128] = rows[i]
        return 0

    lax.fori_loop(0, 4, part, 0)
    out_ref[...] = matmul(y_ref[...].reshape(BX * BK, N), c_ref[...], ((1,), (1,))).reshape(BX, BK, N)


def third_eigen(ez_ref, h):
    k0 = lax.axis_index("pen") * BK + 8 * h
    return jnp.concatenate([jnp.full((1, N), ez_ref[k0 + i], F32) for i in range(8)], axis=0)


def put_states(v, w, h, send_ref, first):
    for side, x in enumerate((v, w)):
        for b in range(4):
            for i in range(8):
                send_ref[8 * h + i, first + 4 * side + b] = x[i : i + 1, 128 * b : 128 * b + 128]


def residual_blocks_kernel(recv_ref, c_ref, ez_ref, ey_ref, fr_hbm, states_ref, y_ref, fr_ref, sem):
    second_modes(recv_ref, c_ref, fr_ref, y_ref)
    copies = start([pltpu.make_async_copy(fr_ref, fr_hbm, sem)])
    for h in range(2):
        rows = pl.ds(8 * h, 8)
        rho, _ = decay(ABSORPTION / CONDUCT + third_eigen(ez_ref, h) + ey_ref[...])

        def sweep(x, carry):
            power, v, w = carry
            f = fr_ref[x, rows]
            return power * rho, f + rho * v, w + power * f

        zero = jnp.zeros((8, N), F32)
        _, v, w = lax.fori_loop(0, BX, sweep, (jnp.ones((8, N), F32), zero, zero), unroll=4)
        put_states(v, w, h, states_ref, 0)
    wait(copies)


def operated_blocks_kernel(
    recv_hbm, fr_hbm, states_ref, c_ref, ez_ref, ey_ref, fq_ref, send_ref, y_ref, recv_ref, fr_ref, sems
):
    def into(b):
        tiles = [b, b + 4]
        return [
            pltpu.make_async_copy(recv_hbm.at[:, t], recv_ref.at[:, t], sems.at[i, b])
            for i, t in enumerate(tiles)
        ]

    for b in range(4):
        start(into(b))
    late = start(
        [
            pltpu.make_async_copy(recv_hbm.at[:, 8], recv_ref.at[:, 8], sems.at[2, 0]),
            pltpu.make_async_copy(fr_hbm, fr_ref, sems.at[2, 1]),
        ]
    )
    second_modes(recv_ref, c_ref, fq_ref, y_ref, lambda b: wait(into(b)))
    wait(late)
    dots = [jnp.zeros((8, 128), F32), jnp.zeros((8, 128), F32)]
    for h in range(2):
        rows = pl.ds(8 * h, 8)
        rho, factor = decay(ABSORPTION / CONDUCT + third_eigen(ez_ref, h) + ey_ref[...])

        def sweep(x, carry):
            power, vr, vq, wq, rq, qq = carry
            r = fr_ref[x, rows]
            q = fq_ref[x, rows]
            before_r, before_q = rho * vr, rho * vq
            vq = q + before_q
            rq = rq + (before_r * q + vq * r)
            qq = qq + (vq + before_q) * q
            return power * rho, r + before_r, vq, wq + power * q, rq, qq

        zero = jnp.zeros((8, N), F32)
        carry = (jnp.ones((8, N), F32),) + (zero,) * 5
        _, _, vq, wq, rq, qq = lax.fori_loop(0, BX, sweep, carry, unroll=4)
        put_states(vq, wq, h, send_ref, 8)
        for i, x in enumerate((rq, qq)):
            x = factor * x
            dots[i] += x[:, 0:128] + x[:, 128:256] + x[:, 256:384] + x[:, 384:512]

    sums = recv_ref[0, 8]
    for j in range(1, PEN):
        sums = sums + recv_ref[j, 8]
    row = lax.broadcasted_iota(jnp.int32, (8, 128), 0)
    four = (jnp.where(row < 4, sums, 0.0), jnp.where(row < 4, 0.0, sums), dots[0], dots[1])
    group = lax.broadcasted_iota(jnp.int32, (1, 128), 1) // 32
    packed = jnp.zeros((1, 128), F32)
    for i, x in enumerate(four):
        x = jnp.sum(x, axis=0, keepdims=True)
        x = x + pltpu.roll(x, 64, 1)
        packed = jnp.where(group == i, x + pltpu.roll(x, 32, 1), packed)
    for j in range(GRP):
        send_ref[j, 0:8] = states_ref[j]
        send_ref[j, 16] = packed


def interface_kernel(recv_ref, ez_ref, ey_ref, send_ref, control_ref):
    row = lax.broadcasted_iota(jnp.int32, (8, 128), 0)
    group = lax.broadcasted_iota(jnp.int32, (1, 128), 1) // 32
    sums = recv_ref[0, 16]
    for p in range(1, GRP):
        sums = sums + recv_ref[p, 16]

    def total(i):
        return jnp.full((8, 128), jnp.sum(jnp.where(group == i, sums, 0.0)), F32)

    curvature, projection, rq, qq = total(0), total(1), total(2), total(3)
    step = projection / curvature
    ez = ez_ref[lax.axis_index("pen") * BK + lax.axis_index("grp")]
    rho, factor = decay(ABSORPTION / CONDUCT + ez + ey_ref[...])
    across = rho
    for _ in range(5):
        across = across * across
    others = [recv_ref[p, 8:16].reshape(8, 128) for p in range(GRP)]
    tiles = [recv_ref[p, 0:8].reshape(8, 128) - step * others[p] for p in range(GRP)]
    zero = jnp.zeros((8, 128), F32)
    rising = [zero]
    for p in range(GRP):
        rising.append(tiles[p] + across * rising[-1])
    falling = [zero]
    for p in reversed(range(GRP)):
        falling.append(tiles[p] + across * falling[-1])
    lower = row < 4
    ends = jnp.where(lower, rising[GRP], falling[GRP])
    powers = [jnp.ones((8, 128), F32)]
    for p in range(GRP):
        powers.append(powers[-1] * across)
    whole = powers[GRP]
    images = (pltpu.roll(ends, 4, 0) + whole * ends) / (1.0 - whole * whole)
    dots = zero
    for p in range(GRP):
        state = jnp.where(
            lower,
            rising[p] + powers[p] * images,
            falling[GRP - 1 - p] + powers[GRP - 1 - p] * images,
        )
        send_ref[p, 0:8] = state.reshape(8, 1, 128)
        dots = dots + state * pltpu.roll(others[p], 4, 0)
    dots = jnp.sum(rho * factor * dots, axis=0, keepdims=True)
    for p in range(GRP):
        send_ref[p, 8] = dots
    control_ref[0] = step
    control_ref[1] = curvature
    control_ref[2] = rq - step * qq


def solve_kernel(fr_ref, fq_ref, recv_ref, control_ref, c_ref, ez_ref, ey_ref, send_ref, f_ref, u_ref, y_ref):
    step = control_ref[0, 0:1, 0:1]
    ez = jnp.concatenate([third_eigen(ez_ref, h) for h in range(2)], axis=0)
    rho, factor = decay(ABSORPTION / CONDUCT + ez + ey_ref[...])

    def state(side):
        return jnp.concatenate(
            [
                jnp.concatenate([recv_ref[i, 4 * side + b] for i in range(BK)], axis=0)
                for b in range(4)
            ],
            axis=1,
        )

    def rise(x, carry):
        f = fr_ref[x] - step * fq_ref[x]
        carry = f + rho * carry
        f_ref[x] = f
        u_ref[x] = carry
        return carry

    def fall(i, carry):
        x = BX - 1 - i
        carry = rho * carry
        u_ref[x] = factor * (u_ref[x] + carry)
        return f_ref[x] + carry

    lax.fori_loop(0, BX, rise, state(0), unroll=4)
    lax.fori_loop(0, BX, fall, state(1), unroll=4)
    y_ref[...] = matmul(u_ref[...].reshape(BX * BK, N), c_ref[...], ((1,), (0,))).reshape(BX, BK, N)

    def part(b, _):
        for s in range(4):
            for a in range(2):
                rows = swap_units(
                    [y_ref[8 * b + i, 8 * a : 8 * a + 8, 128 * s : 128 * s + 128] for i in range(8)]
                )
                for i in range(8):
                    send_ref[8 * s + i, 4 * a + b] = rows[i]
        return 0

    lax.fori_loop(0, 4, part, 0)
    sums = recv_ref[0, 8]
    for p in range(1, GRP):
        sums = sums + recv_ref[p, 8]
    row = lax.broadcasted_iota(jnp.int32, (8, 128), 0)
    first = (row == 0) & (lax.broadcasted_iota(jnp.int32, (8, 128), 1) == 0)
    sums = jnp.where(row == 0, sums, 0.0) + jnp.where(first, control_ref[2], 0.0)
    for j in range(PEN):
        send_ref[j, 8] = sums


def finish_kernel(
    recv_ref, r_ref, d_ref, q_ref, control_ref, c_ref, nr_hbm, nd_hbm, g_ref, nr_ref, nd_ref, sems
):
    nr_ref[...] = r_ref[...] - control_ref[0, 0:1, 0:1] * q_ref[...]
    copies = start([pltpu.make_async_copy(nr_ref, nr_hbm, sems.at[0])])
    for b in range(4):
        for a in range(2):
            g_ref[:, a, :, 128 * b : 128 * b + 128] = recv_ref[:, 4 * a + b]
    sums = recv_ref[0, 8]
    for j in range(1, PEN):
        sums = sums + recv_ref[j, 8]
    conjugacy = jnp.full((8, 128), jnp.sum(sums), F32)
    ratio = (conjugacy / control_ref[1])[0:1, 0:1]
    for h in range(2):
        part = pl.ds(16 * h, 16)
        half = g_ref[:, :, :, 256 * h : 256 * h + 256].reshape(N, 256)
        smoothed = matmul(half, c_ref[...], ((0,), (0,)))
        nd_ref[part] = smoothed.reshape(16, BY, N) - ratio * d_ref[part]
        copies += start([pltpu.make_async_copy(nd_ref.at[part], nd_hbm.at[part], sems.at[1 + h])])
    wait(copies)


def shape(*dims):
    return jax.ShapeDtypeStruct(dims, F32)


def in_hbm(x):
    return pltpu.with_memory_space_constraint(x, pltpu.HBM)


def call(kernel, ins, outs, scratch=()):
    return pl.pallas_call(
        kernel,
        in_specs=ins,
        out_specs=[VMEM if isinstance(out, jax.ShapeDtypeStruct) else HBM for out in outs],
        out_shape=outs,
        scratch_shapes=[pltpu.VMEM(s, F32) if isinstance(s, tuple) else s for s in scratch],
        compiler_params=PARAMS,
    )


def exchange(x, axis):
    return lax.all_to_all(x, axis, 0, 0)


def on_device(residual, direction, material):
    matrix = jnp.asarray(dct_matrix())
    eigen = eigen_values()
    ez = jnp.asarray(eigen)
    ey_row = jnp.asarray(eigen[None, :])
    ey_tile = jnp.asarray(np.concatenate([eigen.reshape(4, 128)] * 2, 0))
    block = shape(BX, BY, N)

    (send,) = call(
        residual_kernel,
        [HBM] * 2,
        [pltpu.HBM((PEN, 8, 8, 128), F32)],
        [(BX, BY, N), (N, N), (PEN, 8, 8, 128), pltpu.SemaphoreType.DMA((12,))],
    )(in_hbm(residual), in_hbm(matrix))
    recv_r = exchange(send, "pen")

    xlo, xhi, ylo, yhi = call(
        faces_kernel, [VMEM] * 2, [shape(1, BY, N), shape(1, BY, N), shape(BX, N), shape(BX, N)]
    )(direction, material)

    def up(x, axis, count):
        return lax.ppermute(x, axis, [(i, i + 1) for i in range(count - 1)])

    def down(x, axis, count):
        return lax.ppermute(x, axis, [(i + 1, i) for i in range(count - 1)])

    xl, xh = up(xhi, "grp", GRP), down(xlo, "grp", GRP)
    yl, yh = up(yhi, "pen", PEN), down(ylo, "pen", PEN)

    inner, sums = call(
        inner_kernel, [VMEM] * 3, [block, shape(2, 8, 128)], [(BX + 2, BY, N)]
    )(residual, direction, material)
    operated, send = call(
        operated_kernel,
        [VMEM] * 9,
        [pltpu.HBM((BX, BY, N), F32), pltpu.HBM((PEN, 9, 8, 128), F32)],
        [(BX, BY, N), (PEN, 9, 8, 128), pltpu.SemaphoreType.DMA((6,))],
    )(inner, sums, direction, material, xl, xh, yl, yh, matrix)
    recv_q = exchange(send, "pen")

    field_r, states = call(
        residual_blocks_kernel,
        [VMEM, VMEM, SMEM, VMEM],
        [pltpu.HBM((BX, BK, N), F32), shape(GRP, 8, 1, 128)],
        [(BX, BK, N), (BX, BK, N), pltpu.SemaphoreType.DMA],
    )(recv_r, matrix, ez, ey_row)
    field_q, send = call(
        operated_blocks_kernel,
        [HBM, HBM, VMEM, VMEM, SMEM, VMEM],
        [block, shape(GRP, 17, 1, 128)],
        [(BX, BK, N), (PEN, 9, 8, 128), (BX, BK, N), pltpu.SemaphoreType.DMA((3, 4))],
    )(in_hbm(recv_q), in_hbm(field_r), states, matrix, ez, ey_row)

    recv = exchange(send, "grp")
    send, control = call(
        interface_kernel, [VMEM, SMEM, VMEM], [shape(GRP, 9, 1, 128), shape(3, 8, 128)]
    )(recv, ez, ey_tile)

    recv = exchange(send, "grp")
    (send,) = call(
        solve_kernel,
        [VMEM] * 5 + [SMEM, VMEM],
        [shape(PEN, 9, 8, 128)],
        [(BX, BK, N)] * 3,
    )(field_r, field_q, recv, control, matrix, ez, ey_row)

    recv = exchange(send, "pen")
    return tuple(
        call(
            finish_kernel,
            [VMEM] * 6,
            [pltpu.HBM((BX, BY, N), F32), pltpu.HBM((BX, BY, N), F32)],
            [(PEN, 2, 8, BX * BY), (BX, BY, N), (BX, BY, N), pltpu.SemaphoreType.DMA((3,))],
        )(recv, residual, direction, operated, control, matrix)
    )


def solution(mesh):
    placed = P("grp", "pen", None)
    return jax.shard_map(
        on_device,
        mesh=mesh,
        in_specs=(placed, placed, placed),
        out_specs=(placed, placed),
        check_vma=False,
    )
```

```python
import functools
import math

import jax
import jax.numpy as jnp
import numpy as np
from jax import lax
from jax.experimental import pallas as pl
from jax.experimental.pallas import tpu as pltpu
from jax.sharding import PartitionSpec as P

N = 512
GRP = 16
PEN = 32
BX = N // GRP
BY = N // PEN
BK = N // PEN
ABSORPTION = 0.02
CONDUCT = 5.0
SOLID = math.sqrt(30.0)
F32 = jnp.float32
VMEM = pl.BlockSpec(memory_space=pltpu.VMEM)
HBM = pl.BlockSpec(memory_space=pltpu.HBM)
SMEM = pl.BlockSpec(memory_space=pltpu.SMEM)
PARAMS = pltpu.CompilerParams(vmem_limit_bytes=48 * 1024 * 1024)


def dct_matrix():
    k = np.arange(N)[:, None]
    n = np.arange(N)[None, :]
    weight = np.where(k == 0, math.sqrt(1.0 / N), math.sqrt(2.0 / N))
    return weight * np.cos(math.pi * (k * (2 * n + 1) % (4 * N)) / (2.0 * N))


def eigen_values():
    return (4.0 * np.sin(math.pi * np.arange(N) / (2.0 * N)) ** 2).astype(np.float32)


def halves(x):
    high = x.astype(jnp.bfloat16)
    return high, (x - high.astype(F32)).astype(jnp.bfloat16)


def product(a, b, dims):
    def one(x, y):
        return lax.dot_general(x, y, (dims, ((), ())), preferred_element_type=F32)

    return one(a[0], b[0]) + (one(a[0], b[1]) + one(a[1], b[0]))


def whole(refs):
    return tuple(ref[...] for ref in refs)


def decay(shift):
    rho = 2.0 / (2.0 + shift + jnp.sqrt(shift * (shift + 4.0)))
    return rho, rho / (CONDUCT * (1.0 - rho * rho))


def swap_units(rows):
    rows = list(rows)
    unit = lax.broadcasted_iota(jnp.int32, rows[0].shape, 1) // 16
    for d in (4, 2, 1):
        keep = (unit & d) == 0
        for i in range(8):
            if i & d == 0:
                a, b = rows[i], rows[i + d]
                rows[i] = jnp.where(keep, a, pltpu.roll(b, 16 * d, 1))
                rows[i + d] = jnp.where(keep, pltpu.roll(a, 128 - 16 * d, 1), b)
    return rows


def to_tile(x):
    x = x[:8] + x[8:]
    return x[:, 0:128] + x[:, 128:256] + x[:, 256:384] + x[:, 384:512]


def fold(x, step):
    return x + pltpu.roll(x, step, 0)


def stiffness_of(material):
    return jnp.where(material == 1, jnp.float32(SOLID), jnp.float32(1.0))


def faces_kernel(d_ref, m_ref, xlo_ref, xhi_ref, ylo_ref, yhi_ref):
    xlo_ref[0] = stiffness_of(m_ref[0]) * d_ref[0]
    xhi_ref[0] = stiffness_of(m_ref[BX - 1]) * d_ref[BX - 1]
    ylo_ref[...] = stiffness_of(m_ref[:, 0, :]) * d_ref[:, 0, :]
    yhi_ref[...] = stiffness_of(m_ref[:, BY - 1, :]) * d_ref[:, BY - 1, :]


def start(copies):
    for copy in copies:
        copy.start()
    return copies


def wait(copies):
    for copy in copies:
        copy.wait()


def third_modes(field_ref, c_refs, send_ref):
    modes = product(whole(c_refs), halves(field_ref[...].reshape(BX * BY, N)), ((1,), (1,)))
    for b in range(4):
        part = modes[:, 128 * b : 128 * b + 128].reshape(PEN, 2, 8, 128)
        for a in range(2):
            send_ref[:, 4 * a + b] = part[:, a]


def residual_kernel(r_hbm, ch_hbm, cl_hbm, send_hbm, r_ref, ch_ref, cl_ref, send_ref, sems):
    wait(
        start(
            [
                pltpu.make_async_copy(r_hbm, r_ref, sems.at[0]),
                pltpu.make_async_copy(ch_hbm, ch_ref, sems.at[1]),
                pltpu.make_async_copy(cl_hbm, cl_ref, sems.at[2]),
            ]
        )
    )
    third_modes(r_ref, (ch_ref, cl_ref), send_ref)
    wait(start([pltpu.make_async_copy(send_ref, send_hbm, sems.at[3])]))


def inner_kernel(r_ref, d_ref, m_ref, q_ref, sums_ref, u_ref):
    u_ref[0] = jnp.zeros((BY, N), F32)
    u_ref[BX + 1] = jnp.zeros((BY, N), F32)

    def scale(x, _):
        u_ref[x + 1] = stiffness_of(m_ref[x]) * d_ref[x]
        return 0

    lax.fori_loop(0, BX, scale, 0, unroll=4)
    row = lax.broadcasted_iota(jnp.int32, (BY, N), 0)
    lane = lax.broadcasted_iota(jnp.int32, (BY, N), 1)

    def stencil(x, sums):
        u = u_ref[x + 1]
        d = d_ref[x]
        beside = u_ref[x] + u_ref[x + 2]
        beside += jnp.where(row == 0, 0.0, pltpu.roll(u, 1, 0))
        beside += jnp.where(row == BY - 1, 0.0, pltpu.roll(u, BY - 1, 0))
        beside += jnp.where(lane == 0, 0.0, pltpu.roll(u, 1, 1))
        beside += jnp.where(lane == N - 1, 0.0, pltpu.roll(u, N - 1, 1))
        q = ABSORPTION * d + stiffness_of(m_ref[x]) * (6.0 * u - beside)
        q_ref[x] = q
        return sums[0] + to_tile(d * q), sums[1] + to_tile(r_ref[x] * d)

    zero = jnp.zeros((8, 128), F32)
    sums = lax.fori_loop(0, BX, stencil, (zero, zero), unroll=4)
    sums_ref[0], sums_ref[1] = sums


def operated_kernel(
    q_ref, sums_ref, d_ref, m_ref, xl_ref, xh_ref, yl_ref, yh_ref, ch_ref, cl_ref, out_hbm, send_hbm, out_ref, send_ref, sems
):
    row = lax.broadcasted_iota(jnp.int32, (8, N), 0)

    def low_high(x, total):
        for first, edge, side_ref in ((0, 0, yl_ref), (8, 7, yh_ref)):
            rows = pl.ds(first, 8)
            add = stiffness_of(m_ref[x, rows]) * jnp.where(row == edge, side_ref[pl.ds(x, 1), :], 0.0)
            out_ref[x, rows] = q_ref[x, rows] - add
            total = total + d_ref[x, rows] * add
        return total

    total = lax.fori_loop(0, BX, low_high, jnp.zeros((8, N), F32), unroll=4)
    total = jnp.concatenate([total, jnp.zeros((8, N), F32)], axis=0)
    for x, side_ref in ((0, xl_ref), (BX - 1, xh_ref)):
        add = stiffness_of(m_ref[x]) * side_ref[0]
        out_ref[x] = out_ref[x] - add
        total = total + d_ref[x] * add
    curvature = sums_ref[0] - to_tile(total)
    half = lax.broadcasted_iota(jnp.int32, (8, 128), 0) < 4
    sums = jnp.where(half, fold(curvature, 4), fold(sums_ref[1], 4))
    for j in range(PEN):
        send_ref[j, 8] = sums
    copies = start([pltpu.make_async_copy(out_ref, out_hbm, sems.at[0])])
    third_modes(out_ref, (ch_ref, cl_ref), send_ref)
    wait(copies + start([pltpu.make_async_copy(send_ref, send_hbm, sems.at[1])]))


def second_modes(recv_ref, c_refs, out_ref, y_ref, ready=lambda b: None):
    def part(b, _):
        ready(b)
        for s in range(4):
            for a in range(2):
                rows = swap_units([recv_ref[8 * s + i, 4 * a + b] for i in range(8)])
                for i in range(8):
                    y_ref[8 * b + i, 8 * a : 8 * a + 8, 128 * s : 128 * s + 128] = rows[i]
        return 0

    lax.fori_loop(0, 4, part, 0)
    field = halves(y_ref[...].reshape(BX * BK, N))
    out_ref[...] = product(field, whole(c_refs), ((1,), (1,))).reshape(BX, BK, N)


def third_eigen(ez_ref, h):
    k0 = lax.axis_index("pen") * BK + 8 * h
    return jnp.concatenate([jnp.full((1, N), ez_ref[k0 + i], F32) for i in range(8)], axis=0)


def put_states(v, w, h, send_ref, first):
    for side, x in enumerate((v, w)):
        for b in range(4):
            for i in range(8):
                send_ref[8 * h + i, first + 4 * side + b] = x[i : i + 1, 128 * b : 128 * b + 128]


def residual_blocks_kernel(
    recv_ref, ch_ref, cl_ref, ez_ref, ey_ref, fr_hbm, states_ref, y_ref, fr_ref, sem
):
    second_modes(recv_ref, (ch_ref, cl_ref), fr_ref, y_ref)
    copies = start([pltpu.make_async_copy(fr_ref, fr_hbm, sem)])
    for h in range(2):
        rows = pl.ds(8 * h, 8)
        rho, _ = decay(ABSORPTION / CONDUCT + third_eigen(ez_ref, h) + ey_ref[...])

        def sweep(x, carry):
            power, v, w = carry
            f = fr_ref[x, rows]
            return power * rho, f + rho * v, w + power * f

        zero = jnp.zeros((8, N), F32)
        _, v, w = lax.fori_loop(0, BX, sweep, (jnp.ones((8, N), F32), zero, zero), unroll=4)
        put_states(v, w, h, states_ref, 0)
    wait(copies)


def operated_blocks_kernel(
    recv_hbm, fr_hbm, states_ref, ch_ref, cl_ref, ez_ref, ey_ref, fq_ref, send_ref, y_ref, recv_ref, fr_ref, sems
):
    def into(b):
        tiles = [b, b + 4]
        return [
            pltpu.make_async_copy(recv_hbm.at[:, t], recv_ref.at[:, t], sems.at[i, b])
            for i, t in enumerate(tiles)
        ]

    for b in range(4):
        start(into(b))
    late = start(
        [
            pltpu.make_async_copy(recv_hbm.at[:, 8], recv_ref.at[:, 8], sems.at[2, 0]),
            pltpu.make_async_copy(fr_hbm, fr_ref, sems.at[2, 1]),
        ]
    )
    second_modes(recv_ref, (ch_ref, cl_ref), fq_ref, y_ref, lambda b: wait(into(b)))
    wait(late)
    dots = [jnp.zeros((8, 128), F32), jnp.zeros((8, 128), F32)]
    for h in range(2):
        rows = pl.ds(8 * h, 8)
        rho, factor = decay(ABSORPTION / CONDUCT + third_eigen(ez_ref, h) + ey_ref[...])

        def sweep(x, carry):
            power, vr, vq, wq, rq, qq = carry
            r = fr_ref[x, rows]
            q = fq_ref[x, rows]
            before_r, before_q = rho * vr, rho * vq
            vq = q + before_q
            rq = rq + (before_r * q + vq * r)
            qq = qq + (vq + before_q) * q
            return power * rho, r + before_r, vq, wq + power * q, rq, qq

        zero = jnp.zeros((8, N), F32)
        carry = (jnp.ones((8, N), F32),) + (zero,) * 5
        _, _, vq, wq, rq, qq = lax.fori_loop(0, BX, sweep, carry, unroll=4)
        put_states(vq, wq, h, send_ref, 8)
        for i, x in enumerate((rq, qq)):
            x = factor * x
            dots[i] += x[:, 0:128] + x[:, 128:256] + x[:, 256:384] + x[:, 384:512]

    sums = recv_ref[0, 8]
    for j in range(1, PEN):
        sums = sums + recv_ref[j, 8]
    row = lax.broadcasted_iota(jnp.int32, (8, 128), 0)
    four = (jnp.where(row < 4, sums, 0.0), jnp.where(row < 4, 0.0, sums), dots[0], dots[1])
    group = lax.broadcasted_iota(jnp.int32, (1, 128), 1) // 32
    packed = jnp.zeros((1, 128), F32)
    for i, x in enumerate(four):
        x = jnp.sum(x, axis=0, keepdims=True)
        x = x + pltpu.roll(x, 64, 1)
        packed = jnp.where(group == i, x + pltpu.roll(x, 32, 1), packed)
    for j in range(GRP):
        send_ref[j, 0:8] = states_ref[j]
        send_ref[j, 16] = packed


def interface_kernel(recv_ref, ez_ref, ey_ref, send_ref, control_ref):
    row = lax.broadcasted_iota(jnp.int32, (8, 128), 0)
    group = lax.broadcasted_iota(jnp.int32, (1, 128), 1) // 32
    sums = recv_ref[0, 16]
    for p in range(1, GRP):
        sums = sums + recv_ref[p, 16]

    def total(i):
        return jnp.full((8, 128), jnp.sum(jnp.where(group == i, sums, 0.0)), F32)

    curvature, projection, rq, qq = total(0), total(1), total(2), total(3)
    step = projection / curvature
    ez = ez_ref[lax.axis_index("pen") * BK + lax.axis_index("grp")]
    rho, factor = decay(ABSORPTION / CONDUCT + ez + ey_ref[...])
    across = rho
    for _ in range(5):
        across = across * across
    others = [recv_ref[p, 8:16].reshape(8, 128) for p in range(GRP)]
    tiles = [recv_ref[p, 0:8].reshape(8, 128) - step * others[p] for p in range(GRP)]
    zero = jnp.zeros((8, 128), F32)
    rising = [zero]
    for p in range(GRP):
        rising.append(tiles[p] + across * rising[-1])
    falling = [zero]
    for p in reversed(range(GRP)):
        falling.append(tiles[p] + across * falling[-1])
    lower = row < 4
    ends = jnp.where(lower, rising[GRP], falling[GRP])
    powers = [jnp.ones((8, 128), F32)]
    for p in range(GRP):
        powers.append(powers[-1] * across)
    whole = powers[GRP]
    images = (pltpu.roll(ends, 4, 0) + whole * ends) / (1.0 - whole * whole)
    dots = zero
    for p in range(GRP):
        state = jnp.where(
            lower,
            rising[p] + powers[p] * images,
            falling[GRP - 1 - p] + powers[GRP - 1 - p] * images,
        )
        send_ref[p, 0:8] = state.reshape(8, 1, 128)
        dots = dots + state * pltpu.roll(others[p], 4, 0)
    dots = jnp.sum(rho * factor * dots, axis=0, keepdims=True)
    for p in range(GRP):
        send_ref[p, 8] = dots
    control_ref[0] = step
    control_ref[1] = curvature
    control_ref[2] = rq - step * qq


def solve_kernel(
    fr_ref, fq_ref, recv_ref, control_ref, ch_ref, cl_ref, ez_ref, ey_ref, send_ref, f_ref, u_ref, y_ref
):
    step = control_ref[0, 0:1, 0:1]
    ez = jnp.concatenate([third_eigen(ez_ref, h) for h in range(2)], axis=0)
    rho, factor = decay(ABSORPTION / CONDUCT + ez + ey_ref[...])

    def state(side):
        return jnp.concatenate(
            [
                jnp.concatenate([recv_ref[i, 4 * side + b] for i in range(BK)], axis=0)
                for b in range(4)
            ],
            axis=1,
        )

    def rise(x, carry):
        f = fr_ref[x] - step * fq_ref[x]
        carry = f + rho * carry
        f_ref[x] = f
        u_ref[x] = carry
        return carry

    def fall(i, carry):
        x = BX - 1 - i
        carry = rho * carry
        u_ref[x] = factor * (u_ref[x] + carry)
        return f_ref[x] + carry

    lax.fori_loop(0, BX, rise, state(0), unroll=4)
    lax.fori_loop(0, BX, fall, state(1), unroll=4)
    solved = halves(u_ref[...].reshape(BX * BK, N))
    y_ref[...] = product(solved, (ch_ref[...], cl_ref[...]), ((1,), (0,))).reshape(BX, BK, N)

    def part(b, _):
        for s in range(4):
            for a in range(2):
                rows = swap_units(
                    [y_ref[8 * b + i, 8 * a : 8 * a + 8, 128 * s : 128 * s + 128] for i in range(8)]
                )
                for i in range(8):
                    send_ref[8 * s + i, 4 * a + b] = rows[i]
        return 0

    lax.fori_loop(0, 4, part, 0)
    sums = recv_ref[0, 8]
    for p in range(1, GRP):
        sums = sums + recv_ref[p, 8]
    row = lax.broadcasted_iota(jnp.int32, (8, 128), 0)
    first = (row == 0) & (lax.broadcasted_iota(jnp.int32, (8, 128), 1) == 0)
    sums = jnp.where(row == 0, sums, 0.0) + jnp.where(first, control_ref[2], 0.0)
    for j in range(PEN):
        send_ref[j, 8] = sums


def finish_kernel(
    recv_ref, r_ref, d_ref, q_ref, control_ref, ch_ref, cl_ref, nr_hbm, nd_hbm, g_ref, nr_ref, nd_ref, sems
):
    nr_ref[...] = r_ref[...] - control_ref[0, 0:1, 0:1] * q_ref[...]
    copies = start([pltpu.make_async_copy(nr_ref, nr_hbm, sems.at[0])])
    for b in range(4):
        for a in range(2):
            g_ref[:, a, :, 128 * b : 128 * b + 128] = recv_ref[:, 4 * a + b]
    sums = recv_ref[0, 8]
    for j in range(1, PEN):
        sums = sums + recv_ref[j, 8]
    conjugacy = jnp.full((8, 128), jnp.sum(sums), F32)
    ratio = (conjugacy / control_ref[1])[0:1, 0:1]
    modes = halves(g_ref[...].reshape(N, BX * BY))
    smoothed = product(modes, (ch_ref[...], cl_ref[...]), ((0,), (0,)))
    nd_ref[...] = smoothed.reshape(BX, BY, N) - ratio * d_ref[...]
    wait(copies + start([pltpu.make_async_copy(nd_ref, nd_hbm, sems.at[1])]))


def shape(*dims):
    return jax.ShapeDtypeStruct(dims, F32)


def in_hbm(x):
    return pltpu.with_memory_space_constraint(x, pltpu.HBM)


def call(kernel, ins, outs, scratch=()):
    return pl.pallas_call(
        kernel,
        in_specs=ins,
        out_specs=[VMEM if isinstance(out, jax.ShapeDtypeStruct) else HBM for out in outs],
        out_shape=outs,
        scratch_shapes=[pltpu.VMEM(s, F32) if isinstance(s, tuple) else s for s in scratch],
        compiler_params=PARAMS,
    )


def exchange(x, axis):
    return lax.all_to_all(x, axis, 0, 0)


def on_device(residual, direction, material):
    matrix = dct_matrix()
    high = matrix.astype(jnp.bfloat16)
    low = (matrix - high.astype(np.float64)).astype(jnp.bfloat16)
    high, low = jnp.asarray(high), jnp.asarray(low)
    eigen = eigen_values()
    ez = jnp.asarray(eigen)
    ey_row = jnp.asarray(eigen[None, :])
    ey_tile = jnp.asarray(np.concatenate([eigen.reshape(4, 128)] * 2, 0))
    block = shape(BX, BY, N)
    half = pltpu.VMEM((N, N), jnp.bfloat16)

    (send,) = call(
        residual_kernel,
        [HBM] * 3,
        [pltpu.HBM((PEN, 8, 8, 128), F32)],
        [(BX, BY, N), half, half, (PEN, 8, 8, 128), pltpu.SemaphoreType.DMA((4,))],
    )(in_hbm(residual), in_hbm(high), in_hbm(low))
    recv_r = exchange(send, "pen")

    xlo, xhi, ylo, yhi = call(
        faces_kernel, [VMEM] * 2, [shape(1, BY, N), shape(1, BY, N), shape(BX, N), shape(BX, N)]
    )(direction, material)

    def up(x, axis, count):
        return lax.ppermute(x, axis, [(i, i + 1) for i in range(count - 1)])

    def down(x, axis, count):
        return lax.ppermute(x, axis, [(i + 1, i) for i in range(count - 1)])

    xl, xh = up(xhi, "grp", GRP), down(xlo, "grp", GRP)
    yl, yh = up(yhi, "pen", PEN), down(ylo, "pen", PEN)

    inner, sums = call(
        inner_kernel, [VMEM] * 3, [block, shape(2, 8, 128)], [(BX + 2, BY, N)]
    )(residual, direction, material)
    operated, send = call(
        operated_kernel,
        [VMEM] * 10,
        [pltpu.HBM((BX, BY, N), F32), pltpu.HBM((PEN, 9, 8, 128), F32)],
        [(BX, BY, N), (PEN, 9, 8, 128), pltpu.SemaphoreType.DMA((2,))],
    )(inner, sums, direction, material, xl, xh, yl, yh, high, low)
    recv_q = exchange(send, "pen")

    field_r, states = call(
        residual_blocks_kernel,
        [VMEM, VMEM, VMEM, SMEM, VMEM],
        [pltpu.HBM((BX, BK, N), F32), shape(GRP, 8, 1, 128)],
        [(BX, BK, N), (BX, BK, N), pltpu.SemaphoreType.DMA],
    )(recv_r, high, low, ez, ey_row)
    field_q, send = call(
        operated_blocks_kernel,
        [HBM, HBM, VMEM, VMEM, VMEM, SMEM, VMEM],
        [block, shape(GRP, 17, 1, 128)],
        [(BX, BK, N), (PEN, 9, 8, 128), (BX, BK, N), pltpu.SemaphoreType.DMA((3, 4))],
    )(in_hbm(recv_q), in_hbm(field_r), states, high, low, ez, ey_row)

    recv = exchange(send, "grp")
    send, control = call(
        interface_kernel, [VMEM, SMEM, VMEM], [shape(GRP, 9, 1, 128), shape(3, 8, 128)]
    )(recv, ez, ey_tile)

    recv = exchange(send, "grp")
    (send,) = call(
        solve_kernel,
        [VMEM] * 6 + [SMEM, VMEM],
        [shape(PEN, 9, 8, 128)],
        [(BX, BK, N)] * 3,
    )(field_r, field_q, recv, control, high, low, ez, ey_row)

    recv = exchange(send, "pen")
    return tuple(
        call(
            finish_kernel,
            [VMEM] * 7,
            [pltpu.HBM((BX, BY, N), F32), pltpu.HBM((BX, BY, N), F32)],
            [(PEN, 2, 8, BX * BY), (BX, BY, N), (BX, BY, N), pltpu.SemaphoreType.DMA((2,))],
        )(recv, residual, direction, operated, control, high, low)
    )


def solution(mesh):
    placed = P("grp", "pen", None)
    return jax.shard_map(
        on_device,
        mesh=mesh,
        in_specs=(placed, placed, placed),
        out_specs=(placed, placed),
        check_vma=False,
    )
```

```python
import functools
import math

import jax
import jax.numpy as jnp
import numpy as np
from jax import lax
from jax.experimental import pallas as pl
from jax.experimental.pallas import tpu as pltpu
from jax.sharding import PartitionSpec as P

N = 512
GRP = 16
PEN = 32
BX = N // GRP
BY = N // PEN
BK = N // PEN
ABSORPTION = 0.02
CONDUCT = 5.0
SOLID = math.sqrt(30.0)
F32 = jnp.float32
VMEM = pl.BlockSpec(memory_space=pltpu.VMEM)
HBM = pl.BlockSpec(memory_space=pltpu.HBM)
SMEM = pl.BlockSpec(memory_space=pltpu.SMEM)
PARAMS = pltpu.CompilerParams(vmem_limit_bytes=48 * 1024 * 1024)


def dct_matrix():
    k = np.arange(N)[:, None]
    n = np.arange(N)[None, :]
    weight = np.where(k == 0, math.sqrt(1.0 / N), math.sqrt(2.0 / N))
    return weight * np.cos(math.pi * (k * (2 * n + 1) % (4 * N)) / (2.0 * N))


def eigen_values():
    return (4.0 * np.sin(math.pi * np.arange(N) / (2.0 * N)) ** 2).astype(np.float32)


def halves(x):
    high = x.astype(jnp.bfloat16)
    return high, (x - high.astype(F32)).astype(jnp.bfloat16)


def product(a, b, dims):
    def one(x, y):
        return lax.dot_general(x, y, (dims, ((), ())), preferred_element_type=F32)

    return one(a[0], b[0]) + (one(a[0], b[1]) + one(a[1], b[0]))


def whole(refs):
    return tuple(ref[...] for ref in refs)


def decay(shift):
    rho = 2.0 / (2.0 + shift + jnp.sqrt(shift * (shift + 4.0)))
    return rho, rho / (CONDUCT * (1.0 - rho * rho))


def turn(x, units):
    return pltpu.roll(x, 16 * units % 128, 1) if units % 8 else x


def swap_units(rows):
    unit = lax.broadcasted_iota(jnp.int32, rows[0].shape, 1) // 16
    rows = [turn(row, i) for i, row in enumerate(rows)]
    for d in (1, 2, 4):
        late = (unit & d) != 0
        rows = [jnp.where(late, rows[(i + d) % 8], rows[i]) for i in range(8)]
    return [turn(rows[-k % 8], -k) for k in range(8)]


def to_tile(x):
    x = x[:8] + x[8:]
    return x[:, 0:128] + x[:, 128:256] + x[:, 256:384] + x[:, 384:512]


def fold(x, step):
    return x + pltpu.roll(x, step, 0)


def stiffness_of(material):
    return jnp.where(material == 1, jnp.float32(SOLID), jnp.float32(1.0))


def faces_kernel(d_ref, m_ref, xlo_ref, xhi_ref, ylo_ref, yhi_ref):
    xlo_ref[0] = stiffness_of(m_ref[0]) * d_ref[0]
    xhi_ref[0] = stiffness_of(m_ref[BX - 1]) * d_ref[BX - 1]
    ylo_ref[...] = stiffness_of(m_ref[:, 0, :]) * d_ref[:, 0, :]
    yhi_ref[...] = stiffness_of(m_ref[:, BY - 1, :]) * d_ref[:, BY - 1, :]


def start(copies):
    for copy in copies:
        copy.start()
    return copies


def wait(copies):
    for copy in copies:
        copy.wait()


def third_modes(field_ref, c_refs, put):
    modes = product(whole(c_refs), halves(field_ref[...].reshape(BX * BY, N)), ((1,), (1,)))
    for b in range(4):
        part = modes[:, 128 * b : 128 * b + 128].reshape(PEN, 2, 8, 128)
        for a in range(2):
            put(4 * a + b, part[:, a])


def residual_kernel(r_hbm, ch_hbm, cl_hbm, send_hbm, r_ref, ch_ref, cl_ref, send_ref, sems):
    wait(
        start(
            [
                pltpu.make_async_copy(r_hbm, r_ref, sems.at[0]),
                pltpu.make_async_copy(ch_hbm, ch_ref, sems.at[1]),
                pltpu.make_async_copy(cl_hbm, cl_ref, sems.at[2]),
            ]
        )
    )

    def put(tile, x):
        send_ref[:, tile] = x

    third_modes(r_ref, (ch_ref, cl_ref), put)
    wait(start([pltpu.make_async_copy(send_ref, send_hbm, sems.at[3])]))


def inner_kernel(r_ref, d_ref, m_ref, q_ref, sums_ref, u_ref):
    u_ref[0] = jnp.zeros((BY, N), F32)
    u_ref[BX + 1] = jnp.zeros((BY, N), F32)

    def scale(x, _):
        u_ref[x + 1] = stiffness_of(m_ref[x]) * d_ref[x]
        return 0

    lax.fori_loop(0, BX, scale, 0, unroll=4)
    row = lax.broadcasted_iota(jnp.int32, (BY, N), 0)
    lane = lax.broadcasted_iota(jnp.int32, (BY, N), 1)

    def stencil(x, sums):
        u = u_ref[x + 1]
        d = d_ref[x]
        beside = u_ref[x] + u_ref[x + 2]
        beside += jnp.where(row == 0, 0.0, pltpu.roll(u, 1, 0))
        beside += jnp.where(row == BY - 1, 0.0, pltpu.roll(u, BY - 1, 0))
        beside += jnp.where(lane == 0, 0.0, pltpu.roll(u, 1, 1))
        beside += jnp.where(lane == N - 1, 0.0, pltpu.roll(u, N - 1, 1))
        q = ABSORPTION * d + stiffness_of(m_ref[x]) * (6.0 * u - beside)
        q_ref[x] = q
        return sums[0] + to_tile(d * q), sums[1] + to_tile(r_ref[x] * d)

    zero = jnp.zeros((8, 128), F32)
    sums = lax.fori_loop(0, BX, stencil, (zero, zero), unroll=4)
    sums_ref[0], sums_ref[1] = sums


def operated_kernel(
    q_ref, sums_ref, d_ref, m_ref, xl_ref, xh_ref, yl_ref, yh_ref, ch_ref, cl_ref, out_hbm, send_hbm, out_ref, send_ref, sems
):
    row = lax.broadcasted_iota(jnp.int32, (8, N), 0)

    def low_high(x, total):
        for first, edge, side_ref in ((0, 0, yl_ref), (8, 7, yh_ref)):
            rows = pl.ds(first, 8)
            add = stiffness_of(m_ref[x, rows]) * jnp.where(row == edge, side_ref[pl.ds(x, 1), :], 0.0)
            out_ref[x, rows] = q_ref[x, rows] - add
            total = total + d_ref[x, rows] * add
        return total

    total = lax.fori_loop(0, BX, low_high, jnp.zeros((8, N), F32), unroll=4)
    total = jnp.concatenate([total, jnp.zeros((8, N), F32)], axis=0)
    for x, side_ref in ((0, xl_ref), (BX - 1, xh_ref)):
        add = stiffness_of(m_ref[x]) * side_ref[0]
        out_ref[x] = out_ref[x] - add
        total = total + d_ref[x] * add
    curvature = sums_ref[0] - to_tile(total)
    first = lax.broadcasted_iota(jnp.int32, (8, 128), 0) < 2
    sums = jnp.where(first, fold(fold(curvature, 4), 2), fold(fold(sums_ref[1], 4), 2))
    for j in range(PEN):
        send_ref[j, 16] = sums[:4]
    copies = start([pltpu.make_async_copy(out_ref, out_hbm, sems.at[0])])

    def put(tile, x):
        send_ref[:, 2 * tile] = x[:, :4]
        send_ref[:, 2 * tile + 1] = x[:, 4:]

    third_modes(out_ref, (ch_ref, cl_ref), put)
    wait(copies + start([pltpu.make_async_copy(send_ref, send_hbm, sems.at[1])]))


def second_modes(get, c_refs, out_ref, y_ref, ready=lambda b: None):
    def part(b, _):
        ready(b)
        for s in range(4):
            for a in range(2):
                rows = swap_units([get(8 * s + i, 4 * a + b) for i in range(8)])
                for i in range(8):
                    y_ref[8 * b + i, 8 * a : 8 * a + 8, 128 * s : 128 * s + 128] = rows[i]
        return 0

    lax.fori_loop(0, 4, part, 0)
    field = halves(y_ref[...].reshape(BX * BK, N))
    out_ref[...] = product(field, whole(c_refs), ((1,), (1,))).reshape(BX, BK, N)


def third_eigen(ez_ref, h):
    k0 = lax.axis_index("pen") * BK + 8 * h
    return jnp.concatenate([jnp.full((1, N), ez_ref[k0 + i], F32) for i in range(8)], axis=0)


def put_states(v, w, h, send_ref, first):
    for side, x in enumerate((v, w)):
        for b in range(4):
            for i in range(8):
                send_ref[8 * h + i, first + 4 * side + b] = x[i : i + 1, 128 * b : 128 * b + 128]


def residual_blocks_kernel(
    recv_ref, ch_ref, cl_ref, ez_ref, ey_ref, fr_hbm, zr_hbm, states_ref, table_ref, y_ref, fr_ref, zr_ref, sems
):
    second_modes(lambda j, tile: recv_ref[j, tile], (ch_ref, cl_ref), fr_ref, y_ref)
    copies = start([pltpu.make_async_copy(fr_ref, fr_hbm, sems.at[0])])
    for h in range(2):
        rows = pl.ds(8 * h, 8)
        rho, factor = decay(ABSORPTION / CONDUCT + third_eigen(ez_ref, h) + ey_ref[...])
        table_ref[0, rows] = rho
        table_ref[1, rows] = factor

        def rise(x, v):
            v = fr_ref[x, rows] + rho * v
            zr_ref[x, rows] = v
            return v

        def fall(i, w):
            x = BX - 1 - i
            before = rho * w
            zr_ref[x, rows] = factor * (zr_ref[x, rows] + before)
            return fr_ref[x, rows] + before

        zero = jnp.zeros((8, N), F32)
        v = lax.fori_loop(0, BX, rise, zero, unroll=4)
        w = lax.fori_loop(0, BX, fall, zero, unroll=4)
        put_states(v, w, h, states_ref, 0)
    wait(copies + start([pltpu.make_async_copy(zr_ref, zr_hbm, sems.at[1])]))


def operated_blocks_kernel(
    recv_hbm, zr_hbm, states_ref, table_ref, ch_ref, cl_ref, fq_ref, send_ref, y_ref, recv_ref, zr_ref, sems
):
    def into(b):
        tiles = [pl.ds(2 * b, 2), pl.ds(2 * b + 8, 2)]
        return [
            pltpu.make_async_copy(recv_hbm.at[:, t], recv_ref.at[:, t], sems.at[i, b])
            for i, t in enumerate(tiles)
        ]

    for b in range(4):
        start(into(b))
    late = start(
        [
            pltpu.make_async_copy(recv_hbm.at[:, 16], recv_ref.at[:, 16], sems.at[2, 0]),
            pltpu.make_async_copy(zr_hbm, zr_ref, sems.at[2, 1]),
        ]
    )

    def get(j, tile):
        return jnp.concatenate([recv_ref[j, 2 * tile], recv_ref[j, 2 * tile + 1]], axis=0)

    second_modes(get, (ch_ref, cl_ref), fq_ref, y_ref, lambda b: wait(into(b)))
    wait(late)
    dots = [jnp.zeros((8, 128), F32), jnp.zeros((8, 128), F32)]
    for h in range(2):
        rows = pl.ds(8 * h, 8)
        rho = table_ref[0, rows]

        def sweep(x, carry):
            power, vq, wq, rq, qq = carry
            q = fq_ref[x, rows]
            before = rho * vq
            vq = q + before
            return power * rho, vq, wq + power * q, rq + zr_ref[x, rows] * q, qq + (vq + before) * q

        zero = jnp.zeros((8, N), F32)
        carry = (jnp.ones((8, N), F32),) + (zero,) * 4
        _, vq, wq, rq, qq = lax.fori_loop(0, BX, sweep, carry, unroll=4)
        put_states(vq, wq, h, send_ref, 8)
        for i, x in enumerate((rq, table_ref[1, rows] * qq)):
            dots[i] += x[:, 0:128] + x[:, 128:256] + x[:, 256:384] + x[:, 384:512]

    sums = recv_ref[0, 16]
    for j in range(1, PEN):
        sums = sums + recv_ref[j, 16]
    group = lax.broadcasted_iota(jnp.int32, (1, 128), 1) // 32
    packed = jnp.zeros((1, 128), F32)
    for i, x in enumerate((sums[0:2], sums[2:4], dots[0], dots[1])):
        x = jnp.sum(x, axis=0, keepdims=True)
        x = x + pltpu.roll(x, 64, 1)
        packed = jnp.where(group == i, x + pltpu.roll(x, 32, 1), packed)
    for j in range(GRP):
        send_ref[j, 0:8] = states_ref[j]
        send_ref[j, 16] = packed


def interface_kernel(recv_ref, ez_ref, ey_ref, send_ref, control_ref):
    row = lax.broadcasted_iota(jnp.int32, (8, 128), 0)
    group = lax.broadcasted_iota(jnp.int32, (1, 128), 1) // 32
    sums = recv_ref[0, 16]
    for p in range(1, GRP):
        sums = sums + recv_ref[p, 16]

    def total(i):
        return jnp.full((8, 128), jnp.sum(jnp.where(group == i, sums, 0.0)), F32)

    curvature, projection, rq, qq = total(0), total(1), total(2), total(3)
    step = projection / curvature
    ez = ez_ref[lax.axis_index("pen") * BK + lax.axis_index("grp")]
    rho, factor = decay(ABSORPTION / CONDUCT + ez + ey_ref[...])
    across = rho
    for _ in range(5):
        across = across * across
    others = [recv_ref[p, 8:16].reshape(8, 128) for p in range(GRP)]
    tiles = [recv_ref[p, 0:8].reshape(8, 128) - step * others[p] for p in range(GRP)]
    zero = jnp.zeros((8, 128), F32)
    rising = [zero]
    for p in range(GRP):
        rising.append(tiles[p] + across * rising[-1])
    falling = [zero]
    for p in reversed(range(GRP)):
        falling.append(tiles[p] + across * falling[-1])
    lower = row < 4
    ends = jnp.where(lower, rising[GRP], falling[GRP])
    powers = [jnp.ones((8, 128), F32)]
    for p in range(GRP):
        powers.append(powers[-1] * across)
    whole = powers[GRP]
    images = (pltpu.roll(ends, 4, 0) + whole * ends) / (1.0 - whole * whole)
    dots = zero
    for p in range(GRP):
        state = jnp.where(
            lower,
            rising[p] + powers[p] * images,
            falling[GRP - 1 - p] + powers[GRP - 1 - p] * images,
        )
        send_ref[p, 0:8] = state.reshape(8, 1, 128)
        dots = dots + state * pltpu.roll(others[p], 4, 0)
    dots = jnp.sum(rho * factor * dots, axis=0, keepdims=True)
    for p in range(GRP):
        send_ref[p, 8] = dots
    control_ref[0] = step
    control_ref[1] = curvature
    control_ref[2] = rq - step * qq


def solve_kernel(
    fr_ref, fq_ref, recv_ref, control_ref, table_ref, ch_ref, cl_ref, send_ref, f_ref, u_ref, y_ref
):
    step = control_ref[0, 0:1, 0:1]
    rho, factor = table_ref[0], table_ref[1]

    def state(side):
        return jnp.concatenate(
            [
                jnp.concatenate([recv_ref[i, 4 * side + b] for i in range(BK)], axis=0)
                for b in range(4)
            ],
            axis=1,
        )

    def rise(x, carry):
        f = fr_ref[x] - step * fq_ref[x]
        carry = f + rho * carry
        f_ref[x] = f
        u_ref[x] = carry
        return carry

    def fall(i, carry):
        x = BX - 1 - i
        carry = rho * carry
        u_ref[x] = factor * (u_ref[x] + carry)
        return f_ref[x] + carry

    lax.fori_loop(0, BX, rise, state(0), unroll=4)
    lax.fori_loop(0, BX, fall, state(1), unroll=4)
    solved = halves(u_ref[...].reshape(BX * BK, N))
    y_ref[...] = product(solved, (ch_ref[...], cl_ref[...]), ((1,), (0,))).reshape(BX, BK, N)

    def part(b, _):
        for s in range(4):
            for a in range(2):
                rows = swap_units(
                    [y_ref[8 * b + i, 8 * a : 8 * a + 8, 128 * s : 128 * s + 128] for i in range(8)]
                )
                for i in range(8):
                    tile = 8 * a + 2 * b
                    send_ref[8 * s + i, tile] = rows[i][:4]
                    send_ref[8 * s + i, tile + 1] = rows[i][4:]
        return 0

    lax.fori_loop(0, 4, part, 0)
    sums = recv_ref[0, 8]
    for p in range(1, GRP):
        sums = sums + recv_ref[p, 8]
    row = lax.broadcasted_iota(jnp.int32, (8, 128), 0)
    first = (row == 0) & (lax.broadcasted_iota(jnp.int32, (8, 128), 1) == 0)
    sums = jnp.where(row == 0, sums, 0.0) + jnp.where(first, control_ref[2], 0.0)
    for j in range(PEN):
        send_ref[j, 16] = sums[:4]


def finish_kernel(
    recv_ref, r_ref, d_ref, q_ref, control_ref, ch_ref, cl_ref, nr_hbm, nd_hbm, g_ref, nr_ref, nd_ref, sems
):
    nr_ref[...] = r_ref[...] - control_ref[0, 0:1, 0:1] * q_ref[...]
    copies = start([pltpu.make_async_copy(nr_ref, nr_hbm, sems.at[0])])
    for b in range(4):
        for a in range(2):
            for c in range(2):
                rows = slice(4 * c, 4 * c + 4)
                g_ref[:, a, rows, 128 * b : 128 * b + 128] = recv_ref[:, 8 * a + 2 * b + c]
    sums = recv_ref[0, 16]
    for j in range(1, PEN):
        sums = sums + recv_ref[j, 16]
    conjugacy = jnp.full((8, 128), jnp.sum(sums), F32)
    ratio = (conjugacy / control_ref[1])[0:1, 0:1]
    modes = halves(g_ref[...].reshape(N, BX * BY))
    smoothed = product(modes, (ch_ref[...], cl_ref[...]), ((0,), (0,)))
    nd_ref[...] = smoothed.reshape(BX, BY, N) - ratio * d_ref[...]
    wait(copies + start([pltpu.make_async_copy(nd_ref, nd_hbm, sems.at[1])]))


def shape(*dims):
    return jax.ShapeDtypeStruct(dims, F32)


def in_hbm(x):
    return pltpu.with_memory_space_constraint(x, pltpu.HBM)


def call(kernel, ins, outs, scratch=()):
    return pl.pallas_call(
        kernel,
        in_specs=ins,
        out_specs=[VMEM if isinstance(out, jax.ShapeDtypeStruct) else HBM for out in outs],
        out_shape=outs,
        scratch_shapes=[pltpu.VMEM(s, F32) if isinstance(s, tuple) else s for s in scratch],
        compiler_params=PARAMS,
    )


def exchange(x, axis):
    return lax.all_to_all(x, axis, 0, 0)


def on_device(residual, direction, material):
    matrix = dct_matrix()
    high = matrix.astype(jnp.bfloat16)
    low = (matrix - high.astype(np.float64)).astype(jnp.bfloat16)
    high, low = jnp.asarray(high), jnp.asarray(low)
    eigen = eigen_values()
    ez = jnp.asarray(eigen)
    ey_row = jnp.asarray(eigen[None, :])
    ey_tile = jnp.asarray(np.concatenate([eigen.reshape(4, 128)] * 2, 0))
    block = shape(BX, BY, N)
    half = pltpu.VMEM((N, N), jnp.bfloat16)

    (send,) = call(
        residual_kernel,
        [HBM] * 3,
        [pltpu.HBM((PEN, 8, 8, 128), F32)],
        [(BX, BY, N), half, half, (PEN, 8, 8, 128), pltpu.SemaphoreType.DMA((4,))],
    )(in_hbm(residual), in_hbm(high), in_hbm(low))
    recv_r = exchange(send, "pen")

    xlo, xhi, ylo, yhi = call(
        faces_kernel, [VMEM] * 2, [shape(1, BY, N), shape(1, BY, N), shape(BX, N), shape(BX, N)]
    )(direction, material)

    def up(x, axis, count):
        return lax.ppermute(x, axis, [(i, i + 1) for i in range(count - 1)])

    def down(x, axis, count):
        return lax.ppermute(x, axis, [(i + 1, i) for i in range(count - 1)])

    xl, xh = up(xhi, "grp", GRP), down(xlo, "grp", GRP)
    yl, yh = up(yhi, "pen", PEN), down(ylo, "pen", PEN)

    inner, sums = call(
        inner_kernel, [VMEM] * 3, [block, shape(2, 8, 128)], [(BX + 2, BY, N)]
    )(residual, direction, material)
    operated, send = call(
        operated_kernel,
        [VMEM] * 10,
        [pltpu.HBM((BX, BY, N), F32), pltpu.HBM((PEN, 17, 4, 128), F32)],
        [(BX, BY, N), (PEN, 17, 4, 128), pltpu.SemaphoreType.DMA((2,))],
    )(inner, sums, direction, material, xl, xh, yl, yh, high, low)
    recv_q = exchange(send, "pen")

    field_r, inside_r, states, table = call(
        residual_blocks_kernel,
        [VMEM, VMEM, VMEM, SMEM, VMEM],
        [
            pltpu.HBM((BX, BK, N), F32),
            pltpu.HBM((BX, BK, N), F32),
            shape(GRP, 8, 1, 128),
            shape(2, BK, N),
        ],
        [(BX, BK, N)] * 3 + [pltpu.SemaphoreType.DMA((2,))],
    )(recv_r, high, low, ez, ey_row)
    field_q, send = call(
        operated_blocks_kernel,
        [HBM, HBM] + [VMEM] * 4,
        [block, shape(GRP, 17, 1, 128)],
        [(BX, BK, N), (PEN, 17, 4, 128), (BX, BK, N), pltpu.SemaphoreType.DMA((3, 4))],
    )(in_hbm(recv_q), in_hbm(inside_r), states, table, high, low)

    recv = exchange(send, "grp")
    send, control = call(
        interface_kernel, [VMEM, SMEM, VMEM], [shape(GRP, 9, 1, 128), shape(3, 8, 128)]
    )(recv, ez, ey_tile)

    recv = exchange(send, "grp")
    (send,) = call(
        solve_kernel,
        [VMEM] * 7,
        [shape(PEN, 17, 4, 128)],
        [(BX, BK, N)] * 3,
    )(field_r, field_q, recv, control, table, high, low)

    recv = exchange(send, "pen")
    return tuple(
        call(
            finish_kernel,
            [VMEM] * 7,
            [pltpu.HBM((BX, BY, N), F32), pltpu.HBM((BX, BY, N), F32)],
            [(PEN, 2, 8, BX * BY), (BX, BY, N), (BX, BY, N), pltpu.SemaphoreType.DMA((2,))],
        )(recv, residual, direction, operated, control, high, low)
    )


def solution(mesh):
    placed = P("grp", "pen", None)
    return jax.shard_map(
        on_device,
        mesh=mesh,
        in_specs=(placed, placed, placed),
        out_specs=(placed, placed),
        check_vma=False,
    )
```

```python
import functools
import math

import jax
import jax.numpy as jnp
import numpy as np
from jax import lax
from jax.experimental import pallas as pl
from jax.experimental.pallas import tpu as pltpu
from jax.sharding import PartitionSpec as P

N = 512
GRP = 16
PEN = 32
BX = N // GRP
BY = N // PEN
BK = N // PEN
ABSORPTION = 0.02
CONDUCT = 5.0
SOLID = math.sqrt(30.0)
F32 = jnp.float32
VMEM = pl.BlockSpec(memory_space=pltpu.VMEM)
HBM = pl.BlockSpec(memory_space=pltpu.HBM)
SMEM = pl.BlockSpec(memory_space=pltpu.SMEM)
PARAMS = pltpu.CompilerParams(vmem_limit_bytes=48 * 1024 * 1024)


def dct_matrix():
    k = np.arange(N)[:, None]
    n = np.arange(N)[None, :]
    weight = np.where(k == 0, math.sqrt(1.0 / N), math.sqrt(2.0 / N))
    return weight * np.cos(math.pi * (k * (2 * n + 1) % (4 * N)) / (2.0 * N))


def eigen_values():
    return (4.0 * np.sin(math.pi * np.arange(N) / (2.0 * N)) ** 2).astype(np.float32)


def halves(x):
    high = x.astype(jnp.bfloat16)
    return high, (x - high.astype(F32)).astype(jnp.bfloat16)


def product(a, b, dims):
    def one(x, y):
        return lax.dot_general(x, y, (dims, ((), ())), preferred_element_type=F32)

    return one(a[0], b[0]) + (one(a[0], b[1]) + one(a[1], b[0]))


def whole(refs):
    return tuple(ref[...] for ref in refs)


def decay(shift):
    rho = 2.0 / (2.0 + shift + jnp.sqrt(shift * (shift + 4.0)))
    return rho, rho / (CONDUCT * (1.0 - rho * rho))


def turn(x, units):
    return pltpu.roll(x, 16 * units % 128, 1) if units % 8 else x


def swap_units(rows):
    unit = lax.broadcasted_iota(jnp.int32, rows[0].shape, 1) // 16
    rows = [turn(row, i) for i, row in enumerate(rows)]
    for d in (1, 2, 4):
        late = (unit & d) != 0
        rows = [jnp.where(late, rows[(i + d) % 8], rows[i]) for i in range(8)]
    return [turn(rows[-k % 8], -k) for k in range(8)]


def to_tile(x):
    x = x[:8] + x[8:]
    return x[:, 0:128] + x[:, 128:256] + x[:, 256:384] + x[:, 384:512]


def fold(x, step):
    return x + pltpu.roll(x, step, 0)


def stiffness_of(material):
    return jnp.where(material == 1, jnp.float32(SOLID), jnp.float32(1.0))


def even_pen():
    return lax.rem(lax.axis_index("pen"), 2) == 0


def faces_kernel(d_ref, m_ref, xlo_ref, xhi_ref, first_ref, second_ref):
    xlo_ref[0] = stiffness_of(m_ref[0]) * d_ref[0]
    xhi_ref[0] = stiffness_of(m_ref[BX - 1]) * d_ref[BX - 1]
    low = stiffness_of(m_ref[:, 0, :]) * d_ref[:, 0, :]
    high = stiffness_of(m_ref[:, BY - 1, :]) * d_ref[:, BY - 1, :]
    first_ref[...] = jnp.where(even_pen(), high, low)
    second_ref[...] = jnp.where(even_pen(), low, high)


def start(copies):
    for copy in copies:
        copy.start()
    return copies


def wait(copies):
    for copy in copies:
        copy.wait()


def third_modes(field_ref, c_refs, put):
    modes = product(whole(c_refs), halves(field_ref[...].reshape(BX * BY, N)), ((1,), (1,)))
    for b in range(4):
        part = modes[:, 128 * b : 128 * b + 128].reshape(PEN, 2, 8, 128)
        for a in range(2):
            put(4 * a + b, part[:, a])


def residual_kernel(r_hbm, ch_hbm, cl_hbm, send_hbm, r_ref, ch_ref, cl_ref, send_ref, sems):
    wait(
        start(
            [
                pltpu.make_async_copy(r_hbm, r_ref, sems.at[0]),
                pltpu.make_async_copy(ch_hbm, ch_ref, sems.at[1]),
                pltpu.make_async_copy(cl_hbm, cl_ref, sems.at[2]),
            ]
        )
    )

    def put(tile, x):
        send_ref[:, tile] = x

    third_modes(r_ref, (ch_ref, cl_ref), put)
    wait(start([pltpu.make_async_copy(send_ref, send_hbm, sems.at[3])]))


def inner_kernel(r_ref, d_ref, m_ref, q_ref, sums_ref, u_ref):
    u_ref[0] = jnp.zeros((BY, N), F32)
    u_ref[BX + 1] = jnp.zeros((BY, N), F32)

    def scale(x, _):
        u_ref[x + 1] = stiffness_of(m_ref[x]) * d_ref[x]
        return 0

    lax.fori_loop(0, BX, scale, 0, unroll=4)
    row = lax.broadcasted_iota(jnp.int32, (BY, N), 0)
    lane = lax.broadcasted_iota(jnp.int32, (BY, N), 1)

    def stencil(x, sums):
        u = u_ref[x + 1]
        d = d_ref[x]
        beside = u_ref[x] + u_ref[x + 2]
        beside += jnp.where(row == 0, 0.0, pltpu.roll(u, 1, 0))
        beside += jnp.where(row == BY - 1, 0.0, pltpu.roll(u, BY - 1, 0))
        beside += jnp.where(lane == 0, 0.0, pltpu.roll(u, 1, 1))
        beside += jnp.where(lane == N - 1, 0.0, pltpu.roll(u, N - 1, 1))
        q = ABSORPTION * d + stiffness_of(m_ref[x]) * (6.0 * u - beside)
        q_ref[x] = q
        return sums[0] + to_tile(d * q), sums[1] + to_tile(r_ref[x] * d)

    zero = jnp.zeros((8, 128), F32)
    sums = lax.fori_loop(0, BX, stencil, (zero, zero), unroll=4)
    sums_ref[0], sums_ref[1] = sums


def operated_kernel(
    q_ref, sums_ref, d_ref, m_ref, xl_ref, xh_ref, ya_ref, yb_ref, ch_ref, cl_ref, out_hbm, send_hbm, out_ref, send_ref, sems
):
    row = lax.broadcasted_iota(jnp.int32, (8, N), 0)

    def low_high(x, total):
        ya, yb = ya_ref[pl.ds(x, 1), :], yb_ref[pl.ds(x, 1), :]
        low, high = jnp.where(even_pen(), yb, ya), jnp.where(even_pen(), ya, yb)
        for first, edge, side in ((0, 0, low), (8, 7, high)):
            rows = pl.ds(first, 8)
            add = stiffness_of(m_ref[x, rows]) * jnp.where(row == edge, side, 0.0)
            out_ref[x, rows] = q_ref[x, rows] - add
            total = total + d_ref[x, rows] * add
        return total

    total = lax.fori_loop(0, BX, low_high, jnp.zeros((8, N), F32), unroll=4)
    total = jnp.concatenate([total, jnp.zeros((8, N), F32)], axis=0)
    for x, side_ref in ((0, xl_ref), (BX - 1, xh_ref)):
        add = stiffness_of(m_ref[x]) * side_ref[0]
        out_ref[x] = out_ref[x] - add
        total = total + d_ref[x] * add
    curvature = sums_ref[0] - to_tile(total)
    first = lax.broadcasted_iota(jnp.int32, (8, 128), 0) < 2
    sums = jnp.where(first, fold(fold(curvature, 4), 2), fold(fold(sums_ref[1], 4), 2))
    for j in range(PEN):
        send_ref[j, 16] = sums[:4]
    copies = start([pltpu.make_async_copy(out_ref, out_hbm, sems.at[0])])

    def put(tile, x):
        send_ref[:, 2 * tile] = x[:, :4]
        send_ref[:, 2 * tile + 1] = x[:, 4:]

    third_modes(out_ref, (ch_ref, cl_ref), put)
    wait(copies + start([pltpu.make_async_copy(send_ref, send_hbm, sems.at[1])]))


def second_modes(get, c_refs, out_ref, y_ref, ready=lambda b: None):
    def part(b, _):
        ready(b)
        for s in range(4):
            for a in range(2):
                rows = swap_units([get(8 * s + i, 4 * a + b) for i in range(8)])
                for i in range(8):
                    y_ref[8 * b + i, 8 * a : 8 * a + 8, 128 * s : 128 * s + 128] = rows[i]
        return 0

    lax.fori_loop(0, 4, part, 0)
    field = halves(y_ref[...].reshape(BX * BK, N))
    out_ref[...] = product(field, whole(c_refs), ((1,), (1,))).reshape(BX, BK, N)


def third_eigen(ez_ref, h):
    k0 = lax.axis_index("pen") * BK + 8 * h
    return jnp.concatenate([jnp.full((1, N), ez_ref[k0 + i], F32) for i in range(8)], axis=0)


def put_states(v, w, h, send_ref, first):
    for side, x in enumerate((v, w)):
        for b in range(4):
            for i in range(8):
                send_ref[8 * h + i, first + 4 * side + b] = x[i : i + 1, 128 * b : 128 * b + 128]


def residual_blocks_kernel(
    recv_ref, ch_ref, cl_ref, ez_ref, ey_ref, fr_hbm, zr_hbm, states_ref, table_ref, y_ref, fr_ref, zr_ref, sems
):
    second_modes(lambda j, tile: recv_ref[j, tile], (ch_ref, cl_ref), fr_ref, y_ref)
    copies = start([pltpu.make_async_copy(fr_ref, fr_hbm, sems.at[0])])
    for h in range(2):
        rows = pl.ds(8 * h, 8)
        rho, factor = decay(ABSORPTION / CONDUCT + third_eigen(ez_ref, h) + ey_ref[...])
        table_ref[0, rows] = rho
        table_ref[1, rows] = factor

        def rise(x, v):
            v = fr_ref[x, rows] + rho * v
            zr_ref[x, rows] = v
            return v

        def fall(i, w):
            x = BX - 1 - i
            before = rho * w
            zr_ref[x, rows] = factor * (zr_ref[x, rows] + before)
            return fr_ref[x, rows] + before

        zero = jnp.zeros((8, N), F32)
        v = lax.fori_loop(0, BX, rise, zero, unroll=4)
        w = lax.fori_loop(0, BX, fall, zero, unroll=4)
        put_states(v, w, h, states_ref, 0)
    wait(copies + start([pltpu.make_async_copy(zr_ref, zr_hbm, sems.at[1])]))


def operated_blocks_kernel(
    recv_hbm, zr_hbm, states_ref, table_ref, ch_ref, cl_ref, fq_ref, send_ref, y_ref, recv_ref, zr_ref, sems
):
    def into(b):
        tiles = [pl.ds(2 * b, 2), pl.ds(2 * b + 8, 2)]
        return [
            pltpu.make_async_copy(recv_hbm.at[:, t], recv_ref.at[:, t], sems.at[i, b])
            for i, t in enumerate(tiles)
        ]

    for b in range(4):
        start(into(b))
    late = start(
        [
            pltpu.make_async_copy(recv_hbm.at[:, 16], recv_ref.at[:, 16], sems.at[2, 0]),
            pltpu.make_async_copy(zr_hbm, zr_ref, sems.at[2, 1]),
        ]
    )

    def get(j, tile):
        return jnp.concatenate([recv_ref[j, 2 * tile], recv_ref[j, 2 * tile + 1]], axis=0)

    second_modes(get, (ch_ref, cl_ref), fq_ref, y_ref, lambda b: wait(into(b)))
    wait(late)
    dots = [jnp.zeros((8, 128), F32), jnp.zeros((8, 128), F32)]
    for h in range(2):
        rows = pl.ds(8 * h, 8)
        rho = table_ref[0, rows]

        def sweep(x, carry):
            power, vq, wq, rq, qq = carry
            q = fq_ref[x, rows]
            before = rho * vq
            vq = q + before
            return power * rho, vq, wq + power * q, rq + zr_ref[x, rows] * q, qq + (vq + before) * q

        zero = jnp.zeros((8, N), F32)
        carry = (jnp.ones((8, N), F32),) + (zero,) * 4
        _, vq, wq, rq, qq = lax.fori_loop(0, BX, sweep, carry, unroll=4)
        put_states(vq, wq, h, send_ref, 8)
        for i, x in enumerate((rq, table_ref[1, rows] * qq)):
            dots[i] += x[:, 0:128] + x[:, 128:256] + x[:, 256:384] + x[:, 384:512]

    sums = recv_ref[0, 16]
    for j in range(1, PEN):
        sums = sums + recv_ref[j, 16]
    group = lax.broadcasted_iota(jnp.int32, (1, 128), 1) // 32
    packed = jnp.zeros((1, 128), F32)
    for i, x in enumerate((sums[0:2], sums[2:4], dots[0], dots[1])):
        x = jnp.sum(x, axis=0, keepdims=True)
        x = x + pltpu.roll(x, 64, 1)
        packed = jnp.where(group == i, x + pltpu.roll(x, 32, 1), packed)
    for j in range(GRP):
        send_ref[j, 0:8] = states_ref[j]
        send_ref[j, 16] = packed


def interface_kernel(recv_ref, ez_ref, ey_ref, send_ref, control_ref):
    row = lax.broadcasted_iota(jnp.int32, (8, 128), 0)
    group = lax.broadcasted_iota(jnp.int32, (1, 128), 1) // 32
    sums = recv_ref[0, 16]
    for p in range(1, GRP):
        sums = sums + recv_ref[p, 16]

    def total(i):
        return jnp.full((8, 128), jnp.sum(jnp.where(group == i, sums, 0.0)), F32)

    curvature, projection, rq, qq = total(0), total(1), total(2), total(3)
    step = projection / curvature
    ez = ez_ref[lax.axis_index("pen") * BK + lax.axis_index("grp")]
    rho, factor = decay(ABSORPTION / CONDUCT + ez + ey_ref[...])
    across = rho
    for _ in range(5):
        across = across * across
    others = [recv_ref[p, 8:16].reshape(8, 128) for p in range(GRP)]
    tiles = [recv_ref[p, 0:8].reshape(8, 128) - step * others[p] for p in range(GRP)]
    zero = jnp.zeros((8, 128), F32)
    rising = [zero]
    for p in range(GRP):
        rising.append(tiles[p] + across * rising[-1])
    falling = [zero]
    for p in reversed(range(GRP)):
        falling.append(tiles[p] + across * falling[-1])
    lower = row < 4
    ends = jnp.where(lower, rising[GRP], falling[GRP])
    powers = [jnp.ones((8, 128), F32)]
    for p in range(GRP):
        powers.append(powers[-1] * across)
    whole = powers[GRP]
    images = (pltpu.roll(ends, 4, 0) + whole * ends) / (1.0 - whole * whole)
    dots = zero
    for p in range(GRP):
        state = jnp.where(
            lower,
            rising[p] + powers[p] * images,
            falling[GRP - 1 - p] + powers[GRP - 1 - p] * images,
        )
        send_ref[p, 0:8] = state.reshape(8, 1, 128)
        dots = dots + state * pltpu.roll(others[p], 4, 0)
    dots = jnp.sum(rho * factor * dots, axis=0, keepdims=True)
    for p in range(GRP):
        send_ref[p, 8] = dots
    control_ref[0] = step
    control_ref[1] = curvature
    control_ref[2] = rq - step * qq


def solve_kernel(
    fr_ref, fq_ref, recv_ref, control_ref, table_ref, ch_ref, cl_ref, send_ref, f_ref, u_ref, y_ref
):
    step = control_ref[0, 0:1, 0:1]
    rho, factor = table_ref[0], table_ref[1]

    def state(side):
        return jnp.concatenate(
            [
                jnp.concatenate([recv_ref[i, 4 * side + b] for i in range(BK)], axis=0)
                for b in range(4)
            ],
            axis=1,
        )

    def rise(x, carry):
        f = fr_ref[x] - step * fq_ref[x]
        carry = f + rho * carry
        f_ref[x] = f
        u_ref[x] = carry
        return carry

    def fall(i, carry):
        x = BX - 1 - i
        carry = rho * carry
        u_ref[x] = factor * (u_ref[x] + carry)
        return f_ref[x] + carry

    lax.fori_loop(0, BX, rise, state(0), unroll=4)
    lax.fori_loop(0, BX, fall, state(1), unroll=4)
    solved = halves(u_ref[...].reshape(BX * BK, N))
    y_ref[...] = product(solved, (ch_ref[...], cl_ref[...]), ((1,), (0,))).reshape(BX, BK, N)

    def part(b, _):
        for s in range(4):
            for a in range(2):
                rows = swap_units(
                    [y_ref[8 * b + i, 8 * a : 8 * a + 8, 128 * s : 128 * s + 128] for i in range(8)]
                )
                for i in range(8):
                    tile = 8 * a + 2 * b
                    send_ref[8 * s + i, tile] = rows[i][:4]
                    send_ref[8 * s + i, tile + 1] = rows[i][4:]
        return 0

    lax.fori_loop(0, 4, part, 0)
    sums = recv_ref[0, 8]
    for p in range(1, GRP):
        sums = sums + recv_ref[p, 8]
    row = lax.broadcasted_iota(jnp.int32, (8, 128), 0)
    first = (row == 0) & (lax.broadcasted_iota(jnp.int32, (8, 128), 1) == 0)
    sums = jnp.where(row == 0, sums, 0.0) + jnp.where(first, control_ref[2], 0.0)
    for j in range(PEN):
        send_ref[j, 16] = sums[:4]


def finish_kernel(
    recv_ref, r_ref, d_ref, q_ref, control_ref, ch_ref, cl_ref, nr_hbm, nd_hbm, g_ref, nr_ref, nd_ref, sems
):
    nr_ref[...] = r_ref[...] - control_ref[0, 0:1, 0:1] * q_ref[...]
    copies = start([pltpu.make_async_copy(nr_ref, nr_hbm, sems.at[0])])
    for b in range(4):
        for a in range(2):
            for c in range(2):
                rows = slice(4 * c, 4 * c + 4)
                g_ref[:, a, rows, 128 * b : 128 * b + 128] = recv_ref[:, 8 * a + 2 * b + c]
    sums = recv_ref[0, 16]
    for j in range(1, PEN):
        sums = sums + recv_ref[j, 16]
    conjugacy = jnp.full((8, 128), jnp.sum(sums), F32)
    ratio = (conjugacy / control_ref[1])[0:1, 0:1]
    modes = halves(g_ref[...].reshape(N, BX * BY))
    smoothed = product(modes, (ch_ref[...], cl_ref[...]), ((0,), (0,)))
    nd_ref[...] = smoothed.reshape(BX, BY, N) - ratio * d_ref[...]
    wait(copies + start([pltpu.make_async_copy(nd_ref, nd_hbm, sems.at[1])]))


def shape(*dims):
    return jax.ShapeDtypeStruct(dims, F32)


def in_hbm(x):
    return pltpu.with_memory_space_constraint(x, pltpu.HBM)


def call(kernel, ins, outs, scratch=()):
    return pl.pallas_call(
        kernel,
        in_specs=ins,
        out_specs=[VMEM if isinstance(out, jax.ShapeDtypeStruct) else HBM for out in outs],
        out_shape=outs,
        scratch_shapes=[pltpu.VMEM(s, F32) if isinstance(s, tuple) else s for s in scratch],
        compiler_params=PARAMS,
    )


def exchange(x, axis):
    return lax.all_to_all(x, axis, 0, 0)


def on_device(residual, direction, material):
    matrix = dct_matrix()
    high = matrix.astype(jnp.bfloat16)
    low = (matrix - high.astype(np.float64)).astype(jnp.bfloat16)
    high, low = jnp.asarray(high), jnp.asarray(low)
    eigen = eigen_values()
    ez = jnp.asarray(eigen)
    ey_row = jnp.asarray(eigen[None, :])
    ey_tile = jnp.asarray(np.concatenate([eigen.reshape(4, 128)] * 2, 0))
    block = shape(BX, BY, N)
    half = pltpu.VMEM((N, N), jnp.bfloat16)

    (send,) = call(
        residual_kernel,
        [HBM] * 3,
        [pltpu.HBM((PEN, 8, 8, 128), F32)],
        [(BX, BY, N), half, half, (PEN, 8, 8, 128), pltpu.SemaphoreType.DMA((4,))],
    )(in_hbm(residual), in_hbm(high), in_hbm(low))
    recv_r = exchange(send, "pen")

    xlo, xhi, first, second = call(
        faces_kernel, [VMEM] * 2, [shape(1, BY, N), shape(1, BY, N), shape(BX, N), shape(BX, N)]
    )(direction, material)

    def up(x, axis, count):
        return lax.ppermute(x, axis, [(i, i + 1) for i in range(count - 1)])

    def down(x, axis, count):
        return lax.ppermute(x, axis, [(i + 1, i) for i in range(count - 1)])

    xl, xh = up(xhi, "grp", GRP), down(xlo, "grp", GRP)
    ya = lax.ppermute(first, "pen", [(i, i ^ 1) for i in range(PEN)])
    yb = lax.ppermute(second, "pen", [(i, i + 1 if i % 2 else i - 1) for i in range(1, PEN - 1)])

    inner, sums = call(
        inner_kernel, [VMEM] * 3, [block, shape(2, 8, 128)], [(BX + 2, BY, N)]
    )(residual, direction, material)
    operated, send = call(
        operated_kernel,
        [VMEM] * 10,
        [pltpu.HBM((BX, BY, N), F32), pltpu.HBM((PEN, 17, 4, 128), F32)],
        [(BX, BY, N), (PEN, 17, 4, 128), pltpu.SemaphoreType.DMA((2,))],
    )(inner, sums, direction, material, xl, xh, ya, yb, high, low)
    recv_q = exchange(send, "pen")

    field_r, inside_r, states, table = call(
        residual_blocks_kernel,
        [VMEM, VMEM, VMEM, SMEM, VMEM],
        [
            pltpu.HBM((BX, BK, N), F32),
            pltpu.HBM((BX, BK, N), F32),
            shape(GRP, 8, 1, 128),
            shape(2, BK, N),
        ],
        [(BX, BK, N)] * 3 + [pltpu.SemaphoreType.DMA((2,))],
    )(recv_r, high, low, ez, ey_row)
    field_q, send = call(
        operated_blocks_kernel,
        [HBM, HBM] + [VMEM] * 4,
        [block, shape(GRP, 17, 1, 128)],
        [(BX, BK, N), (PEN, 17, 4, 128), (BX, BK, N), pltpu.SemaphoreType.DMA((3, 4))],
    )(in_hbm(recv_q), in_hbm(inside_r), states, table, high, low)

    recv = exchange(send, "grp")
    send, control = call(
        interface_kernel, [VMEM, SMEM, VMEM], [shape(GRP, 9, 1, 128), shape(3, 8, 128)]
    )(recv, ez, ey_tile)

    recv = exchange(send, "grp")
    (send,) = call(
        solve_kernel,
        [VMEM] * 7,
        [shape(PEN, 17, 4, 128)],
        [(BX, BK, N)] * 3,
    )(field_r, field_q, recv, control, table, high, low)

    recv = exchange(send, "pen")
    return tuple(
        call(
            finish_kernel,
            [VMEM] * 7,
            [pltpu.HBM((BX, BY, N), F32), pltpu.HBM((BX, BY, N), F32)],
            [(PEN, 2, 8, BX * BY), (BX, BY, N), (BX, BY, N), pltpu.SemaphoreType.DMA((2,))],
        )(recv, residual, direction, operated, control, high, low)
    )


def solution(mesh):
    placed = P("grp", "pen", None)
    return jax.shard_map(
        on_device,
        mesh=mesh,
        in_specs=(placed, placed, placed),
        out_specs=(placed, placed),
        check_vma=False,
    )
```

```python
import functools
import math

import jax
import jax.numpy as jnp
import numpy as np
from jax import lax
from jax.experimental import pallas as pl
from jax.experimental.pallas import tpu as pltpu
from jax.sharding import PartitionSpec as P

N = 512
GRP = 16
PEN = 32
BX = N // GRP
BY = N // PEN
BK = N // PEN
ABSORPTION = 0.02
CONDUCT = 5.0
SOLID = math.sqrt(30.0)
F32 = jnp.float32
VMEM = pl.BlockSpec(memory_space=pltpu.VMEM)
HBM = pl.BlockSpec(memory_space=pltpu.HBM)
SMEM = pl.BlockSpec(memory_space=pltpu.SMEM)
PARAMS = pltpu.CompilerParams(vmem_limit_bytes=48 * 1024 * 1024)


def dct_matrix():
    k = np.arange(N)[:, None]
    n = np.arange(N)[None, :]
    weight = np.where(k == 0, math.sqrt(1.0 / N), math.sqrt(2.0 / N))
    return weight * np.cos(math.pi * (k * (2 * n + 1) % (4 * N)) / (2.0 * N))


def eigen_values():
    return (4.0 * np.sin(math.pi * np.arange(N) / (2.0 * N)) ** 2).astype(np.float32)


def halves(x):
    high = x.astype(jnp.bfloat16)
    return high, (x - high.astype(F32)).astype(jnp.bfloat16)


def product(a, b, dims):
    def one(x, y):
        return lax.dot_general(x, y, (dims, ((), ())), preferred_element_type=F32)

    return one(a[0], b[0]) + (one(a[0], b[1]) + one(a[1], b[0]))


def whole(refs):
    return tuple(ref[...] for ref in refs)


def decay(shift):
    rho = 2.0 / (2.0 + shift + jnp.sqrt(shift * (shift + 4.0)))
    return rho, rho / (CONDUCT * (1.0 - rho * rho))


def turn(x, units):
    return pltpu.roll(x, 16 * units % 128, 1) if units % 8 else x


def swap_units(rows):
    unit = lax.broadcasted_iota(jnp.int32, rows[0].shape, 1) // 16
    rows = [turn(row, i) for i, row in enumerate(rows)]
    for d in (1, 2, 4):
        late = (unit & d) != 0
        rows = [jnp.where(late, rows[(i + d) % 8], rows[i]) for i in range(8)]
    return [turn(rows[-k % 8], -k) for k in range(8)]


def to_tile(x):
    x = x[:8] + x[8:]
    return x[:, 0:128] + x[:, 128:256] + x[:, 256:384] + x[:, 384:512]


def fold(x, step):
    return x + pltpu.roll(x, step, 0)


def stiffness_of(material):
    return jnp.where(material == 1, jnp.float32(SOLID), jnp.float32(1.0))


def even_pen():
    return lax.rem(lax.axis_index("pen"), 2) == 0


def faces_kernel(d_ref, m_ref, xlo_ref, xhi_ref, first_ref, second_ref):
    xlo_ref[0] = stiffness_of(m_ref[0]) * d_ref[0]
    xhi_ref[0] = stiffness_of(m_ref[BX - 1]) * d_ref[BX - 1]
    low = stiffness_of(m_ref[:, 0, :]) * d_ref[:, 0, :]
    high = stiffness_of(m_ref[:, BY - 1, :]) * d_ref[:, BY - 1, :]
    first_ref[...] = jnp.where(even_pen(), high, low)
    second_ref[...] = jnp.where(even_pen(), low, high)


def start(copies):
    for copy in copies:
        copy.start()
    return copies


def wait(copies):
    for copy in copies:
        copy.wait()


def third_modes(field_ref, c_refs, put):
    modes = product(whole(c_refs), halves(field_ref[...].reshape(BX * BY, N)), ((1,), (1,)))
    for b in range(4):
        part = modes[:, 128 * b : 128 * b + 128].reshape(PEN, 2, 8, 128)
        for a in range(2):
            put(4 * a + b, part[:, a])


def residual_kernel(r_hbm, ch_hbm, cl_hbm, send_hbm, r_ref, ch_ref, cl_ref, send_ref, sems):
    wait(
        start(
            [
                pltpu.make_async_copy(r_hbm, r_ref, sems.at[0]),
                pltpu.make_async_copy(ch_hbm, ch_ref, sems.at[1]),
                pltpu.make_async_copy(cl_hbm, cl_ref, sems.at[2]),
            ]
        )
    )

    def put(tile, x):
        send_ref[:, tile] = x

    third_modes(r_ref, (ch_ref, cl_ref), put)
    wait(start([pltpu.make_async_copy(send_ref, send_hbm, sems.at[3])]))


def inner_kernel(r_ref, d_ref, m_ref, q_ref, sums_ref, u_ref):
    u_ref[0] = jnp.zeros((BY, N), F32)
    u_ref[BX + 1] = jnp.zeros((BY, N), F32)

    def scale(x, _):
        u_ref[x + 1] = stiffness_of(m_ref[x]) * d_ref[x]
        return 0

    lax.fori_loop(0, BX, scale, 0, unroll=4)
    row = lax.broadcasted_iota(jnp.int32, (BY, N), 0)
    lane = lax.broadcasted_iota(jnp.int32, (BY, N), 1)

    def stencil(x, sums):
        u = u_ref[x + 1]
        d = d_ref[x]
        beside = u_ref[x] + u_ref[x + 2]
        beside += jnp.where(row == 0, 0.0, pltpu.roll(u, 1, 0))
        beside += jnp.where(row == BY - 1, 0.0, pltpu.roll(u, BY - 1, 0))
        beside += jnp.where(lane == 0, 0.0, pltpu.roll(u, 1, 1))
        beside += jnp.where(lane == N - 1, 0.0, pltpu.roll(u, N - 1, 1))
        q = ABSORPTION * d + stiffness_of(m_ref[x]) * (6.0 * u - beside)
        q_ref[x] = q
        return sums[0] + to_tile(d * q), sums[1] + to_tile(r_ref[x] * d)

    zero = jnp.zeros((8, 128), F32)
    sums = lax.fori_loop(0, BX, stencil, (zero, zero), unroll=4)
    sums_ref[0], sums_ref[1] = sums


def operated_kernel(
    q_ref, sums_ref, d_ref, m_ref, yb_ref, xl_ref, xh_ref, ya_ref, ch_ref, cl_ref, out_hbm, send_hbm, out_ref, send_ref, sems
):
    row = lax.broadcasted_iota(jnp.int32, (8, N), 0)

    def low_high(x, total):
        ya, yb = ya_ref[pl.ds(x, 1), :], yb_ref[pl.ds(x, 1), :]
        low, high = jnp.where(even_pen(), yb, ya), jnp.where(even_pen(), ya, yb)
        for first, edge, side in ((0, 0, low), (8, 7, high)):
            rows = pl.ds(first, 8)
            add = stiffness_of(m_ref[x, rows]) * jnp.where(row == edge, side, 0.0)
            out_ref[x, rows] = q_ref[x, rows] - add
            total = total + d_ref[x, rows] * add
        return total

    total = lax.fori_loop(0, BX, low_high, jnp.zeros((8, N), F32), unroll=4)
    total = jnp.concatenate([total, jnp.zeros((8, N), F32)], axis=0)
    for x, side_ref in ((0, xl_ref), (BX - 1, xh_ref)):
        add = stiffness_of(m_ref[x]) * side_ref[0]
        out_ref[x] = out_ref[x] - add
        total = total + d_ref[x] * add
    curvature = sums_ref[0] - to_tile(total)
    first = lax.broadcasted_iota(jnp.int32, (8, 128), 0) < 2
    sums = jnp.where(first, fold(fold(curvature, 4), 2), fold(fold(sums_ref[1], 4), 2))
    for j in range(PEN):
        send_ref[j, 16] = sums[:4]
    copies = start([pltpu.make_async_copy(out_ref, out_hbm, sems.at[0])])

    def put(tile, x):
        send_ref[:, 2 * tile] = x[:, :4]
        send_ref[:, 2 * tile + 1] = x[:, 4:]

    third_modes(out_ref, (ch_ref, cl_ref), put)
    wait(copies + start([pltpu.make_async_copy(send_ref, send_hbm, sems.at[1])]))


def second_modes(get, c_refs, out_ref, y_ref, ready=lambda b: None):
    def part(b, _):
        ready(b)
        for s in range(4):
            for a in range(2):
                rows = swap_units([get(8 * s + i, 4 * a + b) for i in range(8)])
                for i in range(8):
                    y_ref[8 * b + i, 8 * a : 8 * a + 8, 128 * s : 128 * s + 128] = rows[i]
        return 0

    lax.fori_loop(0, 4, part, 0)
    field = halves(y_ref[...].reshape(BX * BK, N))
    out_ref[...] = product(field, whole(c_refs), ((1,), (1,))).reshape(BX, BK, N)


def third_eigen(ez_ref, h):
    k0 = lax.axis_index("pen") * BK + 8 * h
    return jnp.concatenate([jnp.full((1, N), ez_ref[k0 + i], F32) for i in range(8)], axis=0)


def put_states(v, w, h, send_ref, first):
    for side, x in enumerate((v, w)):
        for b in range(4):
            for i in range(8):
                send_ref[8 * h + i, first + 4 * side + b] = x[i : i + 1, 128 * b : 128 * b + 128]


def residual_blocks_kernel(
    recv_ref, ch_ref, cl_ref, ez_ref, ey_ref, fr_hbm, zr_hbm, states_ref, table_ref, y_ref, fr_ref, zr_ref, sems
):
    second_modes(lambda j, tile: recv_ref[j, tile], (ch_ref, cl_ref), fr_ref, y_ref)
    copies = start([pltpu.make_async_copy(fr_ref, fr_hbm, sems.at[0])])
    for h in range(2):
        rows = pl.ds(8 * h, 8)
        rho, factor = decay(ABSORPTION / CONDUCT + third_eigen(ez_ref, h) + ey_ref[...])
        table_ref[0, rows] = rho
        table_ref[1, rows] = factor

        def rise(x, v):
            v = fr_ref[x, rows] + rho * v
            zr_ref[x, rows] = v
            return v

        def fall(i, w):
            x = BX - 1 - i
            before = rho * w
            zr_ref[x, rows] = factor * (zr_ref[x, rows] + before)
            return fr_ref[x, rows] + before

        zero = jnp.zeros((8, N), F32)
        v = lax.fori_loop(0, BX, rise, zero, unroll=4)
        w = lax.fori_loop(0, BX, fall, zero, unroll=4)
        put_states(v, w, h, states_ref, 0)
    wait(copies + start([pltpu.make_async_copy(zr_ref, zr_hbm, sems.at[1])]))


def operated_blocks_kernel(
    recv_hbm, zr_hbm, states_ref, table_ref, ch_ref, cl_ref, fq_ref, send_ref, y_ref, recv_ref, zr_ref, sems
):
    def into(b):
        tiles = [pl.ds(2 * b, 2), pl.ds(2 * b + 8, 2)]
        return [
            pltpu.make_async_copy(recv_hbm.at[:, t], recv_ref.at[:, t], sems.at[i, b])
            for i, t in enumerate(tiles)
        ]

    for b in range(4):
        start(into(b))
    late = start(
        [
            pltpu.make_async_copy(recv_hbm.at[:, 16], recv_ref.at[:, 16], sems.at[2, 0]),
            pltpu.make_async_copy(zr_hbm, zr_ref, sems.at[2, 1]),
        ]
    )

    def get(j, tile):
        return jnp.concatenate([recv_ref[j, 2 * tile], recv_ref[j, 2 * tile + 1]], axis=0)

    second_modes(get, (ch_ref, cl_ref), fq_ref, y_ref, lambda b: wait(into(b)))
    wait(late)
    dots = [jnp.zeros((8, 128), F32), jnp.zeros((8, 128), F32)]
    for h in range(2):
        rows = pl.ds(8 * h, 8)
        rho = table_ref[0, rows]

        def sweep(x, carry):
            power, vq, wq, rq, qq = carry
            q = fq_ref[x, rows]
            before = rho * vq
            vq = q + before
            return power * rho, vq, wq + power * q, rq + zr_ref[x, rows] * q, qq + (vq + before) * q

        zero = jnp.zeros((8, N), F32)
        carry = (jnp.ones((8, N), F32),) + (zero,) * 4
        _, vq, wq, rq, qq = lax.fori_loop(0, BX, sweep, carry, unroll=4)
        put_states(vq, wq, h, send_ref, 8)
        for i, x in enumerate((rq, table_ref[1, rows] * qq)):
            dots[i] += x[:, 0:128] + x[:, 128:256] + x[:, 256:384] + x[:, 384:512]

    sums = recv_ref[0, 16]
    for j in range(1, PEN):
        sums = sums + recv_ref[j, 16]
    group = lax.broadcasted_iota(jnp.int32, (1, 128), 1) // 32
    packed = jnp.zeros((1, 128), F32)
    for i, x in enumerate((sums[0:2], sums[2:4], dots[0], dots[1])):
        x = jnp.sum(x, axis=0, keepdims=True)
        x = x + pltpu.roll(x, 64, 1)
        packed = jnp.where(group == i, x + pltpu.roll(x, 32, 1), packed)
    for j in range(GRP):
        send_ref[j, 0:8] = states_ref[j]
        send_ref[j, 16] = packed


def interface_kernel(recv_ref, ez_ref, ey_ref, send_ref, control_ref):
    row = lax.broadcasted_iota(jnp.int32, (8, 128), 0)
    group = lax.broadcasted_iota(jnp.int32, (1, 128), 1) // 32
    sums = recv_ref[0, 16]
    for p in range(1, GRP):
        sums = sums + recv_ref[p, 16]

    def total(i):
        return jnp.full((8, 128), jnp.sum(jnp.where(group == i, sums, 0.0)), F32)

    curvature, projection, rq, qq = total(0), total(1), total(2), total(3)
    step = projection / curvature
    ez = ez_ref[lax.axis_index("pen") * BK + lax.axis_index("grp")]
    rho, factor = decay(ABSORPTION / CONDUCT + ez + ey_ref[...])
    across = rho
    for _ in range(5):
        across = across * across
    others = [recv_ref[p, 8:16].reshape(8, 128) for p in range(GRP)]
    tiles = [recv_ref[p, 0:8].reshape(8, 128) - step * others[p] for p in range(GRP)]
    zero = jnp.zeros((8, 128), F32)
    rising = [zero]
    for p in range(GRP):
        rising.append(tiles[p] + across * rising[-1])
    falling = [zero]
    for p in reversed(range(GRP)):
        falling.append(tiles[p] + across * falling[-1])
    lower = row < 4
    ends = jnp.where(lower, rising[GRP], falling[GRP])
    powers = [jnp.ones((8, 128), F32)]
    for p in range(GRP):
        powers.append(powers[-1] * across)
    whole = powers[GRP]
    images = (pltpu.roll(ends, 4, 0) + whole * ends) / (1.0 - whole * whole)
    dots = zero
    for p in range(GRP):
        state = jnp.where(
            lower,
            rising[p] + powers[p] * images,
            falling[GRP - 1 - p] + powers[GRP - 1 - p] * images,
        )
        send_ref[p, 0:8] = state.reshape(8, 1, 128)
        dots = dots + state * pltpu.roll(others[p], 4, 0)
    dots = jnp.sum(rho * factor * dots, axis=0, keepdims=True)
    for p in range(GRP):
        send_ref[p, 8] = dots
    control_ref[0] = step
    control_ref[1] = curvature
    control_ref[2] = rq - step * qq


def solve_kernel(
    fr_ref, fq_ref, recv_ref, control_ref, table_ref, ch_ref, cl_ref, send_ref, f_ref, u_ref, y_ref
):
    step = control_ref[0, 0:1, 0:1]
    rho, factor = table_ref[0], table_ref[1]

    def state(side):
        return jnp.concatenate(
            [
                jnp.concatenate([recv_ref[i, 4 * side + b] for i in range(BK)], axis=0)
                for b in range(4)
            ],
            axis=1,
        )

    def rise(x, carry):
        f = fr_ref[x] - step * fq_ref[x]
        carry = f + rho * carry
        f_ref[x] = f
        u_ref[x] = carry
        return carry

    def fall(i, carry):
        x = BX - 1 - i
        carry = rho * carry
        u_ref[x] = factor * (u_ref[x] + carry)
        return f_ref[x] + carry

    lax.fori_loop(0, BX, rise, state(0), unroll=4)
    lax.fori_loop(0, BX, fall, state(1), unroll=4)
    solved = halves(u_ref[...].reshape(BX * BK, N))
    y_ref[...] = product(solved, (ch_ref[...], cl_ref[...]), ((1,), (0,))).reshape(BX, BK, N)

    def part(b, _):
        for s in range(4):
            for a in range(2):
                rows = swap_units(
                    [y_ref[8 * b + i, 8 * a : 8 * a + 8, 128 * s : 128 * s + 128] for i in range(8)]
                )
                for i in range(8):
                    tile = 8 * a + 2 * b
                    send_ref[8 * s + i, tile] = rows[i][:4]
                    send_ref[8 * s + i, tile + 1] = rows[i][4:]
        return 0

    lax.fori_loop(0, 4, part, 0)
    sums = recv_ref[0, 8]
    for p in range(1, GRP):
        sums = sums + recv_ref[p, 8]
    row = lax.broadcasted_iota(jnp.int32, (8, 128), 0)
    first = (row == 0) & (lax.broadcasted_iota(jnp.int32, (8, 128), 1) == 0)
    sums = jnp.where(row == 0, sums, 0.0) + jnp.where(first, control_ref[2], 0.0)
    for j in range(PEN):
        send_ref[j, 16] = sums[:4]


def finish_kernel(
    recv_ref, r_ref, d_ref, q_ref, control_ref, ch_ref, cl_ref, nr_hbm, nd_hbm, g_ref, nr_ref, nd_ref, sems
):
    nr_ref[...] = r_ref[...] - control_ref[0, 0:1, 0:1] * q_ref[...]
    copies = start([pltpu.make_async_copy(nr_ref, nr_hbm, sems.at[0])])
    for b in range(4):
        for a in range(2):
            for c in range(2):
                rows = slice(4 * c, 4 * c + 4)
                g_ref[:, a, rows, 128 * b : 128 * b + 128] = recv_ref[:, 8 * a + 2 * b + c]
    sums = recv_ref[0, 16]
    for j in range(1, PEN):
        sums = sums + recv_ref[j, 16]
    conjugacy = jnp.full((8, 128), jnp.sum(sums), F32)
    ratio = (conjugacy / control_ref[1])[0:1, 0:1]
    modes = halves(g_ref[...].reshape(N, BX * BY))
    smoothed = product(modes, (ch_ref[...], cl_ref[...]), ((0,), (0,)))
    nd_ref[...] = smoothed.reshape(BX, BY, N) - ratio * d_ref[...]
    wait(copies + start([pltpu.make_async_copy(nd_ref, nd_hbm, sems.at[1])]))


def shape(*dims):
    return jax.ShapeDtypeStruct(dims, F32)


def in_hbm(x):
    return pltpu.with_memory_space_constraint(x, pltpu.HBM)


def call(kernel, ins, outs, scratch=()):
    return pl.pallas_call(
        kernel,
        in_specs=ins,
        out_specs=[VMEM if isinstance(out, jax.ShapeDtypeStruct) else HBM for out in outs],
        out_shape=outs,
        scratch_shapes=[pltpu.VMEM(s, F32) if isinstance(s, tuple) else s for s in scratch],
        compiler_params=PARAMS,
    )


def exchange(x, axis):
    return lax.all_to_all(x, axis, 0, 0)


def on_device(residual, direction, material):
    matrix = dct_matrix()
    high = matrix.astype(jnp.bfloat16)
    low = (matrix - high.astype(np.float64)).astype(jnp.bfloat16)
    high, low = jnp.asarray(high), jnp.asarray(low)
    eigen = eigen_values()
    ez = jnp.asarray(eigen)
    ey_row = jnp.asarray(eigen[None, :])
    ey_tile = jnp.asarray(np.concatenate([eigen.reshape(4, 128)] * 2, 0))
    block = shape(BX, BY, N)
    half = pltpu.VMEM((N, N), jnp.bfloat16)

    (send,) = call(
        residual_kernel,
        [HBM] * 3,
        [pltpu.HBM((PEN, 8, 8, 128), F32)],
        [(BX, BY, N), half, half, (PEN, 8, 8, 128), pltpu.SemaphoreType.DMA((4,))],
    )(in_hbm(residual), in_hbm(high), in_hbm(low))
    recv_r = exchange(send, "pen")

    xlo, xhi, first, second = call(
        faces_kernel, [VMEM] * 2, [shape(1, BY, N), shape(1, BY, N), shape(BX, N), shape(BX, N)]
    )(direction, material)

    def up(x, axis, count):
        return lax.ppermute(x, axis, [(i, i + 1) for i in range(count - 1)])

    def down(x, axis, count):
        return lax.ppermute(x, axis, [(i + 1, i) for i in range(count - 1)])

    yb = lax.ppermute(second, "pen", [(i, i + 1 if i % 2 else i - 1) for i in range(1, PEN - 1)])
    xl, xh = up(xhi, "grp", GRP), down(xlo, "grp", GRP)
    ya = lax.ppermute(first, "pen", [(i, i ^ 1) for i in range(PEN)])
    inner, sums = call(
        inner_kernel, [VMEM] * 3, [block, shape(2, 8, 128)], [(BX + 2, BY, N)]
    )(residual, direction, material)
    operated, send = call(
        operated_kernel,
        [VMEM] * 10,
        [pltpu.HBM((BX, BY, N), F32), pltpu.HBM((PEN, 17, 4, 128), F32)],
        [(BX, BY, N), (PEN, 17, 4, 128), pltpu.SemaphoreType.DMA((2,))],
    )(inner, sums, direction, material, yb, xl, xh, ya, high, low)
    recv_q = exchange(send, "pen")

    field_r, inside_r, states, table = call(
        residual_blocks_kernel,
        [VMEM, VMEM, VMEM, SMEM, VMEM],
        [
            pltpu.HBM((BX, BK, N), F32),
            pltpu.HBM((BX, BK, N), F32),
            shape(GRP, 8, 1, 128),
            shape(2, BK, N),
        ],
        [(BX, BK, N)] * 3 + [pltpu.SemaphoreType.DMA((2,))],
    )(recv_r, high, low, ez, ey_row)
    field_q, send = call(
        operated_blocks_kernel,
        [HBM, HBM] + [VMEM] * 4,
        [block, shape(GRP, 17, 1, 128)],
        [(BX, BK, N), (PEN, 17, 4, 128), (BX, BK, N), pltpu.SemaphoreType.DMA((3, 4))],
    )(in_hbm(recv_q), in_hbm(inside_r), states, table, high, low)

    recv = exchange(send, "grp")
    send, control = call(
        interface_kernel, [VMEM, SMEM, VMEM], [shape(GRP, 9, 1, 128), shape(3, 8, 128)]
    )(recv, ez, ey_tile)

    recv = exchange(send, "grp")
    (send,) = call(
        solve_kernel,
        [VMEM] * 7,
        [shape(PEN, 17, 4, 128)],
        [(BX, BK, N)] * 3,
    )(field_r, field_q, recv, control, table, high, low)

    recv = exchange(send, "pen")
    return tuple(
        call(
            finish_kernel,
            [VMEM] * 7,
            [pltpu.HBM((BX, BY, N), F32), pltpu.HBM((BX, BY, N), F32)],
            [(PEN, 2, 8, BX * BY), (BX, BY, N), (BX, BY, N), pltpu.SemaphoreType.DMA((2,))],
        )(recv, residual, direction, operated, control, high, low)
    )


def solution(mesh):
    placed = P("grp", "pen", None)
    return jax.shard_map(
        on_device,
        mesh=mesh,
        in_specs=(placed, placed, placed),
        out_specs=(placed, placed),
        check_vma=False,
    )
```

```python
import functools
import math

import jax
import jax.numpy as jnp
import numpy as np
from jax import lax
from jax.experimental import pallas as pl
from jax.experimental.pallas import tpu as pltpu
from jax.sharding import PartitionSpec as P

N = 512
GRP = 16
PEN = 32
BX = N // GRP
BY = N // PEN
BK = N // PEN
ABSORPTION = 0.02
CONDUCT = 5.0
SOLID = math.sqrt(30.0)
F32 = jnp.float32
VMEM = pl.BlockSpec(memory_space=pltpu.VMEM)
HBM = pl.BlockSpec(memory_space=pltpu.HBM)
SMEM = pl.BlockSpec(memory_space=pltpu.SMEM)
PARAMS = pltpu.CompilerParams(vmem_limit_bytes=48 * 1024 * 1024)


def dct_matrix():
    k = np.arange(N)[:, None]
    n = np.arange(N)[None, :]
    weight = np.where(k == 0, math.sqrt(1.0 / N), math.sqrt(2.0 / N))
    return weight * np.cos(math.pi * (k * (2 * n + 1) % (4 * N)) / (2.0 * N))


def eigen_values():
    return (4.0 * np.sin(math.pi * np.arange(N) / (2.0 * N)) ** 2).astype(np.float32)


def halves(x):
    high = x.astype(jnp.bfloat16)
    return high, (x - high.astype(F32)).astype(jnp.bfloat16)


def product(a, b, dims):
    def one(x, y):
        return lax.dot_general(x, y, (dims, ((), ())), preferred_element_type=F32)

    return one(a[0], b[0]) + (one(a[0], b[1]) + one(a[1], b[0]))


def whole(refs):
    return tuple(ref[...] for ref in refs)


def decay(shift):
    rho = 2.0 / (2.0 + shift + jnp.sqrt(shift * (shift + 4.0)))
    return rho, rho / (CONDUCT * (1.0 - rho * rho))


def turn(x, units):
    return pltpu.roll(x, 16 * units % 128, 1) if units % 8 else x


def swap_units(rows):
    unit = lax.broadcasted_iota(jnp.int32, rows[0].shape, 1) // 16
    rows = [turn(row, i) for i, row in enumerate(rows)]
    for d in (1, 2, 4):
        late = (unit & d) != 0
        rows = [jnp.where(late, rows[(i + d) % 8], rows[i]) for i in range(8)]
    return [turn(rows[-k % 8], -k) for k in range(8)]


def to_tile(x):
    x = x[:8] + x[8:]
    return x[:, 0:128] + x[:, 128:256] + x[:, 256:384] + x[:, 384:512]


def fold(x, step):
    return x + pltpu.roll(x, step, 0)


def stiffness_of(material):
    return jnp.where(material == 1, jnp.float32(SOLID), jnp.float32(1.0))


def even_pen():
    return lax.rem(lax.axis_index("pen"), 2) == 0


def faces_kernel(d_ref, m_ref, xlo_ref, xhi_ref, first_ref, second_ref):
    xlo_ref[0] = stiffness_of(m_ref[0]) * d_ref[0]
    xhi_ref[0] = stiffness_of(m_ref[BX - 1]) * d_ref[BX - 1]
    low = stiffness_of(m_ref[:, 0, :]) * d_ref[:, 0, :]
    high = stiffness_of(m_ref[:, BY - 1, :]) * d_ref[:, BY - 1, :]
    first_ref[...] = jnp.where(even_pen(), high, low)
    second_ref[...] = jnp.where(even_pen(), low, high)


def start(copies):
    for copy in copies:
        copy.start()
    return copies


def wait(copies):
    for copy in copies:
        copy.wait()


def send_third_modes(field_ref, c_refs, put, send_ref, send_hbm, sems):
    field = halves(field_ref[...].reshape(BX * BY, N))
    copies = []
    for h in range(2):
        devices = slice(h * PEN // 2, (h + 1) * PEN // 2)
        rows = slice(h * N // 2, (h + 1) * N // 2)
        modes = product(tuple(ref[rows] for ref in c_refs), field, ((1,), (1,)))
        for b in range(4):
            part = modes[:, 128 * b : 128 * b + 128].reshape(PEN // 2, 2, 8, 128)
            for a in range(2):
                put(devices, 4 * a + b, part[:, a])
        target = pl.ds(h * PEN // 2, PEN // 2)
        copies += start(
            [pltpu.make_async_copy(send_ref.at[target], send_hbm.at[target], sems.at[h])]
        )
    return copies


def residual_kernel(r_hbm, ch_hbm, cl_hbm, send_hbm, r_ref, ch_ref, cl_ref, send_ref, sems):
    wait(
        start(
            [
                pltpu.make_async_copy(r_hbm, r_ref, sems.at[2]),
                pltpu.make_async_copy(ch_hbm, ch_ref, sems.at[3]),
                pltpu.make_async_copy(cl_hbm, cl_ref, sems.at[4]),
            ]
        )
    )

    def put(devices, tile, x):
        send_ref[devices, tile] = x

    wait(send_third_modes(r_ref, (ch_ref, cl_ref), put, send_ref, send_hbm, sems))


def inner_kernel(r_ref, d_ref, m_ref, q_ref, sums_ref, u_ref):
    u_ref[0] = jnp.zeros((BY, N), F32)
    u_ref[BX + 1] = jnp.zeros((BY, N), F32)

    def scale(x, _):
        u_ref[x + 1] = stiffness_of(m_ref[x]) * d_ref[x]
        return 0

    lax.fori_loop(0, BX, scale, 0, unroll=4)
    row = lax.broadcasted_iota(jnp.int32, (BY, N), 0)
    lane = lax.broadcasted_iota(jnp.int32, (BY, N), 1)

    def stencil(x, sums):
        u = u_ref[x + 1]
        d = d_ref[x]
        beside = u_ref[x] + u_ref[x + 2]
        beside += jnp.where(row == 0, 0.0, pltpu.roll(u, 1, 0))
        beside += jnp.where(row == BY - 1, 0.0, pltpu.roll(u, BY - 1, 0))
        beside += jnp.where(lane == 0, 0.0, pltpu.roll(u, 1, 1))
        beside += jnp.where(lane == N - 1, 0.0, pltpu.roll(u, N - 1, 1))
        q = ABSORPTION * d + stiffness_of(m_ref[x]) * (6.0 * u - beside)
        q_ref[x] = q
        return sums[0] + to_tile(d * q), sums[1] + to_tile(r_ref[x] * d)

    zero = jnp.zeros((8, 128), F32)
    sums = lax.fori_loop(0, BX, stencil, (zero, zero), unroll=4)
    sums_ref[0], sums_ref[1] = sums


def operated_kernel(
    q_ref, sums_ref, d_ref, m_ref, yb_ref, xl_ref, xh_ref, ya_ref, ch_ref, cl_ref, out_hbm, send_hbm, out_ref, send_ref, sems
):
    row = lax.broadcasted_iota(jnp.int32, (8, N), 0)

    def low_high(x, total):
        ya, yb = ya_ref[pl.ds(x, 1), :], yb_ref[pl.ds(x, 1), :]
        low, high = jnp.where(even_pen(), yb, ya), jnp.where(even_pen(), ya, yb)
        for first, edge, side in ((0, 0, low), (8, 7, high)):
            rows = pl.ds(first, 8)
            add = stiffness_of(m_ref[x, rows]) * jnp.where(row == edge, side, 0.0)
            out_ref[x, rows] = q_ref[x, rows] - add
            total = total + d_ref[x, rows] * add
        return total

    total = lax.fori_loop(0, BX, low_high, jnp.zeros((8, N), F32), unroll=4)
    total = jnp.concatenate([total, jnp.zeros((8, N), F32)], axis=0)
    for x, side_ref in ((0, xl_ref), (BX - 1, xh_ref)):
        add = stiffness_of(m_ref[x]) * side_ref[0]
        out_ref[x] = out_ref[x] - add
        total = total + d_ref[x] * add
    curvature = sums_ref[0] - to_tile(total)
    first = lax.broadcasted_iota(jnp.int32, (8, 128), 0) < 2
    sums = jnp.where(first, fold(fold(curvature, 4), 2), fold(fold(sums_ref[1], 4), 2))
    for j in range(PEN):
        send_ref[j, 16] = sums[:4]
    copies = start([pltpu.make_async_copy(out_ref, out_hbm, sems.at[2])])

    def put(devices, tile, x):
        send_ref[devices, 2 * tile] = x[:, :4]
        send_ref[devices, 2 * tile + 1] = x[:, 4:]

    wait(copies + send_third_modes(out_ref, (ch_ref, cl_ref), put, send_ref, send_hbm, sems))


def second_modes(get, c_refs, out_ref, y_ref, ready=lambda b: None):
    def part(b, _):
        ready(b)
        for s in range(4):
            for a in range(2):
                rows = swap_units([get(8 * s + i, 4 * a + b) for i in range(8)])
                for i in range(8):
                    y_ref[8 * b + i, 8 * a : 8 * a + 8, 128 * s : 128 * s + 128] = rows[i]
        return 0

    lax.fori_loop(0, 4, part, 0)
    field = halves(y_ref[...].reshape(BX * BK, N))
    out_ref[...] = product(field, whole(c_refs), ((1,), (1,))).reshape(BX, BK, N)


def third_eigen(ez_ref, h):
    k0 = lax.axis_index("pen") * BK + 8 * h
    return jnp.concatenate([jnp.full((1, N), ez_ref[k0 + i], F32) for i in range(8)], axis=0)


def put_states(v, w, h, send_ref, first):
    for side, x in enumerate((v, w)):
        for b in range(4):
            for i in range(8):
                send_ref[8 * h + i, first + 4 * side + b] = x[i : i + 1, 128 * b : 128 * b + 128]


def residual_blocks_kernel(
    recv_ref,
    ch_ref,
    cl_ref,
    ez_ref,
    ey_ref,
    tile_ref,
    fr_hbm,
    zr_hbm,
    states_ref,
    table_ref,
    across_ref,
    y_ref,
    fr_ref,
    zr_ref,
    sems,
):
    second_modes(lambda j, tile: recv_ref[j, tile], (ch_ref, cl_ref), fr_ref, y_ref)
    copies = start([pltpu.make_async_copy(fr_ref, fr_hbm, sems.at[0])])
    for h in range(2):
        rows = pl.ds(8 * h, 8)
        rho, factor = decay(ABSORPTION / CONDUCT + third_eigen(ez_ref, h) + ey_ref[...])
        table_ref[0, rows] = rho
        table_ref[1, rows] = factor

        def rise(x, v):
            v = fr_ref[x, rows] + rho * v
            zr_ref[x, rows] = v
            return v

        def fall(i, w):
            x = BX - 1 - i
            before = rho * w
            zr_ref[x, rows] = factor * (zr_ref[x, rows] + before)
            return fr_ref[x, rows] + before

        zero = jnp.zeros((8, N), F32)
        v = lax.fori_loop(0, BX, rise, zero, unroll=4)
        w = lax.fori_loop(0, BX, fall, zero, unroll=4)
        put_states(v, w, h, states_ref, 0)
    copies += start([pltpu.make_async_copy(zr_ref, zr_hbm, sems.at[1])])
    ez = ez_ref[lax.axis_index("pen") * BK + lax.axis_index("grp")]
    rho, factor = decay(ABSORPTION / CONDUCT + ez + tile_ref[...])
    across = rho
    for _ in range(5):
        across = across * across
    power = jnp.ones((8, 128), F32)
    for p in range(GRP):
        across_ref[p] = power
        power = power * across
    across_ref[GRP] = power
    across_ref[GRP + 1] = rho * factor
    across_ref[GRP + 2] = 1.0 / (1.0 - power * power)
    wait(copies)


def operated_blocks_kernel(
    recv_hbm, zr_hbm, states_ref, table_ref, ch_ref, cl_ref, fq_ref, send_ref, y_ref, recv_ref, zr_ref, sems
):
    def into(b):
        tiles = [pl.ds(2 * b, 2), pl.ds(2 * b + 8, 2)]
        return [
            pltpu.make_async_copy(recv_hbm.at[:, t], recv_ref.at[:, t], sems.at[i, b])
            for i, t in enumerate(tiles)
        ]

    for b in range(4):
        start(into(b))
    late = start(
        [
            pltpu.make_async_copy(recv_hbm.at[:, 16], recv_ref.at[:, 16], sems.at[2, 0]),
            pltpu.make_async_copy(zr_hbm, zr_ref, sems.at[2, 1]),
        ]
    )

    def get(j, tile):
        return jnp.concatenate([recv_ref[j, 2 * tile], recv_ref[j, 2 * tile + 1]], axis=0)

    second_modes(get, (ch_ref, cl_ref), fq_ref, y_ref, lambda b: wait(into(b)))
    wait(late)
    dots = [jnp.zeros((8, 128), F32), jnp.zeros((8, 128), F32)]
    for h in range(2):
        rows = pl.ds(8 * h, 8)
        rho = table_ref[0, rows]

        def sweep(x, carry):
            power, vq, wq, rq, qq = carry
            q = fq_ref[x, rows]
            before = rho * vq
            vq = q + before
            return power * rho, vq, wq + power * q, rq + zr_ref[x, rows] * q, qq + (vq + before) * q

        zero = jnp.zeros((8, N), F32)
        carry = (jnp.ones((8, N), F32),) + (zero,) * 4
        _, vq, wq, rq, qq = lax.fori_loop(0, BX, sweep, carry, unroll=4)
        put_states(vq, wq, h, send_ref, 8)
        for i, x in enumerate((rq, table_ref[1, rows] * qq)):
            dots[i] += x[:, 0:128] + x[:, 128:256] + x[:, 256:384] + x[:, 384:512]

    sums = recv_ref[0, 16]
    for j in range(1, PEN):
        sums = sums + recv_ref[j, 16]
    group = lax.broadcasted_iota(jnp.int32, (1, 128), 1) // 32
    packed = jnp.zeros((1, 128), F32)
    for i, x in enumerate((sums[0:2], sums[2:4], dots[0], dots[1])):
        x = jnp.sum(x, axis=0, keepdims=True)
        x = x + pltpu.roll(x, 64, 1)
        packed = jnp.where(group == i, x + pltpu.roll(x, 32, 1), packed)
    for j in range(GRP):
        send_ref[j, 0:8] = states_ref[j]
        send_ref[j, 16] = packed


def interface_kernel(recv_ref, across_ref, send_ref, control_ref):
    row = lax.broadcasted_iota(jnp.int32, (8, 128), 0)
    group = lax.broadcasted_iota(jnp.int32, (1, 128), 1) // 32
    sums = recv_ref[0, 16]
    for p in range(1, GRP):
        sums = sums + recv_ref[p, 16]

    def total(i):
        return jnp.full((8, 128), jnp.sum(jnp.where(group == i, sums, 0.0)), F32)

    curvature, projection, rq, qq = total(0), total(1), total(2), total(3)
    step = projection / curvature
    across = across_ref[1]
    others = [recv_ref[p, 8:16].reshape(8, 128) for p in range(GRP)]
    tiles = [recv_ref[p, 0:8].reshape(8, 128) - step * others[p] for p in range(GRP)]
    zero = jnp.zeros((8, 128), F32)
    rising = [zero]
    for p in range(GRP):
        rising.append(tiles[p] + across * rising[-1])
    falling = [zero]
    for p in reversed(range(GRP)):
        falling.append(tiles[p] + across * falling[-1])
    lower = row < 4
    ends = jnp.where(lower, rising[GRP], falling[GRP])
    images = (pltpu.roll(ends, 4, 0) + across_ref[GRP] * ends) * across_ref[GRP + 2]
    dots = zero
    for p in range(GRP):
        state = jnp.where(
            lower,
            rising[p] + across_ref[p] * images,
            falling[GRP - 1 - p] + across_ref[GRP - 1 - p] * images,
        )
        send_ref[p, 0:8] = state.reshape(8, 1, 128)
        dots = dots + state * pltpu.roll(others[p], 4, 0)
    dots = jnp.sum(across_ref[GRP + 1] * dots, axis=0, keepdims=True)
    for p in range(GRP):
        send_ref[p, 8] = dots
    control_ref[0] = step
    control_ref[1] = curvature
    control_ref[2] = rq - step * qq


def solve_kernel(
    fr_ref, fq_ref, recv_ref, control_ref, table_ref, ch_ref, cl_ref, send_ref, f_ref, u_ref, y_ref
):
    step = control_ref[0, 0:1, 0:1]
    rho, factor = table_ref[0], table_ref[1]

    def state(side):
        return jnp.concatenate(
            [
                jnp.concatenate([recv_ref[i, 4 * side + b] for i in range(BK)], axis=0)
                for b in range(4)
            ],
            axis=1,
        )

    def rise(x, carry):
        f = fr_ref[x] - step * fq_ref[x]
        carry = f + rho * carry
        f_ref[x] = f
        u_ref[x] = carry
        return carry

    def fall(i, carry):
        x = BX - 1 - i
        carry = rho * carry
        u_ref[x] = factor * (u_ref[x] + carry)
        return f_ref[x] + carry

    lax.fori_loop(0, BX, rise, state(0), unroll=4)
    lax.fori_loop(0, BX, fall, state(1), unroll=4)
    solved = halves(u_ref[...].reshape(BX * BK, N))
    y_ref[...] = product(solved, (ch_ref[...], cl_ref[...]), ((1,), (0,))).reshape(BX, BK, N)

    def part(b, _):
        for s in range(4):
            for a in range(2):
                rows = swap_units(
                    [y_ref[8 * b + i, 8 * a : 8 * a + 8, 128 * s : 128 * s + 128] for i in range(8)]
                )
                for i in range(8):
                    tile = 8 * a + 2 * b
                    send_ref[8 * s + i, tile] = rows[i][:4]
                    send_ref[8 * s + i, tile + 1] = rows[i][4:]
        return 0

    lax.fori_loop(0, 4, part, 0)
    sums = recv_ref[0, 8]
    for p in range(1, GRP):
        sums = sums + recv_ref[p, 8]
    row = lax.broadcasted_iota(jnp.int32, (8, 128), 0)
    first = (row == 0) & (lax.broadcasted_iota(jnp.int32, (8, 128), 1) == 0)
    sums = jnp.where(row == 0, sums, 0.0) + jnp.where(first, control_ref[2], 0.0)
    for j in range(PEN):
        send_ref[j, 16] = sums[:4]


def finish_kernel(
    recv_ref, r_ref, d_ref, q_ref, control_ref, ch_ref, cl_ref, nr_hbm, nd_hbm, g_ref, nr_ref, nd_ref, sems
):
    nr_ref[...] = r_ref[...] - control_ref[0, 0:1, 0:1] * q_ref[...]
    copies = start([pltpu.make_async_copy(nr_ref, nr_hbm, sems.at[0])])
    for b in range(4):
        for a in range(2):
            for c in range(2):
                rows = slice(4 * c, 4 * c + 4)
                g_ref[:, a, rows, 128 * b : 128 * b + 128] = recv_ref[:, 8 * a + 2 * b + c]
    sums = recv_ref[0, 16]
    for j in range(1, PEN):
        sums = sums + recv_ref[j, 16]
    conjugacy = jnp.full((8, 128), jnp.sum(sums), F32)
    ratio = (conjugacy / control_ref[1])[0:1, 0:1]
    for h in range(2):
        part = pl.ds(h * BX // 2, BX // 2)
        cells = slice(h * BX * BY // 2, (h + 1) * BX * BY // 2)
        modes = halves(g_ref[:, :, :, cells].reshape(N, BX * BY // 2))
        smoothed = product(modes, (ch_ref[...], cl_ref[...]), ((0,), (0,)))
        nd_ref[part] = smoothed.reshape(BX // 2, BY, N) - ratio * d_ref[part]
        copies += start([pltpu.make_async_copy(nd_ref.at[part], nd_hbm.at[part], sems.at[1 + h])])
    wait(copies)


def shape(*dims):
    return jax.ShapeDtypeStruct(dims, F32)


def in_hbm(x):
    return pltpu.with_memory_space_constraint(x, pltpu.HBM)


def call(kernel, ins, outs, scratch=()):
    return pl.pallas_call(
        kernel,
        in_specs=ins,
        out_specs=[VMEM if isinstance(out, jax.ShapeDtypeStruct) else HBM for out in outs],
        out_shape=outs,
        scratch_shapes=[pltpu.VMEM(s, F32) if isinstance(s, tuple) else s for s in scratch],
        compiler_params=PARAMS,
    )


def exchange(x, axis):
    return lax.all_to_all(x, axis, 0, 0)


def on_device(residual, direction, material):
    matrix = dct_matrix()
    high = matrix.astype(jnp.bfloat16)
    low = (matrix - high.astype(np.float64)).astype(jnp.bfloat16)
    high, low = jnp.asarray(high), jnp.asarray(low)
    eigen = eigen_values()
    ez = jnp.asarray(eigen)
    ey_row = jnp.asarray(eigen[None, :])
    ey_tile = jnp.asarray(np.concatenate([eigen.reshape(4, 128)] * 2, 0))
    block = shape(BX, BY, N)
    half = pltpu.VMEM((N, N), jnp.bfloat16)

    (send,) = call(
        residual_kernel,
        [HBM] * 3,
        [pltpu.HBM((PEN, 8, 8, 128), F32)],
        [(BX, BY, N), half, half, (PEN, 8, 8, 128), pltpu.SemaphoreType.DMA((5,))],
    )(in_hbm(residual), in_hbm(high), in_hbm(low))
    recv_r = exchange(send, "pen")

    xlo, xhi, first, second = call(
        faces_kernel, [VMEM] * 2, [shape(1, BY, N), shape(1, BY, N), shape(BX, N), shape(BX, N)]
    )(direction, material)

    def up(x, axis, count):
        return lax.ppermute(x, axis, [(i, i + 1) for i in range(count - 1)])

    def down(x, axis, count):
        return lax.ppermute(x, axis, [(i + 1, i) for i in range(count - 1)])

    yb = lax.ppermute(second, "pen", [(i, i + 1 if i % 2 else i - 1) for i in range(1, PEN - 1)])
    xl, xh = up(xhi, "grp", GRP), down(xlo, "grp", GRP)
    ya = lax.ppermute(first, "pen", [(i, i ^ 1) for i in range(PEN)])
    inner, sums = call(
        inner_kernel, [VMEM] * 3, [block, shape(2, 8, 128)], [(BX + 2, BY, N)]
    )(residual, direction, material)
    operated, send = call(
        operated_kernel,
        [VMEM] * 10,
        [pltpu.HBM((BX, BY, N), F32), pltpu.HBM((PEN, 17, 4, 128), F32)],
        [(BX, BY, N), (PEN, 17, 4, 128), pltpu.SemaphoreType.DMA((3,))],
    )(inner, sums, direction, material, yb, xl, xh, ya, high, low)
    recv_q = exchange(send, "pen")

    field_r, inside_r, states, table, across = call(
        residual_blocks_kernel,
        [VMEM, VMEM, VMEM, SMEM, VMEM, VMEM],
        [
            pltpu.HBM((BX, BK, N), F32),
            pltpu.HBM((BX, BK, N), F32),
            shape(GRP, 8, 1, 128),
            shape(2, BK, N),
            shape(GRP + 3, 8, 128),
        ],
        [(BX, BK, N)] * 3 + [pltpu.SemaphoreType.DMA((2,))],
    )(recv_r, high, low, ez, ey_row, ey_tile)
    field_q, send = call(
        operated_blocks_kernel,
        [HBM, HBM] + [VMEM] * 4,
        [block, shape(GRP, 17, 1, 128)],
        [(BX, BK, N), (PEN, 17, 4, 128), (BX, BK, N), pltpu.SemaphoreType.DMA((3, 4))],
    )(in_hbm(recv_q), in_hbm(inside_r), states, table, high, low)

    recv = exchange(send, "grp")
    send, control = call(
        interface_kernel, [VMEM, VMEM], [shape(GRP, 9, 1, 128), shape(3, 8, 128)]
    )(recv, across)

    recv = exchange(send, "grp")
    (send,) = call(
        solve_kernel,
        [VMEM] * 7,
        [shape(PEN, 17, 4, 128)],
        [(BX, BK, N)] * 3,
    )(field_r, field_q, recv, control, table, high, low)

    recv = exchange(send, "pen")
    return tuple(
        call(
            finish_kernel,
            [VMEM] * 7,
            [pltpu.HBM((BX, BY, N), F32), pltpu.HBM((BX, BY, N), F32)],
            [(PEN, 2, 8, BX * BY), (BX, BY, N), (BX, BY, N), pltpu.SemaphoreType.DMA((3,))],
        )(recv, residual, direction, operated, control, high, low)
    )


def solution(mesh):
    placed = P("grp", "pen", None)
    return jax.shard_map(
        on_device,
        mesh=mesh,
        in_specs=(placed, placed, placed),
        out_specs=(placed, placed),
        check_vma=False,
    )
```

```python
import functools
import math

import jax
import jax.numpy as jnp
import numpy as np
from jax import lax
from jax.experimental import pallas as pl
from jax.experimental.pallas import tpu as pltpu
from jax.sharding import PartitionSpec as P

N = 512
GRP = 16
PEN = 32
BX = N // GRP
BY = N // PEN
BK = N // PEN
ABSORPTION = 0.02
CONDUCT = 5.0
SOLID = math.sqrt(30.0)
F32 = jnp.float32
VMEM = pl.BlockSpec(memory_space=pltpu.VMEM)
HBM = pl.BlockSpec(memory_space=pltpu.HBM)
SMEM = pl.BlockSpec(memory_space=pltpu.SMEM)
PARAMS = pltpu.CompilerParams(vmem_limit_bytes=48 * 1024 * 1024)


def dct_matrix():
    k = np.arange(N)[:, None]
    n = np.arange(N)[None, :]
    weight = np.where(k == 0, math.sqrt(1.0 / N), math.sqrt(2.0 / N))
    return weight * np.cos(math.pi * (k * (2 * n + 1) % (4 * N)) / (2.0 * N))


def eigen_values():
    return (4.0 * np.sin(math.pi * np.arange(N) / (2.0 * N)) ** 2).astype(np.float32)


def halves(x):
    high = x.astype(jnp.bfloat16)
    return high, (x - high.astype(F32)).astype(jnp.bfloat16)


def product(a, b, dims):
    def one(x, y):
        return lax.dot_general(x, y, (dims, ((), ())), preferred_element_type=F32)

    return one(a[0], b[0]) + (one(a[0], b[1]) + one(a[1], b[0]))


def whole(refs):
    return tuple(ref[...] for ref in refs)


def decay(shift):
    rho = 2.0 / (2.0 + shift + jnp.sqrt(shift * (shift + 4.0)))
    return rho, rho / (CONDUCT * (1.0 - rho * rho))


def turn(x, units):
    return pltpu.roll(x, 16 * units % 128, 1) if units % 8 else x


def swap_units(rows):
    unit = lax.broadcasted_iota(jnp.int32, rows[0].shape, 1) // 16
    rows = [turn(row, i) for i, row in enumerate(rows)]
    for d in (1, 2, 4):
        late = (unit & d) != 0
        rows = [jnp.where(late, rows[(i + d) % 8], rows[i]) for i in range(8)]
    return [turn(rows[-k % 8], -k) for k in range(8)]


def to_tile(x):
    x = x[:8] + x[8:]
    return x[:, 0:128] + x[:, 128:256] + x[:, 256:384] + x[:, 384:512]


def fold(x, step):
    return x + pltpu.roll(x, step, 0)


def stiffness_of(material):
    return jnp.where(material == 1, jnp.float32(SOLID), jnp.float32(1.0))


def even_pen():
    return lax.rem(lax.axis_index("pen"), 2) == 0


def faces_kernel(d_ref, m_ref, xlo_ref, xhi_ref, first_ref, second_ref, third_ref):
    xlo_ref[0] = stiffness_of(m_ref[0]) * d_ref[0]
    xhi_ref[0] = stiffness_of(m_ref[BX - 1]) * d_ref[BX - 1]
    low = stiffness_of(m_ref[:, 0, :]) * d_ref[:, 0, :]
    high = stiffness_of(m_ref[:, BY - 1, :]) * d_ref[:, BY - 1, :]
    first_ref[...] = jnp.where(even_pen(), high, low)
    second = jnp.where(even_pen(), low, high)
    second_ref[...] = second[: BX // 2]
    third_ref[...] = second[BX // 2 :]


def start(copies):
    for copy in copies:
        copy.start()
    return copies


def wait(copies):
    for copy in copies:
        copy.wait()


def send_third_modes(field_ref, c_refs, put, send_ref, send_hbm, sems):
    field = halves(field_ref[...].reshape(BX * BY, N))
    copies = []
    for h in range(2):
        devices = slice(h * PEN // 2, (h + 1) * PEN // 2)
        rows = slice(h * N // 2, (h + 1) * N // 2)
        modes = product(tuple(ref[rows] for ref in c_refs), field, ((1,), (1,)))
        for b in range(4):
            part = modes[:, 128 * b : 128 * b + 128].reshape(PEN // 2, 2, 8, 128)
            for a in range(2):
                put(devices, 4 * a + b, part[:, a])
        target = pl.ds(h * PEN // 2, PEN // 2)
        copies += start(
            [pltpu.make_async_copy(send_ref.at[target], send_hbm.at[target], sems.at[h])]
        )
    return copies


def residual_kernel(r_hbm, ch_hbm, cl_hbm, send_hbm, r_ref, ch_ref, cl_ref, send_ref, sems):
    wait(
        start(
            [
                pltpu.make_async_copy(r_hbm, r_ref, sems.at[2]),
                pltpu.make_async_copy(ch_hbm, ch_ref, sems.at[3]),
                pltpu.make_async_copy(cl_hbm, cl_ref, sems.at[4]),
            ]
        )
    )

    def put(devices, tile, x):
        send_ref[devices, tile] = x

    wait(send_third_modes(r_ref, (ch_ref, cl_ref), put, send_ref, send_hbm, sems))


def inner_kernel(r_ref, d_ref, m_ref, q_ref, sums_ref, u_ref):
    u_ref[0] = jnp.zeros((BY, N), F32)
    u_ref[BX + 1] = jnp.zeros((BY, N), F32)

    def scale(x, _):
        u_ref[x + 1] = stiffness_of(m_ref[x]) * d_ref[x]
        return 0

    lax.fori_loop(0, BX, scale, 0, unroll=4)
    row = lax.broadcasted_iota(jnp.int32, (BY, N), 0)
    lane = lax.broadcasted_iota(jnp.int32, (BY, N), 1)

    def stencil(x, sums):
        u = u_ref[x + 1]
        d = d_ref[x]
        beside = u_ref[x] + u_ref[x + 2]
        beside += jnp.where(row == 0, 0.0, pltpu.roll(u, 1, 0))
        beside += jnp.where(row == BY - 1, 0.0, pltpu.roll(u, BY - 1, 0))
        beside += jnp.where(lane == 0, 0.0, pltpu.roll(u, 1, 1))
        beside += jnp.where(lane == N - 1, 0.0, pltpu.roll(u, N - 1, 1))
        q = ABSORPTION * d + stiffness_of(m_ref[x]) * (6.0 * u - beside)
        q_ref[x] = q
        return sums[0] + to_tile(d * q), sums[1] + to_tile(r_ref[x] * d)

    zero = jnp.zeros((8, 128), F32)
    sums = lax.fori_loop(0, BX, stencil, (zero, zero), unroll=4)
    sums_ref[0], sums_ref[1] = sums


def operated_kernel(
    q_ref, sums_ref, d_ref, m_ref, yb_ref, yc_ref, xl_ref, xh_ref, ya_ref, ch_ref, cl_ref, out_hbm, send_hbm, out_ref, send_ref, y_ref, sems
):
    row = lax.broadcasted_iota(jnp.int32, (8, N), 0)

    y_ref[: BX // 2] = yb_ref[...]
    y_ref[BX // 2 :] = yc_ref[...]

    def low_high(x, total):
        ya, yb = ya_ref[pl.ds(x, 1), :], y_ref[pl.ds(x, 1), :]
        low, high = jnp.where(even_pen(), yb, ya), jnp.where(even_pen(), ya, yb)
        for first, edge, side in ((0, 0, low), (8, 7, high)):
            rows = pl.ds(first, 8)
            add = stiffness_of(m_ref[x, rows]) * jnp.where(row == edge, side, 0.0)
            out_ref[x, rows] = q_ref[x, rows] - add
            total = total + d_ref[x, rows] * add
        return total

    total = lax.fori_loop(0, BX, low_high, jnp.zeros((8, N), F32), unroll=4)
    total = jnp.concatenate([total, jnp.zeros((8, N), F32)], axis=0)
    for x, side_ref in ((0, xl_ref), (BX - 1, xh_ref)):
        add = stiffness_of(m_ref[x]) * side_ref[0]
        out_ref[x] = out_ref[x] - add
        total = total + d_ref[x] * add
    curvature = sums_ref[0] - to_tile(total)
    first = lax.broadcasted_iota(jnp.int32, (8, 128), 0) < 2
    sums = jnp.where(first, fold(fold(curvature, 4), 2), fold(fold(sums_ref[1], 4), 2))
    for j in range(PEN):
        send_ref[j, 16] = sums[:4]
    copies = start([pltpu.make_async_copy(out_ref, out_hbm, sems.at[2])])

    def put(devices, tile, x):
        send_ref[devices, 2 * tile] = x[:, :4]
        send_ref[devices, 2 * tile + 1] = x[:, 4:]

    wait(copies + send_third_modes(out_ref, (ch_ref, cl_ref), put, send_ref, send_hbm, sems))


def second_modes(get, c_refs, out_ref, y_ref, ready=lambda b: None):
    def part(b, _):
        ready(b)
        for s in range(4):
            for a in range(2):
                rows = swap_units([get(8 * s + i, 4 * a + b) for i in range(8)])
                for i in range(8):
                    y_ref[8 * b + i, 8 * a : 8 * a + 8, 128 * s : 128 * s + 128] = rows[i]
        return 0

    lax.fori_loop(0, 4, part, 0)
    field = halves(y_ref[...].reshape(BX * BK, N))
    out_ref[...] = product(field, whole(c_refs), ((1,), (1,))).reshape(BX, BK, N)


def third_eigen(ez_ref, h):
    k0 = lax.axis_index("pen") * BK + 8 * h
    return jnp.concatenate([jnp.full((1, N), ez_ref[k0 + i], F32) for i in range(8)], axis=0)


def put_states(v, w, h, send_ref, first):
    for side, x in enumerate((v, w)):
        for b in range(4):
            for i in range(8):
                send_ref[8 * h + i, first + 4 * side + b] = x[i : i + 1, 128 * b : 128 * b + 128]


def residual_blocks_kernel(
    recv_ref,
    ch_ref,
    cl_ref,
    ez_ref,
    ey_ref,
    tile_ref,
    fr_hbm,
    zr_hbm,
    states_ref,
    table_ref,
    across_ref,
    y_ref,
    fr_ref,
    zr_ref,
    sems,
):
    second_modes(lambda j, tile: recv_ref[j, tile], (ch_ref, cl_ref), fr_ref, y_ref)
    copies = start([pltpu.make_async_copy(fr_ref, fr_hbm, sems.at[0])])
    for h in range(2):
        rows = pl.ds(8 * h, 8)
        rho, factor = decay(ABSORPTION / CONDUCT + third_eigen(ez_ref, h) + ey_ref[...])
        table_ref[0, rows] = rho
        table_ref[1, rows] = factor

        def rise(x, v):
            v = fr_ref[x, rows] + rho * v
            zr_ref[x, rows] = v
            return v

        def fall(i, w):
            x = BX - 1 - i
            before = rho * w
            zr_ref[x, rows] = factor * (zr_ref[x, rows] + before)
            return fr_ref[x, rows] + before

        zero = jnp.zeros((8, N), F32)
        v = lax.fori_loop(0, BX, rise, zero, unroll=4)
        w = lax.fori_loop(0, BX, fall, zero, unroll=4)
        put_states(v, w, h, states_ref, 0)
    copies += start([pltpu.make_async_copy(zr_ref, zr_hbm, sems.at[1])])
    ez = ez_ref[lax.axis_index("pen") * BK + lax.axis_index("grp")]
    rho, factor = decay(ABSORPTION / CONDUCT + ez + tile_ref[...])
    across = rho
    for _ in range(5):
        across = across * across
    power = jnp.ones((8, 128), F32)
    for p in range(GRP):
        across_ref[p] = power
        power = power * across
    across_ref[GRP] = power
    across_ref[GRP + 1] = rho * factor
    across_ref[GRP + 2] = 1.0 / (1.0 - power * power)
    wait(copies)


def operated_blocks_kernel(
    recv_hbm, zr_hbm, states_ref, table_ref, ch_ref, cl_ref, fq_ref, send_ref, y_ref, recv_ref, zr_ref, sems
):
    def into(b):
        tiles = [pl.ds(2 * b, 2), pl.ds(2 * b + 8, 2)]
        return [
            pltpu.make_async_copy(recv_hbm.at[:, t], recv_ref.at[:, t], sems.at[i, b])
            for i, t in enumerate(tiles)
        ]

    for b in range(4):
        start(into(b))
    late = start(
        [
            pltpu.make_async_copy(recv_hbm.at[:, 16], recv_ref.at[:, 16], sems.at[2, 0]),
            pltpu.make_async_copy(zr_hbm, zr_ref, sems.at[2, 1]),
        ]
    )

    def get(j, tile):
        return jnp.concatenate([recv_ref[j, 2 * tile], recv_ref[j, 2 * tile + 1]], axis=0)

    second_modes(get, (ch_ref, cl_ref), fq_ref, y_ref, lambda b: wait(into(b)))
    wait(late)
    dots = [jnp.zeros((8, 128), F32), jnp.zeros((8, 128), F32)]
    for h in range(2):
        rows = pl.ds(8 * h, 8)
        rho = table_ref[0, rows]

        def sweep(x, carry):
            power, vq, wq, rq, qq = carry
            q = fq_ref[x, rows]
            before = rho * vq
            vq = q + before
            return power * rho, vq, wq + power * q, rq + zr_ref[x, rows] * q, qq + (vq + before) * q

        zero = jnp.zeros((8, N), F32)
        carry = (jnp.ones((8, N), F32),) + (zero,) * 4
        _, vq, wq, rq, qq = lax.fori_loop(0, BX, sweep, carry, unroll=4)
        put_states(vq, wq, h, send_ref, 8)
        for i, x in enumerate((rq, table_ref[1, rows] * qq)):
            dots[i] += x[:, 0:128] + x[:, 128:256] + x[:, 256:384] + x[:, 384:512]

    sums = recv_ref[0, 16]
    for j in range(1, PEN):
        sums = sums + recv_ref[j, 16]
    group = lax.broadcasted_iota(jnp.int32, (1, 128), 1) // 32
    packed = jnp.zeros((1, 128), F32)
    for i, x in enumerate((sums[0:2], sums[2:4], dots[0], dots[1])):
        x = jnp.sum(x, axis=0, keepdims=True)
        x = x + pltpu.roll(x, 64, 1)
        packed = jnp.where(group == i, x + pltpu.roll(x, 32, 1), packed)
    for j in range(GRP):
        send_ref[j, 0:8] = states_ref[j]
        send_ref[j, 16] = packed


def interface_kernel(recv_ref, across_ref, send_ref, control_ref):
    row = lax.broadcasted_iota(jnp.int32, (8, 128), 0)
    group = lax.broadcasted_iota(jnp.int32, (1, 128), 1) // 32
    sums = recv_ref[0, 16]
    for p in range(1, GRP):
        sums = sums + recv_ref[p, 16]

    def total(i):
        return jnp.full((8, 128), jnp.sum(jnp.where(group == i, sums, 0.0)), F32)

    curvature, projection, rq, qq = total(0), total(1), total(2), total(3)
    step = projection / curvature
    across = across_ref[1]
    others = [recv_ref[p, 8:16].reshape(8, 128) for p in range(GRP)]
    tiles = [recv_ref[p, 0:8].reshape(8, 128) - step * others[p] for p in range(GRP)]
    zero = jnp.zeros((8, 128), F32)
    rising = [zero]
    for p in range(GRP):
        rising.append(tiles[p] + across * rising[-1])
    falling = [zero]
    for p in reversed(range(GRP)):
        falling.append(tiles[p] + across * falling[-1])
    lower = row < 4
    ends = jnp.where(lower, rising[GRP], falling[GRP])
    images = (pltpu.roll(ends, 4, 0) + across_ref[GRP] * ends) * across_ref[GRP + 2]
    dots = zero
    for p in range(GRP):
        state = jnp.where(
            lower,
            rising[p] + across_ref[p] * images,
            falling[GRP - 1 - p] + across_ref[GRP - 1 - p] * images,
        )
        send_ref[p, 0:8] = state.reshape(8, 1, 128)
        dots = dots + state * pltpu.roll(others[p], 4, 0)
    dots = jnp.sum(across_ref[GRP + 1] * dots, axis=0, keepdims=True)
    for p in range(GRP):
        send_ref[p, 8] = dots
    control_ref[0] = step
    control_ref[1] = curvature
    control_ref[2] = rq - step * qq


def solve_kernel(
    fr_ref, fq_ref, recv_ref, control_ref, table_ref, ch_ref, cl_ref, send_ref, f_ref, u_ref, y_ref
):
    step = control_ref[0, 0:1, 0:1]
    rho, factor = table_ref[0], table_ref[1]

    def state(side):
        return jnp.concatenate(
            [
                jnp.concatenate([recv_ref[i, 4 * side + b] for i in range(BK)], axis=0)
                for b in range(4)
            ],
            axis=1,
        )

    def rise(x, carry):
        f = fr_ref[x] - step * fq_ref[x]
        carry = f + rho * carry
        f_ref[x] = f
        u_ref[x] = carry
        return carry

    def fall(i, carry):
        x = BX - 1 - i
        carry = rho * carry
        u_ref[x] = factor * (u_ref[x] + carry)
        return f_ref[x] + carry

    lax.fori_loop(0, BX, rise, state(0), unroll=4)
    lax.fori_loop(0, BX, fall, state(1), unroll=4)
    solved = halves(u_ref[...].reshape(BX * BK, N))
    y_ref[...] = product(solved, (ch_ref[...], cl_ref[...]), ((1,), (0,))).reshape(BX, BK, N)

    def part(b, _):
        for s in range(4):
            for a in range(2):
                rows = swap_units(
                    [y_ref[8 * b + i, 8 * a : 8 * a + 8, 128 * s : 128 * s + 128] for i in range(8)]
                )
                for i in range(8):
                    tile = 8 * a + 2 * b
                    send_ref[8 * s + i, tile] = rows[i][:4]
                    send_ref[8 * s + i, tile + 1] = rows[i][4:]
        return 0

    lax.fori_loop(0, 4, part, 0)
    sums = recv_ref[0, 8]
    for p in range(1, GRP):
        sums = sums + recv_ref[p, 8]
    row = lax.broadcasted_iota(jnp.int32, (8, 128), 0)
    first = (row == 0) & (lax.broadcasted_iota(jnp.int32, (8, 128), 1) == 0)
    sums = jnp.where(row == 0, sums, 0.0) + jnp.where(first, control_ref[2], 0.0)
    for j in range(PEN):
        send_ref[j, 16] = sums[:4]


def finish_kernel(
    recv_ref, r_ref, d_ref, q_ref, control_ref, ch_ref, cl_ref, nr_hbm, nd_hbm, g_ref, nr_ref, nd_ref, sems
):
    nr_ref[...] = r_ref[...] - control_ref[0, 0:1, 0:1] * q_ref[...]
    copies = start([pltpu.make_async_copy(nr_ref, nr_hbm, sems.at[0])])
    for b in range(4):
        for a in range(2):
            for c in range(2):
                rows = slice(4 * c, 4 * c + 4)
                g_ref[:, a, rows, 128 * b : 128 * b + 128] = recv_ref[:, 8 * a + 2 * b + c]
    sums = recv_ref[0, 16]
    for j in range(1, PEN):
        sums = sums + recv_ref[j, 16]
    conjugacy = jnp.full((8, 128), jnp.sum(sums), F32)
    ratio = (conjugacy / control_ref[1])[0:1, 0:1]
    for h in range(2):
        part = pl.ds(h * BX // 2, BX // 2)
        cells = slice(h * BX * BY // 2, (h + 1) * BX * BY // 2)
        modes = halves(g_ref[:, :, :, cells].reshape(N, BX * BY // 2))
        smoothed = product(modes, (ch_ref[...], cl_ref[...]), ((0,), (0,)))
        nd_ref[part] = smoothed.reshape(BX // 2, BY, N) - ratio * d_ref[part]
        copies += start([pltpu.make_async_copy(nd_ref.at[part], nd_hbm.at[part], sems.at[1 + h])])
    wait(copies)


def shape(*dims):
    return jax.ShapeDtypeStruct(dims, F32)


def in_hbm(x):
    return pltpu.with_memory_space_constraint(x, pltpu.HBM)


def call(kernel, ins, outs, scratch=()):
    return pl.pallas_call(
        kernel,
        in_specs=ins,
        out_specs=[VMEM if isinstance(out, jax.ShapeDtypeStruct) else HBM for out in outs],
        out_shape=outs,
        scratch_shapes=[pltpu.VMEM(s, F32) if isinstance(s, tuple) else s for s in scratch],
        compiler_params=PARAMS,
    )


def exchange(x, axis):
    return lax.all_to_all(x, axis, 0, 0)


def on_device(residual, direction, material):
    matrix = dct_matrix()
    high = matrix.astype(jnp.bfloat16)
    low = (matrix - high.astype(np.float64)).astype(jnp.bfloat16)
    high, low = jnp.asarray(high), jnp.asarray(low)
    eigen = eigen_values()
    ez = jnp.asarray(eigen)
    ey_row = jnp.asarray(eigen[None, :])
    ey_tile = jnp.asarray(np.concatenate([eigen.reshape(4, 128)] * 2, 0))
    block = shape(BX, BY, N)
    half = pltpu.VMEM((N, N), jnp.bfloat16)

    (send,) = call(
        residual_kernel,
        [HBM] * 3,
        [pltpu.HBM((PEN, 8, 8, 128), F32)],
        [(BX, BY, N), half, half, (PEN, 8, 8, 128), pltpu.SemaphoreType.DMA((5,))],
    )(in_hbm(residual), in_hbm(high), in_hbm(low))
    recv_r = exchange(send, "pen")

    xlo, xhi, first, second, third = call(
        faces_kernel, [VMEM] * 2, [shape(1, BY, N)] * 2 + [shape(BX, N)] + [shape(BX // 2, N)] * 2
    )(direction, material)

    def up(x, axis, count):
        return lax.ppermute(x, axis, [(i, i + 1) for i in range(count - 1)])

    def down(x, axis, count):
        return lax.ppermute(x, axis, [(i + 1, i) for i in range(count - 1)])

    across_chips = [(i, i + 1 if i % 2 else i - 1) for i in range(1, PEN - 1)]
    yb = lax.ppermute(second, "pen", across_chips)
    yc = lax.ppermute(third, "pen", across_chips)
    xl, xh = up(xhi, "grp", GRP), down(xlo, "grp", GRP)
    ya = lax.ppermute(first, "pen", [(i, i ^ 1) for i in range(PEN)])
    inner, sums = call(
        inner_kernel, [VMEM] * 3, [block, shape(2, 8, 128)], [(BX + 2, BY, N)]
    )(residual, direction, material)
    operated, send = call(
        operated_kernel,
        [VMEM] * 11,
        [pltpu.HBM((BX, BY, N), F32), pltpu.HBM((PEN, 17, 4, 128), F32)],
        [(BX, BY, N), (PEN, 17, 4, 128), (BX, N), pltpu.SemaphoreType.DMA((3,))],
    )(inner, sums, direction, material, yb, yc, xl, xh, ya, high, low)
    recv_q = exchange(send, "pen")

    field_r, inside_r, states, table, across = call(
        residual_blocks_kernel,
        [VMEM, VMEM, VMEM, SMEM, VMEM, VMEM],
        [
            pltpu.HBM((BX, BK, N), F32),
            pltpu.HBM((BX, BK, N), F32),
            shape(GRP, 8, 1, 128),
            shape(2, BK, N),
            shape(GRP + 3, 8, 128),
        ],
        [(BX, BK, N)] * 3 + [pltpu.SemaphoreType.DMA((2,))],
    )(recv_r, high, low, ez, ey_row, ey_tile)
    field_q, send = call(
        operated_blocks_kernel,
        [HBM, HBM] + [VMEM] * 4,
        [block, shape(GRP, 17, 1, 128)],
        [(BX, BK, N), (PEN, 17, 4, 128), (BX, BK, N), pltpu.SemaphoreType.DMA((3, 4))],
    )(in_hbm(recv_q), in_hbm(inside_r), states, table, high, low)

    recv = exchange(send, "grp")
    send, control = call(
        interface_kernel, [VMEM, VMEM], [shape(GRP, 9, 1, 128), shape(3, 8, 128)]
    )(recv, across)

    recv = exchange(send, "grp")
    (send,) = call(
        solve_kernel,
        [VMEM] * 7,
        [shape(PEN, 17, 4, 128)],
        [(BX, BK, N)] * 3,
    )(field_r, field_q, recv, control, table, high, low)

    recv = exchange(send, "pen")
    return tuple(
        call(
            finish_kernel,
            [VMEM] * 7,
            [pltpu.HBM((BX, BY, N), F32), pltpu.HBM((BX, BY, N), F32)],
            [(PEN, 2, 8, BX * BY), (BX, BY, N), (BX, BY, N), pltpu.SemaphoreType.DMA((3,))],
        )(recv, residual, direction, operated, control, high, low)
    )


def solution(mesh):
    placed = P("grp", "pen", None)
    return jax.shard_map(
        on_device,
        mesh=mesh,
        in_specs=(placed, placed, placed),
        out_specs=(placed, placed),
        check_vma=False,
    )
```

```python
import functools
import math

import jax
import jax.numpy as jnp
import numpy as np
from jax import lax
from jax.experimental import pallas as pl
from jax.experimental.pallas import tpu as pltpu
from jax.sharding import PartitionSpec as P

N = 512
GRP = 16
PEN = 32
BX = N // GRP
BY = N // PEN
BK = N // PEN
ABSORPTION = 0.02
CONDUCT = 5.0
SOLID = math.sqrt(30.0)
F32 = jnp.float32
VMEM = pl.BlockSpec(memory_space=pltpu.VMEM)
HBM = pl.BlockSpec(memory_space=pltpu.HBM)
SMEM = pl.BlockSpec(memory_space=pltpu.SMEM)
PARAMS = pltpu.CompilerParams(vmem_limit_bytes=48 * 1024 * 1024)


def dct_matrix():
    k = np.arange(N)[:, None]
    n = np.arange(N)[None, :]
    weight = np.where(k == 0, math.sqrt(1.0 / N), math.sqrt(2.0 / N))
    return weight * np.cos(math.pi * (k * (2 * n + 1) % (4 * N)) / (2.0 * N))


def eigen_values():
    return (4.0 * np.sin(math.pi * np.arange(N) / (2.0 * N)) ** 2).astype(np.float32)


def halves(x):
    high = x.astype(jnp.bfloat16)
    return high, (x - high.astype(F32)).astype(jnp.bfloat16)


def product(a, b, dims):
    def one(x, y):
        return lax.dot_general(x, y, (dims, ((), ())), preferred_element_type=F32)

    return one(a[0], b[0]) + (one(a[0], b[1]) + one(a[1], b[0]))


def whole(refs):
    return tuple(ref[...] for ref in refs)


def decay(shift):
    rho = 2.0 / (2.0 + shift + jnp.sqrt(shift * (shift + 4.0)))
    return rho, rho / (CONDUCT * (1.0 - rho * rho))


def turn(x, units):
    return pltpu.roll(x, 16 * units % 128, 1) if units % 8 else x


def swap_units(rows):
    unit = lax.broadcasted_iota(jnp.int32, rows[0].shape, 1) // 16
    rows = [turn(row, i) for i, row in enumerate(rows)]
    for d in (1, 2, 4):
        late = (unit & d) != 0
        rows = [jnp.where(late, rows[(i + d) % 8], rows[i]) for i in range(8)]
    return [turn(rows[-k % 8], -k) for k in range(8)]


def to_tile(x):
    x = x[:8] + x[8:]
    return x[:, 0:128] + x[:, 128:256] + x[:, 256:384] + x[:, 384:512]


def fold(x, step):
    return x + pltpu.roll(x, step, 0)


def stiffness_of(material):
    return jnp.where(material == 1, jnp.float32(SOLID), jnp.float32(1.0))


def even(axis):
    return lax.rem(lax.axis_index(axis), 2) == 0


def faces_kernel(d_ref, m_ref, x_first_ref, x_second_ref, first_ref, second_ref):
    low = stiffness_of(m_ref[0]) * d_ref[0]
    high = stiffness_of(m_ref[BX - 1]) * d_ref[BX - 1]
    x_first_ref[0] = jnp.where(even("grp"), high, low)
    x_second_ref[0] = jnp.where(even("grp"), low, high)
    low = stiffness_of(m_ref[:, 0, :]) * d_ref[:, 0, :]
    high = stiffness_of(m_ref[:, BY - 1, :]) * d_ref[:, BY - 1, :]
    first_ref[...] = jnp.where(even("pen"), high, low)
    second_ref[...] = jnp.where(even("pen"), low, high)


def start(copies):
    for copy in copies:
        copy.start()
    return copies


def wait(copies):
    for copy in copies:
        copy.wait()


def send_third_modes(field_ref, c_refs, put, send_ref, send_hbm, sems):
    field = halves(field_ref[...].reshape(BX * BY, N))
    copies = []
    for h in range(2):
        devices = slice(h * PEN // 2, (h + 1) * PEN // 2)
        rows = slice(h * N // 2, (h + 1) * N // 2)
        modes = product(tuple(ref[rows] for ref in c_refs), field, ((1,), (1,)))
        for b in range(4):
            part = modes[:, 128 * b : 128 * b + 128].reshape(PEN // 2, 2, 8, 128)
            for a in range(2):
                put(devices, 4 * a + b, part[:, a])
        target = pl.ds(h * PEN // 2, PEN // 2)
        copies += start(
            [pltpu.make_async_copy(send_ref.at[target], send_hbm.at[target], sems.at[h])]
        )
    return copies


def residual_kernel(r_hbm, ch_hbm, cl_hbm, send_hbm, r_ref, ch_ref, cl_ref, send_ref, sems):
    wait(
        start(
            [
                pltpu.make_async_copy(r_hbm, r_ref, sems.at[2]),
                pltpu.make_async_copy(ch_hbm, ch_ref, sems.at[3]),
                pltpu.make_async_copy(cl_hbm, cl_ref, sems.at[4]),
            ]
        )
    )

    def put(devices, tile, x):
        send_ref[devices, tile] = x

    wait(send_third_modes(r_ref, (ch_ref, cl_ref), put, send_ref, send_hbm, sems))


def inner_kernel(r_ref, d_ref, m_ref, q_ref, sums_ref, u_ref):
    u_ref[0] = jnp.zeros((BY, N), F32)
    u_ref[BX + 1] = jnp.zeros((BY, N), F32)

    def scale(x, _):
        u_ref[x + 1] = stiffness_of(m_ref[x]) * d_ref[x]
        return 0

    lax.fori_loop(0, BX, scale, 0, unroll=4)
    row = lax.broadcasted_iota(jnp.int32, (BY, N), 0)
    lane = lax.broadcasted_iota(jnp.int32, (BY, N), 1)

    def stencil(x, sums):
        u = u_ref[x + 1]
        d = d_ref[x]
        beside = u_ref[x] + u_ref[x + 2]
        beside += jnp.where(row == 0, 0.0, pltpu.roll(u, 1, 0))
        beside += jnp.where(row == BY - 1, 0.0, pltpu.roll(u, BY - 1, 0))
        beside += jnp.where(lane == 0, 0.0, pltpu.roll(u, 1, 1))
        beside += jnp.where(lane == N - 1, 0.0, pltpu.roll(u, N - 1, 1))
        q = ABSORPTION * d + stiffness_of(m_ref[x]) * (6.0 * u - beside)
        q_ref[x] = q
        return sums[0] + to_tile(d * q), sums[1] + to_tile(r_ref[x] * d)

    zero = jnp.zeros((8, 128), F32)
    sums = lax.fori_loop(0, BX, stencil, (zero, zero), unroll=4)
    sums_ref[0], sums_ref[1] = sums


def operated_kernel(
    q_ref, sums_ref, d_ref, m_ref, yb_ref, xa_ref, xb_ref, ya_ref, ch_ref, cl_ref, out_hbm, send_hbm, out_ref, send_ref, sems
):
    row = lax.broadcasted_iota(jnp.int32, (8, N), 0)

    def low_high(x, total):
        ya, yb = ya_ref[pl.ds(x, 1), :], yb_ref[pl.ds(x, 1), :]
        low, high = jnp.where(even("pen"), yb, ya), jnp.where(even("pen"), ya, yb)
        for first, edge, side in ((0, 0, low), (8, 7, high)):
            rows = pl.ds(first, 8)
            add = stiffness_of(m_ref[x, rows]) * jnp.where(row == edge, side, 0.0)
            out_ref[x, rows] = q_ref[x, rows] - add
            total = total + d_ref[x, rows] * add
        return total

    total = lax.fori_loop(0, BX, low_high, jnp.zeros((8, N), F32), unroll=4)
    total = jnp.concatenate([total, jnp.zeros((8, N), F32)], axis=0)
    xa, xb = xa_ref[0], xb_ref[0]
    low, high = jnp.where(even("grp"), xb, xa), jnp.where(even("grp"), xa, xb)
    for x, side in ((0, low), (BX - 1, high)):
        add = stiffness_of(m_ref[x]) * side
        out_ref[x] = out_ref[x] - add
        total = total + d_ref[x] * add
    curvature = sums_ref[0] - to_tile(total)
    first = lax.broadcasted_iota(jnp.int32, (8, 128), 0) < 2
    sums = jnp.where(first, fold(fold(curvature, 4), 2), fold(fold(sums_ref[1], 4), 2))
    for j in range(PEN):
        send_ref[j, 16] = sums[:4]
    copies = start([pltpu.make_async_copy(out_ref, out_hbm, sems.at[2])])

    def put(devices, tile, x):
        send_ref[devices, 2 * tile] = x[:, :4]
        send_ref[devices, 2 * tile + 1] = x[:, 4:]

    wait(copies + send_third_modes(out_ref, (ch_ref, cl_ref), put, send_ref, send_hbm, sems))


def second_modes(get, c_refs, out_ref, y_ref, ready=lambda b: None):
    def part(b, _):
        ready(b)
        for s in range(4):
            for a in range(2):
                rows = swap_units([get(8 * s + i, 4 * a + b) for i in range(8)])
                for i in range(8):
                    y_ref[8 * b + i, 8 * a : 8 * a + 8, 128 * s : 128 * s + 128] = rows[i]
        return 0

    lax.fori_loop(0, 4, part, 0)
    field = halves(y_ref[...].reshape(BX * BK, N))
    out_ref[...] = product(field, whole(c_refs), ((1,), (1,))).reshape(BX, BK, N)


def third_eigen(ez_ref, h):
    k0 = lax.axis_index("pen") * BK + 8 * h
    return jnp.concatenate([jnp.full((1, N), ez_ref[k0 + i], F32) for i in range(8)], axis=0)


def put_states(v, w, h, send_ref, first):
    for side, x in enumerate((v, w)):
        for b in range(4):
            for i in range(8):
                send_ref[8 * h + i, first + 4 * side + b] = x[i : i + 1, 128 * b : 128 * b + 128]


def residual_blocks_kernel(
    recv_ref,
    ch_ref,
    cl_ref,
    ez_ref,
    ey_ref,
    tile_ref,
    fr_hbm,
    zr_hbm,
    states_ref,
    table_ref,
    across_ref,
    y_ref,
    fr_ref,
    zr_ref,
    sems,
):
    second_modes(lambda j, tile: recv_ref[j, tile], (ch_ref, cl_ref), fr_ref, y_ref)
    copies = start([pltpu.make_async_copy(fr_ref, fr_hbm, sems.at[0])])
    for h in range(2):
        rows = pl.ds(8 * h, 8)
        rho, factor = decay(ABSORPTION / CONDUCT + third_eigen(ez_ref, h) + ey_ref[...])
        table_ref[0, rows] = rho
        table_ref[1, rows] = factor

        def rise(x, v):
            v = fr_ref[x, rows] + rho * v
            zr_ref[x, rows] = v
            return v

        def fall(i, w):
            x = BX - 1 - i
            before = rho * w
            zr_ref[x, rows] = factor * (zr_ref[x, rows] + before)
            return fr_ref[x, rows] + before

        zero = jnp.zeros((8, N), F32)
        v = lax.fori_loop(0, BX, rise, zero, unroll=4)
        w = lax.fori_loop(0, BX, fall, zero, unroll=4)
        put_states(v, w, h, states_ref, 0)
    copies += start([pltpu.make_async_copy(zr_ref, zr_hbm, sems.at[1])])
    ez = ez_ref[lax.axis_index("pen") * BK + lax.axis_index("grp")]
    rho, factor = decay(ABSORPTION / CONDUCT + ez + tile_ref[...])
    across = rho
    for _ in range(5):
        across = across * across
    power = jnp.ones((8, 128), F32)
    for p in range(GRP):
        across_ref[p] = power
        power = power * across
    across_ref[GRP] = power
    across_ref[GRP + 1] = rho * factor
    across_ref[GRP + 2] = 1.0 / (1.0 - power * power)
    wait(copies)


def operated_blocks_kernel(
    recv_hbm, zr_hbm, states_ref, table_ref, ch_ref, cl_ref, fq_ref, send_ref, y_ref, recv_ref, zr_ref, sems
):
    def into(b):
        tiles = [pl.ds(2 * b, 2), pl.ds(2 * b + 8, 2)]
        return [
            pltpu.make_async_copy(recv_hbm.at[:, t], recv_ref.at[:, t], sems.at[i, b])
            for i, t in enumerate(tiles)
        ]

    for b in range(4):
        start(into(b))
    late = start(
        [
            pltpu.make_async_copy(recv_hbm.at[:, 16], recv_ref.at[:, 16], sems.at[2, 0]),
            pltpu.make_async_copy(zr_hbm, zr_ref, sems.at[2, 1]),
        ]
    )

    def get(j, tile):
        return jnp.concatenate([recv_ref[j, 2 * tile], recv_ref[j, 2 * tile + 1]], axis=0)

    second_modes(get, (ch_ref, cl_ref), fq_ref, y_ref, lambda b: wait(into(b)))
    wait(late)
    dots = [jnp.zeros((8, 128), F32), jnp.zeros((8, 128), F32)]
    for h in range(2):
        rows = pl.ds(8 * h, 8)
        rho = table_ref[0, rows]

        def sweep(x, carry):
            power, vq, wq, rq, qq = carry
            q = fq_ref[x, rows]
            before = rho * vq
            vq = q + before
            return power * rho, vq, wq + power * q, rq + zr_ref[x, rows] * q, qq + (vq + before) * q

        zero = jnp.zeros((8, N), F32)
        carry = (jnp.ones((8, N), F32),) + (zero,) * 4
        _, vq, wq, rq, qq = lax.fori_loop(0, BX, sweep, carry, unroll=4)
        put_states(vq, wq, h, send_ref, 8)
        for i, x in enumerate((rq, table_ref[1, rows] * qq)):
            dots[i] += x[:, 0:128] + x[:, 128:256] + x[:, 256:384] + x[:, 384:512]

    sums = recv_ref[0, 16]
    for j in range(1, PEN):
        sums = sums + recv_ref[j, 16]
    group = lax.broadcasted_iota(jnp.int32, (1, 128), 1) // 32
    packed = jnp.zeros((1, 128), F32)
    for i, x in enumerate((sums[0:2], sums[2:4], dots[0], dots[1])):
        x = jnp.sum(x, axis=0, keepdims=True)
        x = x + pltpu.roll(x, 64, 1)
        packed = jnp.where(group == i, x + pltpu.roll(x, 32, 1), packed)
    for j in range(GRP):
        send_ref[j, 0:8] = states_ref[j]
        send_ref[j, 16] = packed


def interface_kernel(recv_ref, across_ref, send_ref, control_ref):
    row = lax.broadcasted_iota(jnp.int32, (8, 128), 0)
    group = lax.broadcasted_iota(jnp.int32, (1, 128), 1) // 32
    sums = recv_ref[0, 16]
    for p in range(1, GRP):
        sums = sums + recv_ref[p, 16]

    def total(i):
        return jnp.full((8, 128), jnp.sum(jnp.where(group == i, sums, 0.0)), F32)

    curvature, projection, rq, qq = total(0), total(1), total(2), total(3)
    step = projection / curvature
    across = across_ref[1]
    others = [recv_ref[p, 8:16].reshape(8, 128) for p in range(GRP)]
    tiles = [recv_ref[p, 0:8].reshape(8, 128) - step * others[p] for p in range(GRP)]
    zero = jnp.zeros((8, 128), F32)
    rising = [zero]
    for p in range(GRP):
        rising.append(tiles[p] + across * rising[-1])
    falling = [zero]
    for p in reversed(range(GRP)):
        falling.append(tiles[p] + across * falling[-1])
    lower = row < 4
    ends = jnp.where(lower, rising[GRP], falling[GRP])
    images = (pltpu.roll(ends, 4, 0) + across_ref[GRP] * ends) * across_ref[GRP + 2]
    dots = zero
    for p in range(GRP):
        state = jnp.where(
            lower,
            rising[p] + across_ref[p] * images,
            falling[GRP - 1 - p] + across_ref[GRP - 1 - p] * images,
        )
        send_ref[p, 0:8] = state.reshape(8, 1, 128)
        dots = dots + state * pltpu.roll(others[p], 4, 0)
    dots = jnp.sum(across_ref[GRP + 1] * dots, axis=0, keepdims=True)
    for p in range(GRP):
        send_ref[p, 8] = dots
    control_ref[0] = step
    control_ref[1] = curvature
    control_ref[2] = rq - step * qq


def solve_kernel(
    fr_ref, fq_ref, recv_ref, control_ref, table_ref, ch_ref, cl_ref, send_ref, f_ref, u_ref, y_ref
):
    step = control_ref[0, 0:1, 0:1]
    rho, factor = table_ref[0], table_ref[1]

    def state(side):
        return jnp.concatenate(
            [
                jnp.concatenate([recv_ref[i, 4 * side + b] for i in range(BK)], axis=0)
                for b in range(4)
            ],
            axis=1,
        )

    def rise(x, carry):
        f = fr_ref[x] - step * fq_ref[x]
        carry = f + rho * carry
        f_ref[x] = f
        u_ref[x] = carry
        return carry

    def fall(i, carry):
        x = BX - 1 - i
        carry = rho * carry
        u_ref[x] = factor * (u_ref[x] + carry)
        return f_ref[x] + carry

    lax.fori_loop(0, BX, rise, state(0), unroll=4)
    lax.fori_loop(0, BX, fall, state(1), unroll=4)
    solved = halves(u_ref[...].reshape(BX * BK, N))
    y_ref[...] = product(solved, (ch_ref[...], cl_ref[...]), ((1,), (0,))).reshape(BX, BK, N)

    def part(b, _):
        for s in range(4):
            for a in range(2):
                rows = swap_units(
                    [y_ref[8 * b + i, 8 * a : 8 * a + 8, 128 * s : 128 * s + 128] for i in range(8)]
                )
                for i in range(8):
                    tile = 8 * a + 2 * b
                    send_ref[8 * s + i, tile] = rows[i][:4]
                    send_ref[8 * s + i, tile + 1] = rows[i][4:]
        return 0

    lax.fori_loop(0, 4, part, 0)
    sums = recv_ref[0, 8]
    for p in range(1, GRP):
        sums = sums + recv_ref[p, 8]
    row = lax.broadcasted_iota(jnp.int32, (8, 128), 0)
    first = (row == 0) & (lax.broadcasted_iota(jnp.int32, (8, 128), 1) == 0)
    sums = jnp.where(row == 0, sums, 0.0) + jnp.where(first, control_ref[2], 0.0)
    for j in range(PEN):
        send_ref[j, 16] = sums[:4]


def finish_kernel(
    recv_ref, r_ref, d_ref, q_ref, control_ref, ch_ref, cl_ref, nr_hbm, nd_hbm, g_ref, nr_ref, nd_ref, sems
):
    nr_ref[...] = r_ref[...] - control_ref[0, 0:1, 0:1] * q_ref[...]
    copies = start([pltpu.make_async_copy(nr_ref, nr_hbm, sems.at[0])])
    for b in range(4):
        for a in range(2):
            for c in range(2):
                rows = slice(4 * c, 4 * c + 4)
                g_ref[:, a, rows, 128 * b : 128 * b + 128] = recv_ref[:, 8 * a + 2 * b + c]
    sums = recv_ref[0, 16]
    for j in range(1, PEN):
        sums = sums + recv_ref[j, 16]
    conjugacy = jnp.full((8, 128), jnp.sum(sums), F32)
    ratio = (conjugacy / control_ref[1])[0:1, 0:1]
    for h in range(2):
        part = pl.ds(h * BX // 2, BX // 2)
        cells = slice(h * BX * BY // 2, (h + 1) * BX * BY // 2)
        modes = halves(g_ref[:, :, :, cells].reshape(N, BX * BY // 2))
        smoothed = product(modes, (ch_ref[...], cl_ref[...]), ((0,), (0,)))
        nd_ref[part] = smoothed.reshape(BX // 2, BY, N) - ratio * d_ref[part]
        copies += start([pltpu.make_async_copy(nd_ref.at[part], nd_hbm.at[part], sems.at[1 + h])])
    wait(copies)


def shape(*dims):
    return jax.ShapeDtypeStruct(dims, F32)


def in_hbm(x):
    return pltpu.with_memory_space_constraint(x, pltpu.HBM)


def call(kernel, ins, outs, scratch=()):
    return pl.pallas_call(
        kernel,
        in_specs=ins,
        out_specs=[VMEM if isinstance(out, jax.ShapeDtypeStruct) else HBM for out in outs],
        out_shape=outs,
        scratch_shapes=[pltpu.VMEM(s, F32) if isinstance(s, tuple) else s for s in scratch],
        compiler_params=PARAMS,
    )


def exchange(x, axis):
    return lax.all_to_all(x, axis, 0, 0)


def on_device(residual, direction, material):
    matrix = dct_matrix()
    high = matrix.astype(jnp.bfloat16)
    low = (matrix - high.astype(np.float64)).astype(jnp.bfloat16)
    high, low = jnp.asarray(high), jnp.asarray(low)
    eigen = eigen_values()
    ez = jnp.asarray(eigen)
    ey_row = jnp.asarray(eigen[None, :])
    ey_tile = jnp.asarray(np.concatenate([eigen.reshape(4, 128)] * 2, 0))
    block = shape(BX, BY, N)
    half = pltpu.VMEM((N, N), jnp.bfloat16)

    (send,) = call(
        residual_kernel,
        [HBM] * 3,
        [pltpu.HBM((PEN, 8, 8, 128), F32)],
        [(BX, BY, N), half, half, (PEN, 8, 8, 128), pltpu.SemaphoreType.DMA((5,))],
    )(in_hbm(residual), in_hbm(high), in_hbm(low))
    recv_r = exchange(send, "pen")

    x_first, x_second, first, second = call(
        faces_kernel, [VMEM] * 2, [shape(1, BY, N), shape(1, BY, N), shape(BX, N), shape(BX, N)]
    )(direction, material)

    def swap_pairs(x, axis, count):
        return lax.ppermute(x, axis, [(i, i ^ 1) for i in range(count)])

    def swap_between(x, axis, count):
        return lax.ppermute(x, axis, [(i, i + 1 if i % 2 else i - 1) for i in range(1, count - 1)])

    xa, xb = swap_pairs(x_first, "grp", GRP), swap_between(x_second, "grp", GRP)
    ya, yb = swap_pairs(first, "pen", PEN), swap_between(second, "pen", PEN)

    inner, sums = call(
        inner_kernel, [VMEM] * 3, [block, shape(2, 8, 128)], [(BX + 2, BY, N)]
    )(residual, direction, material)
    operated, send = call(
        operated_kernel,
        [VMEM] * 10,
        [pltpu.HBM((BX, BY, N), F32), pltpu.HBM((PEN, 17, 4, 128), F32)],
        [(BX, BY, N), (PEN, 17, 4, 128), pltpu.SemaphoreType.DMA((3,))],
    )(inner, sums, direction, material, yb, xa, xb, ya, high, low)
    recv_q = exchange(send, "pen")

    field_r, inside_r, states, table, across = call(
        residual_blocks_kernel,
        [VMEM, VMEM, VMEM, SMEM, VMEM, VMEM],
        [
            pltpu.HBM((BX, BK, N), F32),
            pltpu.HBM((BX, BK, N), F32),
            shape(GRP, 8, 1, 128),
            shape(2, BK, N),
            shape(GRP + 3, 8, 128),
        ],
        [(BX, BK, N)] * 3 + [pltpu.SemaphoreType.DMA((2,))],
    )(recv_r, high, low, ez, ey_row, ey_tile)
    field_q, send = call(
        operated_blocks_kernel,
        [HBM, HBM] + [VMEM] * 4,
        [block, shape(GRP, 17, 1, 128)],
        [(BX, BK, N), (PEN, 17, 4, 128), (BX, BK, N), pltpu.SemaphoreType.DMA((3, 4))],
    )(in_hbm(recv_q), in_hbm(inside_r), states, table, high, low)

    recv = exchange(send, "grp")
    send, control = call(
        interface_kernel, [VMEM, VMEM], [shape(GRP, 9, 1, 128), shape(3, 8, 128)]
    )(recv, across)

    recv = exchange(send, "grp")
    (send,) = call(
        solve_kernel,
        [VMEM] * 7,
        [shape(PEN, 17, 4, 128)],
        [(BX, BK, N)] * 3,
    )(field_r, field_q, recv, control, table, high, low)

    recv = exchange(send, "pen")
    return tuple(
        call(
            finish_kernel,
            [VMEM] * 7,
            [pltpu.HBM((BX, BY, N), F32), pltpu.HBM((BX, BY, N), F32)],
            [(PEN, 2, 8, BX * BY), (BX, BY, N), (BX, BY, N), pltpu.SemaphoreType.DMA((3,))],
        )(recv, residual, direction, operated, control, high, low)
    )


def solution(mesh):
    placed = P("grp", "pen", None)
    return jax.shard_map(
        on_device,
        mesh=mesh,
        in_specs=(placed, placed, placed),
        out_specs=(placed, placed),
        check_vma=False,
    )
```

```python
import functools
import math

import jax
import jax.numpy as jnp
import numpy as np
from jax import lax
from jax.experimental import pallas as pl
from jax.experimental.pallas import tpu as pltpu
from jax.sharding import PartitionSpec as P

N = 512
GRP = 16
PEN = 32
BX = N // GRP
BY = N // PEN
BK = N // PEN
ABSORPTION = 0.02
CONDUCT = 5.0
SOLID = math.sqrt(30.0)
F32 = jnp.float32
VMEM = pl.BlockSpec(memory_space=pltpu.VMEM)
HBM = pl.BlockSpec(memory_space=pltpu.HBM)
SMEM = pl.BlockSpec(memory_space=pltpu.SMEM)
PARAMS = pltpu.CompilerParams(vmem_limit_bytes=48 * 1024 * 1024)


def dct_matrix():
    k = np.arange(N)[:, None]
    n = np.arange(N)[None, :]
    weight = np.where(k == 0, math.sqrt(1.0 / N), math.sqrt(2.0 / N))
    return weight * np.cos(math.pi * (k * (2 * n + 1) % (4 * N)) / (2.0 * N))


def eigen_values():
    return (4.0 * np.sin(math.pi * np.arange(N) / (2.0 * N)) ** 2).astype(np.float32)


def halves(x):
    high = x.astype(jnp.bfloat16)
    return high, (x - high.astype(F32)).astype(jnp.bfloat16)


def product(a, b, dims):
    def one(x, y):
        return lax.dot_general(x, y, (dims, ((), ())), preferred_element_type=F32)

    return one(a[0], b[0]) + (one(a[0], b[1]) + one(a[1], b[0]))


def whole(refs):
    return tuple(ref[...] for ref in refs)


def decay(shift):
    rho = 2.0 / (2.0 + shift + jnp.sqrt(shift * (shift + 4.0)))
    return rho, rho / (CONDUCT * (1.0 - rho * rho))


def turn(x, units):
    return pltpu.roll(x, 16 * units % 128, 1) if units % 8 else x


def swap_units(rows):
    unit = lax.broadcasted_iota(jnp.int32, rows[0].shape, 1) // 16
    rows = [turn(row, i) for i, row in enumerate(rows)]
    for d in (1, 2, 4):
        late = (unit & d) != 0
        rows = [jnp.where(late, rows[(i + d) % 8], rows[i]) for i in range(8)]
    return [turn(rows[-k % 8], -k) for k in range(8)]


def to_tile(x):
    x = x[:8] + x[8:]
    return x[:, 0:128] + x[:, 128:256] + x[:, 256:384] + x[:, 384:512]


def fold(x, step):
    return x + pltpu.roll(x, step, 0)


def stiffness_of(material):
    return jnp.where(material == 1, jnp.float32(SOLID), jnp.float32(1.0))


def even_pen():
    return lax.rem(lax.axis_index("pen"), 2) == 0


def faces_kernel(d_ref, m_ref, xlo_ref, xhi_ref, first_ref, second_ref):
    xlo_ref[0] = stiffness_of(m_ref[0]) * d_ref[0]
    xhi_ref[0] = stiffness_of(m_ref[BX - 1]) * d_ref[BX - 1]
    low = stiffness_of(m_ref[:, 0, :]) * d_ref[:, 0, :]
    high = stiffness_of(m_ref[:, BY - 1, :]) * d_ref[:, BY - 1, :]
    first_ref[...] = jnp.where(even_pen(), high, low)
    second_ref[...] = jnp.where(even_pen(), low, high)


def start(copies):
    for copy in copies:
        copy.start()
    return copies


def wait(copies):
    for copy in copies:
        copy.wait()


def send_third_modes(field_ref, c_refs, put, send_ref, send_hbm, sems):
    field = halves(field_ref[...].reshape(BX * BY, N))
    copies = []
    for h in range(2):
        devices = slice(h * PEN // 2, (h + 1) * PEN // 2)
        rows = slice(h * N // 2, (h + 1) * N // 2)
        modes = product(tuple(ref[rows] for ref in c_refs), field, ((1,), (1,)))
        for b in range(4):
            part = modes[:, 128 * b : 128 * b + 128].reshape(PEN // 2, 2, 8, 128)
            for a in range(2):
                put(devices, 4 * a + b, part[:, a])
        target = pl.ds(h * PEN // 2, PEN // 2)
        copies += start(
            [pltpu.make_async_copy(send_ref.at[target], send_hbm.at[target], sems.at[h])]
        )
    return copies


def residual_kernel(r_hbm, ch_hbm, cl_hbm, send_hbm, r_ref, ch_ref, cl_ref, send_ref, sems):
    wait(
        start(
            [
                pltpu.make_async_copy(r_hbm, r_ref, sems.at[2]),
                pltpu.make_async_copy(ch_hbm, ch_ref, sems.at[3]),
                pltpu.make_async_copy(cl_hbm, cl_ref, sems.at[4]),
            ]
        )
    )

    def put(devices, tile, x):
        send_ref[devices, tile] = x

    wait(send_third_modes(r_ref, (ch_ref, cl_ref), put, send_ref, send_hbm, sems))


def inner_kernel(r_ref, d_ref, m_ref, q_ref, sums_ref, u_ref):
    u_ref[0] = jnp.zeros((BY, N), F32)
    u_ref[BX + 1] = jnp.zeros((BY, N), F32)

    def scale(x, _):
        u_ref[x + 1] = stiffness_of(m_ref[x]) * d_ref[x]
        return 0

    lax.fori_loop(0, BX, scale, 0, unroll=4)
    row = lax.broadcasted_iota(jnp.int32, (BY, N), 0)
    lane = lax.broadcasted_iota(jnp.int32, (BY, N), 1)

    def stencil(x, sums):
        u = u_ref[x + 1]
        d = d_ref[x]
        beside = u_ref[x] + u_ref[x + 2]
        beside += jnp.where(row == 0, 0.0, pltpu.roll(u, 1, 0))
        beside += jnp.where(row == BY - 1, 0.0, pltpu.roll(u, BY - 1, 0))
        beside += jnp.where(lane == 0, 0.0, pltpu.roll(u, 1, 1))
        beside += jnp.where(lane == N - 1, 0.0, pltpu.roll(u, N - 1, 1))
        q = ABSORPTION * d + stiffness_of(m_ref[x]) * (6.0 * u - beside)
        q_ref[x] = q
        return sums[0] + to_tile(d * q), sums[1] + to_tile(r_ref[x] * d)

    zero = jnp.zeros((8, 128), F32)
    sums = lax.fori_loop(0, BX, stencil, (zero, zero), unroll=4)
    sums_ref[0], sums_ref[1] = sums


def operated_kernel(
    q_ref, sums_ref, d_ref, m_ref, yb_ref, xl_ref, xh_ref, ya_ref, ch_ref, cl_ref, out_hbm, send_hbm, out_ref, send_ref, sems
):
    row = lax.broadcasted_iota(jnp.int32, (8, N), 0)

    def low_high(x, total):
        ya, yb = ya_ref[pl.ds(x, 1), :], yb_ref[pl.ds(x, 1), :]
        low, high = jnp.where(even_pen(), yb, ya), jnp.where(even_pen(), ya, yb)
        for first, edge, side in ((0, 0, low), (8, 7, high)):
            rows = pl.ds(first, 8)
            add = stiffness_of(m_ref[x, rows]) * jnp.where(row == edge, side, 0.0)
            out_ref[x, rows] = q_ref[x, rows] - add
            total = total + d_ref[x, rows] * add
        return total

    total = lax.fori_loop(0, BX, low_high, jnp.zeros((8, N), F32), unroll=4)
    total = jnp.concatenate([total, jnp.zeros((8, N), F32)], axis=0)
    for x, side_ref in ((0, xl_ref), (BX - 1, xh_ref)):
        add = stiffness_of(m_ref[x]) * side_ref[0]
        out_ref[x] = out_ref[x] - add
        total = total + d_ref[x] * add
    curvature = sums_ref[0] - to_tile(total)
    first = lax.broadcasted_iota(jnp.int32, (8, 128), 0) < 2
    sums = jnp.where(first, fold(fold(curvature, 4), 2), fold(fold(sums_ref[1], 4), 2))
    for j in range(PEN):
        send_ref[j, 16] = sums[:4]
    copies = start([pltpu.make_async_copy(out_ref, out_hbm, sems.at[2])])

    def put(devices, tile, x):
        send_ref[devices, 2 * tile] = x[:, :4]
        send_ref[devices, 2 * tile + 1] = x[:, 4:]

    wait(copies + send_third_modes(out_ref, (ch_ref, cl_ref), put, send_ref, send_hbm, sems))


def second_modes(get, c_refs, out_ref, y_ref, ready=lambda b: None):
    def part(b, _):
        ready(b)
        for s in range(4):
            for a in range(2):
                rows = swap_units([get(8 * s + i, 4 * a + b) for i in range(8)])
                for i in range(8):
                    y_ref[8 * b + i, 8 * a : 8 * a + 8, 128 * s : 128 * s + 128] = rows[i]
        return 0

    lax.fori_loop(0, 4, part, 0)
    field = halves(y_ref[...].reshape(BX * BK, N))
    out_ref[...] = product(field, whole(c_refs), ((1,), (1,))).reshape(BX, BK, N)


def third_eigen(ez_ref, h):
    k0 = lax.axis_index("pen") * BK + 8 * h
    return jnp.concatenate([jnp.full((1, N), ez_ref[k0 + i], F32) for i in range(8)], axis=0)


def put_states(v, w, h, send_ref, first):
    for side, x in enumerate((v, w)):
        for b in range(4):
            for i in range(8):
                send_ref[8 * h + i, first + 4 * side + b] = x[i : i + 1, 128 * b : 128 * b + 128]


def residual_blocks_kernel(
    recv_ref,
    ch_ref,
    cl_ref,
    ez_ref,
    ey_ref,
    tile_ref,
    fr_hbm,
    zr_hbm,
    states_ref,
    table_ref,
    across_ref,
    y_ref,
    fr_ref,
    zr_ref,
    sems,
):
    second_modes(lambda j, tile: recv_ref[j, tile], (ch_ref, cl_ref), fr_ref, y_ref)
    copies = start([pltpu.make_async_copy(fr_ref, fr_hbm, sems.at[0])])
    for h in range(2):
        rows = pl.ds(8 * h, 8)
        rho, factor = decay(ABSORPTION / CONDUCT + third_eigen(ez_ref, h) + ey_ref[...])
        table_ref[0, rows] = rho
        table_ref[1, rows] = factor

        def rise(x, v):
            v = fr_ref[x, rows] + rho * v
            zr_ref[x, rows] = v
            return v

        def fall(i, w):
            x = BX - 1 - i
            before = rho * w
            zr_ref[x, rows] = factor * (zr_ref[x, rows] + before)
            return fr_ref[x, rows] + before

        zero = jnp.zeros((8, N), F32)
        v = lax.fori_loop(0, BX, rise, zero, unroll=4)
        w = lax.fori_loop(0, BX, fall, zero, unroll=4)
        put_states(v, w, h, states_ref, 0)
    copies += start([pltpu.make_async_copy(zr_ref, zr_hbm, sems.at[1])])
    ez = ez_ref[lax.axis_index("pen") * BK + lax.axis_index("grp")]
    rho, factor = decay(ABSORPTION / CONDUCT + ez + tile_ref[...])
    across = rho
    for _ in range(5):
        across = across * across
    power = jnp.ones((8, 128), F32)
    for p in range(GRP):
        across_ref[p] = power
        power = power * across
    across_ref[GRP] = power
    across_ref[GRP + 1] = rho * factor
    across_ref[GRP + 2] = 1.0 / (1.0 - power * power)
    wait(copies)


def operated_blocks_kernel(
    recv_hbm, zr_hbm, states_ref, table_ref, ch_ref, cl_ref, fq_ref, send_ref, y_ref, recv_ref, zr_ref, sems
):
    def into(b):
        tiles = [pl.ds(2 * b, 2), pl.ds(2 * b + 8, 2)]
        return [
            pltpu.make_async_copy(recv_hbm.at[:, t], recv_ref.at[:, t], sems.at[i, b])
            for i, t in enumerate(tiles)
        ]

    for b in range(4):
        start(into(b))
    late = start(
        [
            pltpu.make_async_copy(recv_hbm.at[:, 16], recv_ref.at[:, 16], sems.at[2, 0]),
            pltpu.make_async_copy(zr_hbm, zr_ref, sems.at[2, 1]),
            pltpu.make_async_copy(states_ref, send_ref.at[:, pl.ds(0, 8)], sems.at[2, 2]),
        ]
    )

    def get(j, tile):
        return jnp.concatenate([recv_ref[j, 2 * tile], recv_ref[j, 2 * tile + 1]], axis=0)

    second_modes(get, (ch_ref, cl_ref), fq_ref, y_ref, lambda b: wait(into(b)))
    wait(late)
    dots = [jnp.zeros((8, 128), F32), jnp.zeros((8, 128), F32)]
    for h in range(2):
        rows = pl.ds(8 * h, 8)
        rho = table_ref[0, rows]

        def sweep(x, carry):
            power, vq, wq, rq, qq = carry
            q = fq_ref[x, rows]
            before = rho * vq
            vq = q + before
            return power * rho, vq, wq + power * q, rq + zr_ref[x, rows] * q, qq + (vq + before) * q

        zero = jnp.zeros((8, N), F32)
        carry = (jnp.ones((8, N), F32),) + (zero,) * 4
        _, vq, wq, rq, qq = lax.fori_loop(0, BX, sweep, carry, unroll=4)
        put_states(vq, wq, h, send_ref, 8)
        for i, x in enumerate((rq, table_ref[1, rows] * qq)):
            dots[i] += x[:, 0:128] + x[:, 128:256] + x[:, 256:384] + x[:, 384:512]

    sums = recv_ref[0, 16]
    for j in range(1, PEN):
        sums = sums + recv_ref[j, 16]
    group = lax.broadcasted_iota(jnp.int32, (1, 128), 1) // 32
    packed = jnp.zeros((1, 128), F32)
    for i, x in enumerate((sums[0:2], sums[2:4], dots[0], dots[1])):
        x = jnp.sum(x, axis=0, keepdims=True)
        x = x + pltpu.roll(x, 64, 1)
        packed = jnp.where(group == i, x + pltpu.roll(x, 32, 1), packed)
    for j in range(GRP):
        send_ref[j, 16] = packed


def interface_kernel(recv_ref, across_ref, send_ref, control_ref):
    row = lax.broadcasted_iota(jnp.int32, (8, 128), 0)
    group = lax.broadcasted_iota(jnp.int32, (1, 128), 1) // 32
    sums = recv_ref[0, 16]
    for p in range(1, GRP):
        sums = sums + recv_ref[p, 16]

    def total(i):
        return jnp.full((8, 128), jnp.sum(jnp.where(group == i, sums, 0.0)), F32)

    curvature, projection, rq, qq = total(0), total(1), total(2), total(3)
    step = projection / curvature
    across = across_ref[1]
    others = [recv_ref[p, 8:16].reshape(8, 128) for p in range(GRP)]
    tiles = [recv_ref[p, 0:8].reshape(8, 128) - step * others[p] for p in range(GRP)]
    zero = jnp.zeros((8, 128), F32)
    rising = [zero]
    for p in range(GRP):
        rising.append(tiles[p] + across * rising[-1])
    falling = [zero]
    for p in reversed(range(GRP)):
        falling.append(tiles[p] + across * falling[-1])
    lower = row < 4
    ends = jnp.where(lower, rising[GRP], falling[GRP])
    images = (pltpu.roll(ends, 4, 0) + across_ref[GRP] * ends) * across_ref[GRP + 2]
    dots = zero
    for p in range(GRP):
        state = jnp.where(
            lower,
            rising[p] + across_ref[p] * images,
            falling[GRP - 1 - p] + across_ref[GRP - 1 - p] * images,
        )
        send_ref[p, 0:8] = state.reshape(8, 1, 128)
        dots = dots + state * pltpu.roll(others[p], 4, 0)
    dots = jnp.sum(across_ref[GRP + 1] * dots, axis=0, keepdims=True)
    for p in range(GRP):
        send_ref[p, 8] = dots
    control_ref[0] = step
    control_ref[1] = curvature
    control_ref[2] = rq - step * qq


def solve_kernel(
    fr_ref, fq_ref, recv_ref, control_ref, table_ref, ch_ref, cl_ref, send_ref, f_ref, u_ref, y_ref
):
    step = control_ref[0, 0:1, 0:1]
    rho, factor = table_ref[0], table_ref[1]

    def state(side):
        return jnp.concatenate(
            [
                jnp.concatenate([recv_ref[i, 4 * side + b] for i in range(BK)], axis=0)
                for b in range(4)
            ],
            axis=1,
        )

    def rise(x, carry):
        f = fr_ref[x] - step * fq_ref[x]
        carry = f + rho * carry
        f_ref[x] = f
        u_ref[x] = carry
        return carry

    def fall(i, carry):
        x = BX - 1 - i
        carry = rho * carry
        u_ref[x] = factor * (u_ref[x] + carry)
        return f_ref[x] + carry

    lax.fori_loop(0, BX, rise, state(0), unroll=4)
    lax.fori_loop(0, BX, fall, state(1), unroll=4)
    solved = halves(u_ref[...].reshape(BX * BK, N))
    y_ref[...] = product(solved, (ch_ref[...], cl_ref[...]), ((1,), (0,))).reshape(BX, BK, N)

    def part(b, _):
        for s in range(4):
            for a in range(2):
                rows = swap_units(
                    [y_ref[8 * b + i, 8 * a : 8 * a + 8, 128 * s : 128 * s + 128] for i in range(8)]
                )
                for i in range(8):
                    tile = 8 * a + 2 * b
                    send_ref[8 * s + i, tile] = rows[i][:4]
                    send_ref[8 * s + i, tile + 1] = rows[i][4:]
        return 0

    lax.fori_loop(0, 4, part, 0)
    sums = recv_ref[0, 8]
    for p in range(1, GRP):
        sums = sums + recv_ref[p, 8]
    row = lax.broadcasted_iota(jnp.int32, (8, 128), 0)
    first = (row == 0) & (lax.broadcasted_iota(jnp.int32, (8, 128), 1) == 0)
    sums = jnp.where(row == 0, sums, 0.0) + jnp.where(first, control_ref[2], 0.0)
    for j in range(PEN):
        send_ref[j, 16] = sums[:4]


def finish_kernel(
    recv_ref, r_ref, d_ref, q_ref, control_ref, ch_ref, cl_ref, nr_hbm, nd_hbm, g_ref, nr_ref, nd_ref, sems
):
    nr_ref[...] = r_ref[...] - control_ref[0, 0:1, 0:1] * q_ref[...]
    copies = start([pltpu.make_async_copy(nr_ref, nr_hbm, sems.at[0])])
    for b in range(4):
        for a in range(2):
            for c in range(2):
                rows = slice(4 * c, 4 * c + 4)
                g_ref[:, a, rows, 128 * b : 128 * b + 128] = recv_ref[:, 8 * a + 2 * b + c]
    sums = recv_ref[0, 16]
    for j in range(1, PEN):
        sums = sums + recv_ref[j, 16]
    conjugacy = jnp.full((8, 128), jnp.sum(sums), F32)
    ratio = (conjugacy / control_ref[1])[0:1, 0:1]
    for h in range(2):
        part = pl.ds(h * BX // 2, BX // 2)
        cells = slice(h * BX * BY // 2, (h + 1) * BX * BY // 2)
        modes = halves(g_ref[:, :, :, cells].reshape(N, BX * BY // 2))
        smoothed = product(modes, (ch_ref[...], cl_ref[...]), ((0,), (0,)))
        nd_ref[part] = smoothed.reshape(BX // 2, BY, N) - ratio * d_ref[part]
        copies += start([pltpu.make_async_copy(nd_ref.at[part], nd_hbm.at[part], sems.at[1 + h])])
    wait(copies)


def shape(*dims):
    return jax.ShapeDtypeStruct(dims, F32)


def in_hbm(x):
    return pltpu.with_memory_space_constraint(x, pltpu.HBM)


def call(kernel, ins, outs, scratch=()):
    return pl.pallas_call(
        kernel,
        in_specs=ins,
        out_specs=[VMEM if isinstance(out, jax.ShapeDtypeStruct) else HBM for out in outs],
        out_shape=outs,
        scratch_shapes=[pltpu.VMEM(s, F32) if isinstance(s, tuple) else s for s in scratch],
        compiler_params=PARAMS,
    )


def exchange(x, axis):
    return lax.all_to_all(x, axis, 0, 0)


def on_device(residual, direction, material):
    matrix = dct_matrix()
    high = matrix.astype(jnp.bfloat16)
    low = (matrix - high.astype(np.float64)).astype(jnp.bfloat16)
    high, low = jnp.asarray(high), jnp.asarray(low)
    eigen = eigen_values()
    ez = jnp.asarray(eigen)
    ey_row = jnp.asarray(eigen[None, :])
    ey_tile = jnp.asarray(np.concatenate([eigen.reshape(4, 128)] * 2, 0))
    block = shape(BX, BY, N)
    half = pltpu.VMEM((N, N), jnp.bfloat16)

    (send,) = call(
        residual_kernel,
        [HBM] * 3,
        [pltpu.HBM((PEN, 8, 8, 128), F32)],
        [(BX, BY, N), half, half, (PEN, 8, 8, 128), pltpu.SemaphoreType.DMA((5,))],
    )(in_hbm(residual), in_hbm(high), in_hbm(low))
    recv_r = exchange(send, "pen")

    xlo, xhi, first, second = call(
        faces_kernel, [VMEM] * 2, [shape(1, BY, N), shape(1, BY, N), shape(BX, N), shape(BX, N)]
    )(direction, material)

    def up(x, axis, count):
        return lax.ppermute(x, axis, [(i, i + 1) for i in range(count - 1)])

    def down(x, axis, count):
        return lax.ppermute(x, axis, [(i + 1, i) for i in range(count - 1)])

    yb = lax.ppermute(second, "pen", [(i, i + 1 if i % 2 else i - 1) for i in range(1, PEN - 1)])
    xl, xh = up(xhi, "grp", GRP), down(xlo, "grp", GRP)
    ya = lax.ppermute(first, "pen", [(i, i ^ 1) for i in range(PEN)])
    inner, sums = call(
        inner_kernel, [VMEM] * 3, [block, shape(2, 8, 128)], [(BX + 2, BY, N)]
    )(residual, direction, material)
    operated, send = call(
        operated_kernel,
        [VMEM] * 10,
        [pltpu.HBM((BX, BY, N), F32), pltpu.HBM((PEN, 17, 4, 128), F32)],
        [(BX, BY, N), (PEN, 17, 4, 128), pltpu.SemaphoreType.DMA((3,))],
    )(inner, sums, direction, material, yb, xl, xh, ya, high, low)
    recv_q = exchange(send, "pen")

    field_r, inside_r, states, table, across = call(
        residual_blocks_kernel,
        [VMEM, VMEM, VMEM, SMEM, VMEM, VMEM],
        [
            pltpu.HBM((BX, BK, N), F32),
            pltpu.HBM((BX, BK, N), F32),
            shape(GRP, 8, 1, 128),
            shape(2, BK, N),
            shape(GRP + 3, 8, 128),
        ],
        [(BX, BK, N)] * 3 + [pltpu.SemaphoreType.DMA((2,))],
    )(recv_r, high, low, ez, ey_row, ey_tile)
    field_q, send = call(
        operated_blocks_kernel,
        [HBM, HBM] + [VMEM] * 4,
        [block, shape(GRP, 17, 1, 128)],
        [(BX, BK, N), (PEN, 17, 4, 128), (BX, BK, N), pltpu.SemaphoreType.DMA((3, 4))],
    )(in_hbm(recv_q), in_hbm(inside_r), states, table, high, low)

    recv = exchange(send, "grp")
    send, control = call(
        interface_kernel, [VMEM, VMEM], [shape(GRP, 9, 1, 128), shape(3, 8, 128)]
    )(recv, across)

    recv = exchange(send, "grp")
    (send,) = call(
        solve_kernel,
        [VMEM] * 7,
        [shape(PEN, 17, 4, 128)],
        [(BX, BK, N)] * 3,
    )(field_r, field_q, recv, control, table, high, low)

    recv = exchange(send, "pen")
    return tuple(
        call(
            finish_kernel,
            [VMEM] * 7,
            [pltpu.HBM((BX, BY, N), F32), pltpu.HBM((BX, BY, N), F32)],
            [(PEN, 2, 8, BX * BY), (BX, BY, N), (BX, BY, N), pltpu.SemaphoreType.DMA((3,))],
        )(recv, residual, direction, operated, control, high, low)
    )


def solution(mesh):
    placed = P("grp", "pen", None)
    return jax.shard_map(
        on_device,
        mesh=mesh,
        in_specs=(placed, placed, placed),
        out_specs=(placed, placed),
        check_vma=False,
    )
```
